32 devices in a mesh: blk: 8 (over y, x, core), head: 4 (over z).
Axes of the slice: x: 2, y: 2, z: 4, core: 2. Of those that a mesh axis runs over, the one named last changes fastest.
Arguments:
- inputs: bfloat16 [2, 2048, 2048], P(None, ('blk', 'head')), may hold values from -6 to 6
- cotangent: bfloat16 [2, 2048, 2048], P(None, ('blk', 'head')), may hold values from -6 to 6
- lengths: int32 [2], replicated, may hold values from 1024 to 2048, as said below
- positions: int32 [2, 2048], replicated, may hold values from 0 to 2047, as said below
- attn_gain: bfloat16 [2048], P(('blk', 'head')), may hold values from 0.5 to 1.5
- mlp_gain: bfloat16 [2048], P(('blk', 'head')), may hold values from 0.5 to 1.5
- w_query: bfloat16 [2048, 2048], P(('blk', 'head')), may hold values from -0.5 to 0.5
- key_projection: bfloat16 [2048, 512], P(('blk', 'head')), may hold values from -0.5 to 0.5
- value_projection: bfloat16 [2048, 512], P(('blk', 'head')), may hold values from -0.125 to 0.125
- w_out: bfloat16 [2048, 2048], P(('blk', 'head')), may hold values from -3 to 3
- w_gate: bfloat16 [2048, 8192], P('blk', 'head'), may hold values from -0.125 to 0.125
- w_up: bfloat16 [2048, 8192], P('blk', 'head'), may hold values from -0.125 to 0.125
- w_down: bfloat16 [8192, 2048], P('head', 'blk'), may hold values from -0.25 to 0.25
Outputs:
- output: bfloat16 [2, 2048, 2048], P(None, ('blk', 'head'))
- input_grad: float32 [2, 2048, 2048], P(None, ('blk', 'head'))
- grad_attn_gain: float32 [2048], P(('blk', 'head'))
- grad_mlp_gain: float32 [2048], P(('blk', 'head'))
- grad_query: float32 [2048, 2048], P(('blk', 'head'))
- grad_key: float32 [2048, 512], P(('blk', 'head'))
- grad_value: float32 [2048, 512], P(('blk', 'head'))
- grad_out: float32 [2048, 2048], P(('blk', 'head'))
- grad_gate: float32 [2048, 8192], P('blk', 'head')
- grad_up: float32 [2048, 8192], P('blk', 'head')
- grad_down: float32 [8192, 2048], P('head', 'blk')
The draws below stay inside these ranges and needn't reach their ends.
Inputs may be any that keep to these rules, and one draw needn't show every extreme that they name: `lengths`: at least half of 2048; in every draw one micro-batch has exactly 2048. Each row is a permutation of 0 to 2047; aligned block b of 64 slots holds, in some order, the run of half of 64 positions starting at b times half of 64 and the mirrored run starting at (2048 - (b + 1) times half of 64).
All inputs are finite; a program needn't handle non-finite values.
Results may differ from the reference program's by a relative error of at most 0.02.
Values may be sent and summed in bfloat16 or wider, within the bound.
No kernel may reach another device: no remote copies, remote signals or barrier semaphores. Data moves between devices by JAX's collectives and lax.ppermute only.
A program may use at most 168 MiB of HBM per device.

```python
import jax
import jax.numpy as jnp
from jax import lax

MODEL_WIDTH = 2048
QUERY_HEADS = 32
KEY_VALUE_HEADS = 8
HEAD_SIZE = 64
FF = 8192
TOK_DEV = 64
MICRO = 2
MICRO_SLOTS = 2048


def draw_lengths(key, part):
    key = jax.random.fold_in(key, 11)
    first_key, second_key = jax.random.split(key)
    base_len = MICRO_SLOTS // 2 + jax.random.randint(first_key, (MICRO,), 0, MICRO_SLOTS // 2 + 1)
    full_one = jax.random.randint(second_key, (), 0, MICRO)
    return jnp.where(jnp.arange(MICRO) == full_one, MICRO_SLOTS, base_len).astype(jnp.int32)


def draw_positions(key, part):
    key = jax.random.fold_in(key, 23)
    groups = MICRO_SLOTS // TOK_DEV
    half_run = TOK_DEV // 2
    row_ids = jnp.arange(TOK_DEV)[None, :]
    device_ids = jnp.arange(groups)[:, None]
    base_pos = jnp.where(row_ids < half_run, device_ids * half_run + row_ids, (2 * groups - 1 - device_ids) * half_run + row_ids - half_run)
    scores = jax.random.randint(key, (MICRO, groups, TOK_DEV), 0, 1 << 20) * TOK_DEV + row_ids[None, :, :]
    order = jnp.argsort(scores, axis=-1, stable=True)
    dealt = jnp.take_along_axis(jnp.broadcast_to(base_pos[None, :, :], (MICRO, groups, TOK_DEV)), order, axis=-1)
    return dealt.reshape(MICRO, MICRO_SLOTS).astype(jnp.int32)


def block_levels(rng, shape, shards, least, largest):
    factor_of = 1.0
    for axis_at, shards_of in shards:
        heights = jax.random.uniform(jax.random.fold_in(jax.random.fold_in(rng, 6), axis_at), (shards_of,), jnp.float32, least / len(shards), largest / len(shards))
        factor_of = factor_of * jnp.repeat(jnp.exp(heights), shape[axis_at] // shards_of).reshape((-1,) + (1,) * (len(shape) - 1 - axis_at))
    return factor_of


def bell_draw(own_key, dims, width, bound, cuts=(), held_as=jnp.bfloat16):
    drawn = jax.random.normal(own_key, dims, jnp.float32) * width
    if len(cuts) > 0:
        drawn = block_levels(own_key, dims, cuts, -0.22, 0.18) * drawn
    return jnp.clip(drawn, min=-bound, max=bound).astype(held_as)


def setup_inputs(seed: int = 0) -> dict:
    key_list = jax.random.split(jax.random.key(seed), 14)
    return {
        "inputs": bell_draw(key_list[0], (MICRO, MICRO_SLOTS, MODEL_WIDTH), 1.0, 6.0, ((1, 32),)),
        "cotangent": bell_draw(key_list[1], (MICRO, MICRO_SLOTS, MODEL_WIDTH), 1.0, 6.0, ((1, 32),)),
        "lengths": draw_lengths(jax.random.fold_in(key_list[13], 71), 0),
        "positions": draw_positions(jax.random.fold_in(key_list[13], 71), 0),
        "attn_gain": jnp.clip(1.0 + 0.1 * jax.random.normal(key_list[4], (MODEL_WIDTH,), jnp.float32), 0.5, 1.5).astype(jnp.bfloat16),
        "mlp_gain": jnp.clip(1.0 + 0.1 * jax.random.normal(key_list[5], (MODEL_WIDTH,), jnp.float32), 0.5, 1.5).astype(jnp.bfloat16),
        "w_query": bell_draw(key_list[6], (MODEL_WIDTH, QUERY_HEADS * HEAD_SIZE), (MODEL_WIDTH // 16) ** -0.5, 0.5, ((0, 32),)),
        "key_projection": bell_draw(key_list[7], (MODEL_WIDTH, KEY_VALUE_HEADS * HEAD_SIZE), (MODEL_WIDTH // 16) ** -0.5, 0.5, ((0, 32),)),
        "value_projection": bell_draw(key_list[8], (MODEL_WIDTH, KEY_VALUE_HEADS * HEAD_SIZE), MODEL_WIDTH ** -0.5, 0.125, ((0, 32),)),
        "w_out": bell_draw(key_list[9], (QUERY_HEADS * HEAD_SIZE, MODEL_WIDTH), (max(QUERY_HEADS * HEAD_SIZE // 512, 1)) ** -0.5, 3.0, ((0, 32),)),
        "w_gate": bell_draw(key_list[10], (MODEL_WIDTH, FF), MODEL_WIDTH ** -0.5, 0.125, ((0, 8), (1, 4))),
        "w_up": bell_draw(key_list[11], (MODEL_WIDTH, FF), MODEL_WIDTH ** -0.5, 0.125, ((0, 8), (1, 4))),
        "w_down": bell_draw(key_list[12], (FF, MODEL_WIDTH), (FF // 16) ** -0.5, 0.25, ((0, 4), (1, 8))),
    }


SCORE_SCALE = 0.015625
RESIDUAL_SCALE = 0.22
EPSILON = 1e-06
ROPE_BASE = 10000000.0
NEG_FILL = -1e+30

@jax.custom_vjp
def reduced_precision(v):
    return lax.optimization_barrier(v.astype(jnp.bfloat16)).astype(jnp.float32)

@jax.custom_vjp
def reduced_backward(v):
    return v

def low_keep(v):
    return (reduced_precision(v), None)

def low_pass(kept, grad):
    return (grad,)

def back_keep(v):
    return (v, None)

def back_low(kept, grad):
    return (reduced_precision(grad),)
reduced_precision.defvjp(low_keep, low_pass)
reduced_backward.defvjp(back_keep, back_low)

def matrix_product(left, right):
    return jnp.dot(left, right, precision=lax.Precision.HIGHEST, preferred_element_type=jnp.float32)

def normalize(values, gain):
    scale_inv = lax.rsqrt(lax.optimization_barrier(jnp.mean(values * values, -1, keepdims=True)) + EPSILON)
    return values * scale_inv * gain

def rotary_tables(positions_row):
    half_dim = HEAD_SIZE // 2
    frequency = ROPE_BASE ** (-(jnp.arange(half_dim).astype(jnp.float32) * 2.0) / HEAD_SIZE)
    angles = positions_row.astype(jnp.float32)[:, None] * frequency[None, :]
    angles = jnp.concatenate([angles, angles], -1)
    return (jnp.cos(angles)[:, None, :], jnp.sin(angles)[:, None, :])

def rotate(values):
    half_dim = values.shape[-1] // 2
    return jnp.concatenate([-values[..., half_dim:], values[..., :half_dim]], -1)

def rotary(values, cosine, sine):
    return values * cosine + rotate(values) * sine

def attention_layer(query_rows, key_row_table, value_row_table, slot_position, sequence_length):
    rows_per_block = min(256, MICRO_SLOTS)
    block_count = MICRO_SLOTS // rows_per_block
    query_block_list = query_rows.reshape(block_count, rows_per_block, KEY_VALUE_HEADS, QUERY_HEADS // KEY_VALUE_HEADS, HEAD_SIZE)
    pos_blocks = slot_position.reshape(block_count, rows_per_block)

    def one_block(args):
        query_block, query_pos = args
        scores = SCORE_SCALE * jnp.einsum('qhgd,khd->qhgk', query_block, key_row_table, precision=lax.Precision.HIGHEST)
        scores = reduced_backward(scores)
        visible = (slot_position[None, :] <= query_pos[:, None]) & (slot_position[None, :] < sequence_length)
        scores = jnp.where(visible[:, None, None, :], scores, NEG_FILL)
        top = lax.optimization_barrier(jnp.max(scores, -1, keepdims=True))
        expo = jnp.exp(scores - top)
        probs = expo / lax.optimization_barrier(jnp.sum(expo, -1, keepdims=True))
        return jnp.einsum('qhgk,khd->qhgd', reduced_precision(probs), value_row_table, precision=lax.Precision.HIGHEST)
    result = lax.map(jax.checkpoint(one_block), (query_block_list, pos_blocks))
    return result.reshape(MICRO_SLOTS, QUERY_HEADS * HEAD_SIZE)

def layer_block(x_rows, gain_one, gain_two, wq, key_weight, value_weight, wo, wg, wu, wd, slot_position, sequence_length):
    first_normed_input = reduced_precision(normalize(x_rows, gain_one))
    cosine, sine = rotary_tables(slot_position)
    q_raw = reduced_backward(matrix_product(first_normed_input, wq)).reshape(MICRO_SLOTS, QUERY_HEADS, HEAD_SIZE)
    query_rows = reduced_backward(reduced_precision(rotary(q_raw, cosine, sine)))
    unrotated_keys = reduced_backward(matrix_product(first_normed_input, key_weight)).reshape(MICRO_SLOTS, KEY_VALUE_HEADS, HEAD_SIZE)
    key_row_table = reduced_backward(reduced_precision(rotary(unrotated_keys, cosine, sine)))
    value_row_table = reduced_backward(reduced_precision(matrix_product(first_normed_input, value_weight))).reshape(MICRO_SLOTS, KEY_VALUE_HEADS, HEAD_SIZE)
    attention_output = attention_layer(query_rows.reshape(MICRO_SLOTS, KEY_VALUE_HEADS, QUERY_HEADS // KEY_VALUE_HEADS, HEAD_SIZE), key_row_table, value_row_table, slot_position, sequence_length)
    attn_low = reduced_backward(reduced_precision(attention_output))
    branch = reduced_backward(matrix_product(attn_low, wo))
    resid = x_rows + RESIDUAL_SCALE * branch
    xn2 = reduced_precision(normalize(resid, gain_two))
    gate_pre = reduced_backward(matrix_product(xn2, wg))
    up_proj = reduced_backward(matrix_product(xn2, wu))
    hidden = reduced_precision(jax.nn.silu(gate_pre) * up_proj)
    mlp_out = reduced_backward(matrix_product(hidden, wd))
    return resid + RESIDUAL_SCALE * mlp_out

def reference(inputs, cotangent, lengths, positions, attn_gain, mlp_gain, w_query, key_projection, value_projection, w_out, w_gate, w_up, w_down):
    floats = [arr.astype(jnp.float32) for arr in (inputs, attn_gain, mlp_gain, w_query, key_projection, value_projection, w_out, w_gate, w_up, w_down)]

    def forward(x_all, gain_one, gain_two, wq, key_weight, value_weight, wo, wg, wu, wd):
        results = []
        for micro_idx in range(MICRO):
            results.append(layer_block(x_all[micro_idx], gain_one, gain_two, wq, key_weight, value_weight, wo, wg, wu, wd, positions[micro_idx], lengths[micro_idx]))
        return jnp.stack(results)
    result, pullback = jax.vjp(forward, *floats)
    grads = pullback(cotangent.astype(jnp.float32))
    return (result.astype(jnp.bfloat16), grads[0], grads[1], grads[2], grads[3], grads[4], grads[5], grads[6], grads[7], grads[8], grads[9])
```

```python
import functools

import jax
import jax.numpy as jnp
from jax import lax
from jax.experimental import pallas as pl
from jax.experimental.pallas import tpu as pltpu
from jax.sharding import PartitionSpec as P

MODEL_WIDTH = 2048
QUERY_HEADS = 32
KEY_VALUE_HEADS = 8
HEAD_SIZE = 64
SHARED = QUERY_HEADS // KEY_VALUE_HEADS
MICRO = 2

SCORE_SCALE = 0.015625
RESIDUAL_SCALE = 0.22
EPSILON = 1e-06
ROPE_BASE = 10000000.0
NEG_FILL = -1e30

BF = jnp.bfloat16
F32 = jnp.float32
VMEM_LIMIT = 56 * 1024 * 1024


def dot(left, right, contract):
    return lax.dot_general(left, right, (contract, ((), ())), preferred_element_type=F32)


def nn(left, right):
    return dot(left, right, ((1,), (0,)))


def tn(left, right):
    return dot(left, right, ((0,), (0,)))


def nt(left, right):
    return dot(left, right, ((1,), (1,)))


def swap(x, bit, devices):
    return lax.ppermute(x, "blk", [(i, i ^ bit) for i in range(devices)])


def xor_gather(x, devices):
    if devices == 8:
        half = x.shape[0] // 2
        r2 = swap(x, 2, devices)
        r4 = swap(x, 4, devices)
        top = swap(r2[:half], 4, devices)
        low = swap(r4[half:], 2, devices)
        even = jnp.concatenate([x, r2, r4, top, low], 0)
        odd = swap(even, 1, devices)
        rows = x.shape[0]
        found = [None] * 8
        for place, j in enumerate((0, 2, 4, 6)):
            found[j] = even[place * rows : (place + 1) * rows]
            found[j ^ 1] = odd[place * rows : (place + 1) * rows]
        return found
    found = {0: x}
    bit = devices // 2
    while bit:
        order = sorted(found)
        came = swap(jnp.stack([found[j] for j in order]), bit, devices)
        for place, j in enumerate(order):
            found[j ^ bit] = came[place]
        bit //= 2
    return [found[j] for j in range(devices)]


def natural(found, me, axis):
    block = found[0].shape[axis]
    shape = list(found[0].shape)
    shape[axis] = block * len(found)
    whole = jnp.zeros(shape, found[0].dtype)
    for j, piece in enumerate(found):
        whole = lax.dynamic_update_slice_in_dim(whole, piece, (me ^ j) * block, axis)
    return whole


def add(left, right):
    return (left.astype(F32) + right.astype(F32)).astype(BF)


def xor_scatter(make, devices):
    if devices == 8:
        odd = [make(j) for j in (1, 3, 5, 7)]
        came = swap(jnp.stack(odd), 1, devices)
        even = [add(make(j), came[place]) for place, j in enumerate((0, 2, 4, 6))]
        h0, h2, h4, h6 = even
        half = h0.shape[0] // 2
        from_x = swap(h6[:half], 2, devices)
        from_y = swap(h6[half:], 4, devices)
        h4 = jnp.concatenate([add(h4[:half], from_x), h4[half:]], 0)
        h2 = jnp.concatenate([h2[:half], add(h2[half:], from_y)], 0)
        came_x = swap(h2, 2, devices)
        came_y = swap(h4, 4, devices)
        return h0.astype(F32) + came_x.astype(F32) + came_y.astype(F32)
    held = {j: make(j) for j in range(devices)}
    bit = 1
    while bit < devices:
        away = sorted(j for j in held if j & bit)
        came = swap(jnp.stack([held.pop(j) for j in away]), bit, devices)
        for place, j in enumerate(away):
            held[j ^ bit] = add(held[j ^ bit], came[place])
        bit *= 2
    return held[0].astype(F32)


def run_offset(index, run, tile, half):
    if run == 0:
        return index
    return (tile - half) - (index // half) * half + index % half


def tile_place(t, blocks):
    late = t >= blocks
    return jnp.where(late, 2 * blocks - 1 - t, t), jnp.where(late, 1, 0)


def tile_mask(t, own, length, run, tile, rows, half, blocks):
    key_row = lax.broadcasted_iota(jnp.int32, (tile, 1), 0)
    key_pos = t * tile + jnp.where(
        t >= blocks, run_offset(key_row, 1, tile, half), run_offset(key_row, 0, tile, half)
    )
    query_pos = own * tile + run_offset(
        lax.broadcasted_iota(jnp.int32, (1, rows), 1) % tile, run, tile, half
    )
    key_pos = jnp.where(key_pos < length, key_pos, jnp.int32(1 << 30))
    return key_pos <= query_pos


def own_tiles(scalars, run, tile, blocks):
    micro = pl.program_id(0)
    mine = scalars[0]
    length = scalars[1 + micro]
    own = mine if run == 0 else 2 * blocks - 1 - mine
    count = jnp.minimum(own + 1, (length + tile - 1) // tile)
    return own, length, count


def head_part(values, head, heads):
    if heads == 1:
        return values
    lane = lax.broadcasted_iota(jnp.int32, values.shape, 1) // HEAD_SIZE
    return jnp.where(lane == head, values, jnp.zeros_like(values))


def fold_rows(values, combine):
    rows, lanes = values.shape
    return combine(values.reshape(rows // 8, 8, lanes), axis=0)


def forward_kernel(scalars, q_ref, kv_ref, o_ref, lse_ref, s_ref, *, blocks, tile, half, heads):
    width = heads * HEAD_SIZE
    rows = q_ref.shape[2]
    for run in range(2):
        own, length, count = own_tiles(scalars, run, tile, blocks)
        done = jnp.zeros((rows, width), F32)
        for head in range(heads):
            q = head_part(q_ref[0, run], head, heads)

            def scores(t, top, q=q, own=own, length=length, run=run):
                place, late = tile_place(t, blocks)
                s = nt(kv_ref[place, 0, late, :, :width], q)
                s = jnp.where(
                    tile_mask(t, own, length, run, tile, rows, half, blocks), s, NEG_FILL
                )
                s_ref[t] = s
                return jnp.maximum(top, fold_rows(s, jnp.max))

            top = lax.fori_loop(0, count, scores, jnp.full((8, rows), NEG_FILL, F32))
            top = jnp.max(top, 0, keepdims=True)

            def mix(t, held, top=top):
                total, acc = held
                place, late = tile_place(t, blocks)
                p = jnp.exp(s_ref[t] - top)
                v = kv_ref[place, 0, late, :, width:]
                return total + fold_rows(p, jnp.sum), acc + tn(v, p.astype(BF))

            total, acc = lax.fori_loop(
                0, count, mix, (jnp.zeros((8, rows), F32), jnp.zeros((width, rows), F32))
            )
            total = jnp.sum(total, 0, keepdims=True)
            lse_ref[0, run, head] = top + jnp.log(total)
            done = done + head_part((acc / total).T, head, heads)
        o_ref[0, run] = done.astype(BF)


def backward_kernel(
    scalars, q_ref, kv_ref, do_ref, lse_ref, delta_ref, dq_ref, dkv_ref, acc_ref, *, blocks, tile, half, heads
):
    width = heads * HEAD_SIZE
    rows = q_ref.shape[2]
    acc_ref[...] = jnp.zeros(acc_ref.shape, F32)
    for run in range(2):
        own, length, count = own_tiles(scalars, run, tile, blocks)
        done = jnp.zeros((rows, width), F32)
        for head in range(heads):
            q = head_part(q_ref[0, run], head, heads)
            do = head_part(do_ref[0, run], head, heads)
            lse = lse_ref[0, run, head]
            delta = delta_ref[0, run, head]

            def step(t, dq, q=q, do=do, lse=lse, delta=delta, own=own, length=length, run=run):
                place, late = tile_place(t, blocks)
                k = kv_ref[place, 0, late, :, :width]
                v = kv_ref[place, 0, late, :, width:]
                s = nt(k, q)
                seen = tile_mask(t, own, length, run, tile, rows, half, blocks)
                p = jnp.where(seen, jnp.exp(jnp.where(seen, s - lse, NEG_FILL)), 0.0)
                ds = (p * (nt(v, do) - delta)).astype(BF)
                acc_ref[t, :, :width] += nn(ds, q)
                acc_ref[t, :, width:] += nn(p.astype(BF), do)
                return dq + tn(k, ds)

            dq = lax.fori_loop(0, count, step, jnp.zeros((width, rows), F32))
            done = done + head_part(dq.T, head, heads)
        dq_ref[0, run] = (SCORE_SCALE * done).astype(BF)
    for t in range(2 * blocks):
        place, late = (t, 0) if t < blocks else (2 * blocks - 1 - t, 1)
        dkv_ref[place, 0, late] = acc_ref[t].astype(BF)


def attention_specs(q, kv, heads):
    micros, _, rows, width = q.shape
    blocks, _, _, tile, _ = kv.shape
    per_q = pl.BlockSpec((1, 2, rows, width), lambda m, s: (m, 0, 0, 0))
    per_kv = pl.BlockSpec((blocks, 1, 2, tile, 2 * width), lambda m, s: (0, m, 0, 0, 0))
    per_row = pl.BlockSpec((1, 2, heads, 1, rows), lambda m, s: (m, 0, 0, 0, 0))
    return per_q, per_kv, per_row


def attention_forward(scalars, q, kv, heads, half):
    micros, _, rows, width = q.shape
    blocks, _, _, tile, _ = kv.shape
    per_q, per_kv, per_row = attention_specs(q, kv, heads)
    return pl.pallas_call(
        functools.partial(forward_kernel, blocks=blocks, tile=tile, half=half, heads=heads),
        grid_spec=pltpu.PrefetchScalarGridSpec(
            num_scalar_prefetch=1,
            grid=(micros,),
            in_specs=[per_q, per_kv],
            out_specs=[per_q, per_row],
            scratch_shapes=[pltpu.VMEM((2 * blocks, tile, rows), F32)],
        ),
        out_shape=[
            jax.ShapeDtypeStruct(q.shape, BF),
            jax.ShapeDtypeStruct((micros, 2, heads, 1, rows), F32),
        ],
        compiler_params=pltpu.CompilerParams(vmem_limit_bytes=VMEM_LIMIT),
        cost_estimate=pl.CostEstimate(
            flops=4 * micros * blocks * tile * rows * width * heads,
            bytes_accessed=2 * (q.size * 2 + kv.size),
            transcendentals=micros * blocks * tile * rows * heads,
        ),
    )(scalars, q, kv)


def attention_backward(scalars, q, kv, do, lse, delta, heads, half):
    micros, _, rows, width = q.shape
    blocks, _, _, tile, _ = kv.shape
    per_q, per_kv, per_row = attention_specs(q, kv, heads)
    return pl.pallas_call(
        functools.partial(backward_kernel, blocks=blocks, tile=tile, half=half, heads=heads),
        grid_spec=pltpu.PrefetchScalarGridSpec(
            num_scalar_prefetch=1,
            grid=(micros,),
            in_specs=[per_q, per_kv, per_q, per_row, per_row],
            out_specs=[per_q, per_kv],
            scratch_shapes=[pltpu.VMEM((2 * blocks, tile, 2 * width), F32)],
        ),
        out_shape=[
            jax.ShapeDtypeStruct(q.shape, BF),
            jax.ShapeDtypeStruct(kv.shape, BF),
        ],
        compiler_params=pltpu.CompilerParams(vmem_limit_bytes=VMEM_LIMIT),
        cost_estimate=pl.CostEstimate(
            flops=10 * micros * blocks * tile * rows * width * heads,
            bytes_accessed=2 * (q.size * 3 + kv.size * 2),
            transcendentals=micros * blocks * tile * rows * heads,
        ),
    )(scalars, q, kv, do, lse, delta)


def norm_parts(values):
    inverse = lax.rsqrt(jnp.mean(values * values, -1, keepdims=True) + EPSILON)
    return inverse, values * inverse


def norm_back(upstream, gain, inverse, scaled):
    through = upstream * gain
    inner = jnp.mean(through * scaled, -1, keepdims=True)
    return inverse * (through - scaled * inner)


def rotary_tables(positions):
    half_dim = HEAD_SIZE // 2
    frequency = ROPE_BASE ** (-(jnp.arange(half_dim).astype(F32) * 2.0) / HEAD_SIZE)
    angles = positions.astype(F32)[:, None] * frequency[None, :]
    angles = jnp.concatenate([angles, angles], -1)
    return jnp.cos(angles)[:, None, :], jnp.sin(angles)[:, None, :]


def rotate(values):
    half_dim = values.shape[-1] // 2
    return jnp.concatenate([-values[..., half_dim:], values[..., :half_dim]], -1)


def body(
    inputs,
    cotangent,
    lengths,
    positions,
    attn_gain,
    mlp_gain,
    w_query,
    key_projection,
    value_projection,
    w_out,
    w_gate,
    w_up,
    w_down,
):
    B = lax.axis_size("blk")
    H = lax.axis_size("head")
    me = lax.axis_index("blk")
    mine = lax.axis_index("head")
    T = inputs.shape[1]
    D = MODEL_WIDTH
    half = T // 2
    slots = T * H * B
    tile = H * half
    heads = KEY_VALUE_HEADS // H
    KD = heads * HEAD_SIZE
    QD = KD * SHARED
    tokens = MICRO * T
    group = H * tokens
    wrows = w_query.shape[0]
    F = w_gate.shape[1]
    block = D // B

    def by_group(w):
        return w.reshape(wrows, H, w.shape[1] // H).transpose(1, 0, 2)

    gains = jnp.zeros((wrows, 128), BF)
    gains = gains.at[:, 0].set(attn_gain).at[:, 1].set(mlp_gain)
    pack = jnp.concatenate(
        [
            by_group(w_query),
            by_group(key_projection),
            by_group(value_projection),
            jnp.broadcast_to(gains[None], (H, wrows, 128)),
        ],
        2,
    )
    pack = lax.all_to_all(pack, "head", split_axis=0, concat_axis=0, tiled=True)
    pack = pack.reshape(H * wrows, QD + 2 * KD + 128)
    qkvg = natural(xor_gather(pack, B), me, 0)
    w_qkv = qkvg[:, : QD + 2 * KD]
    gain_cols = qkvg[:, QD + 2 * KD : QD + 2 * KD + 2].astype(F32).T
    gain_one = gain_cols[0]
    gain_two = gain_cols[1]

    linear = me * H + mine
    my_pos = lax.dynamic_slice_in_dim(positions, linear * T, T, axis=1)
    place = jnp.where(
        my_pos < slots // 2, my_pos - half * linear, half + my_pos - (slots - half * (linear + 1))
    )
    order = (place[:, None, :] == jnp.arange(T)[None, :, None]).astype(BF)
    x_own = jnp.einsum("mrs,msd->mrd", order, inputs, preferred_element_type=F32)
    x_own = x_own.astype(BF).reshape(tokens, D)
    upstream = jnp.einsum("mrs,msd->mrd", order, cotangent, preferred_element_type=F32)
    upstream = upstream.reshape(tokens, D)
    x_group = lax.all_gather(x_own, "head", axis=0, tiled=True).astype(F32)
    d_mlp = (RESIDUAL_SCALE * upstream).astype(BF)

    w_out_rows = lax.all_gather(w_out, "head", axis=0, tiled=True)
    w_gate_up = natural(xor_gather(jnp.concatenate([w_gate, w_up], 1), B), me, 0)
    w_o = natural(xor_gather(w_out_rows, B), me, 0)
    w_d = natural(xor_gather(w_down, B), me, 1)

    inv_one, scaled_one = norm_parts(x_group)
    xn1 = (scaled_one * gain_one).astype(BF)
    qkv = nn(xn1, w_qkv)
    run_start = jnp.arange(H)[:, None, None] + me * H
    i = jnp.arange(half)[None, None, :]
    group_pos = jnp.concatenate(
        [half * run_start + i, slots - half * (run_start + 1) + i], 1
    )
    group_pos = jnp.broadcast_to(group_pos[:, None], (H, MICRO, 2, half)).reshape(group)
    cosine, sine = rotary_tables(group_pos)

    def rope(values, width):
        values = values.reshape(group, width // HEAD_SIZE, HEAD_SIZE)
        return values * cosine + rotate(values) * sine

    def rope_back(values, width):
        values = values.astype(F32).reshape(group, width // HEAD_SIZE, HEAD_SIZE)
        return (values * cosine - rotate(values) * sine).astype(BF).reshape(group, width)

    def to_heads(values):
        values = values.reshape(H, MICRO, 2, half, heads, SHARED, HEAD_SIZE)
        return values.transpose(1, 2, 5, 0, 3, 4, 6).reshape(MICRO, 2, SHARED * tile, KD)

    def from_heads(values):
        values = values.reshape(MICRO, 2, SHARED, H, half, heads, HEAD_SIZE)
        return values.transpose(3, 0, 1, 4, 5, 2, 6).reshape(group, QD)

    def to_tiles(values):
        return values.reshape(H, MICRO, 2, half, -1).transpose(1, 2, 0, 3, 4).reshape(
            MICRO, 2, tile, -1
        )

    def from_tiles(values):
        return values.reshape(MICRO, 2, H, half, -1).transpose(2, 0, 1, 3, 4).reshape(group, -1)

    q = to_heads((SCORE_SCALE * rope(qkv[:, :QD], QD).astype(BF)).astype(BF))
    k = rope(qkv[:, QD : QD + KD], KD).astype(BF).reshape(group, KD)
    v = qkv[:, QD + KD :].astype(BF)
    kv = lax.all_gather(to_tiles(jnp.concatenate([k, v], 1)), "blk", axis=0)
    scalars = jnp.concatenate([me[None].astype(jnp.int32), lengths.astype(jnp.int32)])
    o_heads, lse = attention_forward(scalars, q, kv, heads, half)
    o = from_heads(o_heads)
    o_full = lax.all_gather(o, "head", axis=1, tiled=True)

    resid = x_group + RESIDUAL_SCALE * nn(o_full, w_o)
    inv_two, scaled_two = norm_parts(resid)
    xn2 = (scaled_two * gain_two).astype(BF)
    dmo = lax.all_gather(d_mlp, "head", axis=0, tiled=True)
    gate_up = nn(xn2, w_gate_up)
    gate = gate_up[:, :F]
    up = gate_up[:, F:]
    sigma = jax.nn.sigmoid(gate)
    silu = gate * sigma
    hidden = (silu * up).astype(BF)
    d_hidden = nt(dmo, w_d)
    d_gate_up = jnp.concatenate(
        [d_hidden * up * (sigma * (1.0 + gate * (1.0 - sigma))), d_hidden * silu], 1
    ).astype(BF)
    d_xn2 = lax.psum_scatter(
        nt(d_gate_up, w_gate_up).astype(BF), "head", scatter_dimension=0, tiled=True
    ).astype(F32)
    mlp_out = lax.psum_scatter(
        nn(hidden, w_d).astype(BF), "head", scatter_dimension=0, tiled=True
    ).astype(F32)

    def columns(values, j):
        return lax.dynamic_slice_in_dim(values, (me ^ j) * block, block, 1)

    grad_gate_up = xor_scatter(lambda j: tn(columns(xn2, j), d_gate_up).astype(BF), B)
    grad_down = xor_scatter(lambda j: tn(hidden, columns(dmo, j)).astype(BF), B)

    def own(values):
        return lax.dynamic_slice_in_dim(values, mine * tokens, tokens, 0)

    resid_own = own(resid)
    scaled_two_own = own(scaled_two)
    grad_gain_two = jnp.sum(d_xn2 * scaled_two_own, 0)
    d_resid = upstream + norm_back(d_xn2, gain_two, own(inv_two), scaled_two_own)
    d_branch = (RESIDUAL_SCALE * d_resid).astype(BF)
    output = (resid_own + RESIDUAL_SCALE * mlp_out).astype(BF)

    d_attn = nt(d_branch, w_o).astype(BF)
    d_attn = d_attn.reshape(tokens, H, QD).transpose(1, 0, 2)
    d_attn = lax.all_to_all(d_attn, "head", split_axis=0, concat_axis=0, tiled=True)
    d_attn = d_attn.reshape(group, QD)
    delta = jnp.sum((d_attn.astype(F32) * o.astype(F32)).reshape(group, QD // HEAD_SIZE, HEAD_SIZE), -1)
    delta = delta.reshape(H, MICRO, 2, half, heads, SHARED).transpose(1, 2, 4, 5, 0, 3)
    delta = delta.reshape(MICRO, 2, heads, 1, SHARED * tile)
    dq, dkv = attention_backward(scalars, q, kv, to_heads(d_attn), lse, delta, heads, half)
    dkv = lax.psum_scatter(
        dkv.reshape(B * MICRO * 2 * tile, 2 * KD), "blk", scatter_dimension=0, tiled=True
    )
    dkv = from_tiles(dkv)
    d_qkv = jnp.concatenate(
        [rope_back(from_heads(dq), QD), rope_back(dkv[:, :KD], KD), dkv[:, KD:].astype(BF)], 1
    )
    d_xn1_part = nt(d_qkv, w_qkv)
    d_xn1 = lax.psum_scatter(
        d_xn1_part.astype(BF), "head", scatter_dimension=0, tiled=True
    ).astype(F32)
    grad_gain_one = jnp.sum(d_xn1_part * scaled_one, 0)

    d_branch_group = lax.all_gather(d_branch, "head", axis=0, tiled=True)
    grad_out = tn(o, d_branch_group).astype(BF)
    out_rows = QD // B
    grad_out = xor_scatter(
        lambda j: lax.dynamic_slice_in_dim(grad_out, (me ^ j) * out_rows, out_rows, 0), B
    )
    grad_out = lax.ppermute(
        grad_out.astype(BF),
        ("blk", "head"),
        [(b * H + h, h * B + b) for b in range(B) for h in range(H)],
    ).astype(F32)

    gain_grads = jnp.stack([grad_gain_one, grad_gain_two], 1).astype(BF)
    gain_grads = jnp.concatenate([gain_grads, jnp.zeros((D, 126), BF)], 1)

    def qkv_block(j):
        rows = lax.dynamic_slice_in_dim(gain_grads, (me ^ j) * block, block, 0)
        return jnp.concatenate([tn(columns(xn1, j), d_qkv).astype(BF), rows], 1)

    grad_qkv = xor_scatter(qkv_block, B).astype(BF).reshape(H, wrows, QD + 2 * KD + 128)
    grad_qkv = lax.all_to_all(grad_qkv, "head", split_axis=0, concat_axis=0, tiled=True)
    grad_qkv = grad_qkv.astype(F32)
    grad_gains = jnp.sum(grad_qkv[:, :, QD + 2 * KD : QD + 2 * KD + 2], 0)

    def side_by_side(values):
        return values.transpose(1, 0, 2).reshape(wrows, -1)

    scaled_one_own = own(scaled_one)
    d_input = d_resid + norm_back(d_xn1, gain_one, own(inv_one), scaled_one_own)
    output = jnp.einsum(
        "mrs,mrd->msd", order, output.reshape(MICRO, T, D), preferred_element_type=F32
    ).astype(BF)
    d_input = jnp.einsum(
        "mrs,mrd->msd",
        order.astype(F32),
        d_input.reshape(MICRO, T, D),
        precision=lax.Precision.HIGHEST,
        preferred_element_type=F32,
    )
    return (
        output,
        d_input,
        grad_gains[:, 0],
        grad_gains[:, 1],
        side_by_side(grad_qkv[:, :, :QD]),
        side_by_side(grad_qkv[:, :, QD : QD + KD]),
        side_by_side(grad_qkv[:, :, QD + KD : QD + 2 * KD]),
        grad_out,
        grad_gate_up[:, :F],
        grad_gate_up[:, F:],
        grad_down,
    )


def solution(mesh):
    both = ("blk", "head")
    return jax.shard_map(
        body,
        mesh=mesh,
        in_specs=(
            P(None, both, None),
            P(None, both, None),
            P(),
            P(),
            P(both),
            P(both),
            P(both, None),
            P(both, None),
            P(both, None),
            P(both, None),
            P("blk", "head"),
            P("blk", "head"),
            P("head", "blk"),
        ),
        out_specs=(
            P(None, both, None),
            P(None, both, None),
            P(both),
            P(both),
            P(both, None),
            P(both, None),
            P(both, None),
            P(both, None),
            P("blk", "head"),
            P("blk", "head"),
            P("head", "blk"),
        ),
        check_vma=False,
    )
```

```python
import functools

import jax
import jax.numpy as jnp
from jax import lax
from jax.experimental import pallas as pl
from jax.experimental.pallas import tpu as pltpu
from jax.sharding import PartitionSpec as P

MODEL_WIDTH = 2048
QUERY_HEADS = 32
KEY_VALUE_HEADS = 8
HEAD_SIZE = 64
SHARED = QUERY_HEADS // KEY_VALUE_HEADS
MICRO = 2
LANES = 128

SCORE_SCALE = 0.015625
RESIDUAL_SCALE = 0.22
EPSILON = 1e-06
ROPE_BASE = 10000000.0
NEG_FILL = -1e30

BF = jnp.bfloat16
F32 = jnp.float32
VMEM_LIMIT = 56 * 1024 * 1024
COST = 0.1


def dot(left, right, contract):
    return lax.dot_general(left, right, (contract, ((), ())), preferred_element_type=F32)


def nn(left, right):
    return dot(left, right, ((1,), (0,)))


def tn(left, right):
    return dot(left, right, ((0,), (0,)))


def nt(left, right):
    return dot(left, right, ((1,), (1,)))


def swap(x, bit, devices):
    return lax.ppermute(x, "blk", [(i, i ^ bit) for i in range(devices)])


def xor_gather(x, devices, join=None):
    even = [x] + [swap(x, bit, devices) for bit in range(2, devices, 2)]
    even = (join or jnp.stack)(even)
    return even, swap(even, 1, devices)


def add(left, right):
    return (left.astype(F32) + right.astype(F32)).astype(BF)


def core_scatter(held, devices):
    came = [swap(held[bit // 2], bit, devices) for bit in range(2, devices, 2)]
    return sum((part.astype(F32) for part in came), held[0].astype(F32))


def core_scatter_steps(held, devices):
    if devices != 8:
        return core_scatter(held, devices)
    h0, h2, h4, h6 = held
    half = h0.shape[0] // 2
    from_x = swap(h6[:half], 2, devices)
    from_y = swap(h6[half:], 4, devices)
    h4 = jnp.concatenate([add(h4[:half], from_x), h4[half:]], 0)
    h2 = jnp.concatenate([h2[:half], add(h2[half:], from_y)], 0)
    came_x = swap(h2, 2, devices)
    came_y = swap(h4, 4, devices)
    return h0.astype(F32) + came_x.astype(F32) + came_y.astype(F32)


def xor_scatter(even, odd, devices):
    return core_scatter(add(even, swap(odd, 1, devices)), devices)


def head_exchange(parts):
    return lax.all_to_all(parts, "head", split_axis=0, concat_axis=0, tiled=True)


def head_shift(x, by, devices):
    return lax.ppermute(x, "head", [(i, (i + by) % devices) for i in range(devices)])


def head_gather(x, devices):
    return [x] + [head_shift(x, k, devices) for k in range(1, devices)]


def head_deal(parts, devices):
    return [parts[0]] + [head_shift(parts[k], k, devices) for k in range(1, devices)]


def same_core_groups(devices):
    return [list(range(core, devices, 2)) for core in range(2)]


def plane_scatter(kept, devices, axis):
    return lax.psum_scatter(
        kept,
        "blk",
        scatter_dimension=axis,
        tiled=True,
        axis_index_groups=same_core_groups(devices),
    )


def call(kernel, grid, in_specs, out_specs, out_shape, scratch, flops, moved, args, wait=()):
    wait = tuple(wait)
    given = 1 + len(in_specs)
    in_specs = list(in_specs) + [pl.BlockSpec(memory_space=pl.ANY)] * len(wait)
    args = tuple(args) + wait

    def run(*refs):
        kernel(*refs[:given], *refs[given + len(wait) :])

    return pl.pallas_call(
        run,
        grid_spec=pltpu.PrefetchScalarGridSpec(
            num_scalar_prefetch=1,
            grid=grid,
            in_specs=in_specs,
            out_specs=out_specs,
            scratch_shapes=scratch,
        ),
        out_shape=out_shape,
        compiler_params=pltpu.CompilerParams(vmem_limit_bytes=VMEM_LIMIT),
        cost_estimate=pl.CostEstimate(
            flops=int(flops * COST), bytes_accessed=int(moved * COST), transcendentals=0
        ),
    )(*args)


def whole(shape):
    return pl.BlockSpec(shape, lambda *_: (0,) * len(shape))


def shape_of(shape, dtype):
    return jax.ShapeDtypeStruct(shape, dtype)


def chunk(scalars, j, width):
    return pl.ds(pl.multiple_of((scalars[0] ^ j) * width, LANES), width)


def turned(values):
    lane = lax.broadcasted_iota(jnp.int32, values.shape, 1) % HEAD_SIZE
    quarter = HEAD_SIZE // 2
    return jnp.where(
        lane < quarter,
        pltpu.roll(values, LANES - quarter, 1),
        pltpu.roll(values, quarter, 1),
    )


def rope_lanes(values, cosine, sine, first, limit):
    out = values * cosine + turned(values) * sine
    if first + LANES <= limit:
        return out
    lane = lax.broadcasted_iota(jnp.int32, values.shape, 1)
    return jnp.where(lane < limit - first, out, values)


def before(s, k, devices):
    return (s[1] + devices - k) % devices


def after(s, k, devices):
    return (s[1] + k) % devices


def order_kernel(s, x_ref, up_ref, place_ref, xs_ref, us_ref):
    M, T, D = x_ref.shape
    for m in range(M):
        rank = lax.broadcasted_iota(jnp.int32, (T, T), 0)
        order = (place_ref[m] == rank).astype(BF)
        at = pl.ds(m * T, T)
        x = nn(order, x_ref[m]).astype(BF)
        for h in range(xs_ref.shape[0]):
            xs_ref[h, at, :] = x
        us_ref[at, :] = nn(order, up_ref[m]).astype(BF)


def in_order(scalars, x, upstream, place, H, wait):
    M, T, D = x.shape
    out = shape_of((M * T, D), BF)
    return call(
        order_kernel,
        (1,),
        [whole(x.shape), whole(x.shape), whole((M, 1, T))],
        [whole((H,) + out.shape), whole(out.shape)],
        [shape_of((H,) + out.shape, BF), out],
        [],
        4 * M * T * T * D,
        10 * M * T * D,
        (scalars, x, upstream, place.reshape(M, 1, T)),
        wait,
    )


def pack_kernel(s, q_ref, k_ref, v_ref, g_ref, *outs):
    devices = len(outs)
    QD = q_ref.shape[1] // devices
    KD = k_ref.shape[1] // devices
    for k, out_ref in enumerate(outs):
        for h in range(devices):

            @pl.when(after(s, k, devices) == h)
            def _(out_ref=out_ref, h=h):
                out_ref[:, :QD] = q_ref[:, h * QD : (h + 1) * QD]
                out_ref[:, QD : QD + 2 * KD] = jnp.concatenate(
                    [k_ref[:, h * KD : (h + 1) * KD], v_ref[:, h * KD : (h + 1) * KD]], 1
                )
                out_ref[:, QD + 2 * KD :] = g_ref[...]


def pack_weights(scalars, w_query, w_key, w_value, gains, devices):
    rows = w_query.shape[0]
    columns = (w_query.shape[1] + w_key.shape[1] + w_value.shape[1]) // devices + LANES
    out = shape_of((rows, columns), BF)
    args = (scalars, w_query, w_key, w_value, gains)
    return call(
        pack_kernel,
        (1,),
        [whole(a.shape) for a in args[1:]],
        [whole(out.shape)] * devices,
        [out] * devices,
        [],
        0,
        8 * rows * columns * devices,
        args,
    )


def copies_kernel(s, from_ref, out_ref, *, scale):
    values = from_ref[...]
    if scale is not None:
        values = (scale * values.astype(F32)).astype(BF)
    for h in range(out_ref.shape[0]):
        out_ref[h] = values


def copies(scalars, values, H, scale, wait):
    shape = (H,) + values.shape
    return call(
        functools.partial(copies_kernel, scale=scale),
        (1,),
        [whole(values.shape)],
        [whole(shape)],
        [shape_of(shape, BF)],
        [],
        0,
        4 * H * values.size,
        (scalars, values),
        wait,
    )[0]


def hold_kernel(s, *refs):
    count = len(refs) // 2
    for from_ref, to_ref in zip(refs[:count], refs[count:]):
        to_ref[...] = from_ref[...]


def hold(scalars, arrays, wait):
    return call(
        hold_kernel,
        (1,),
        [whole(a.shape) for a in arrays],
        [whole(a.shape) for a in arrays],
        [shape_of(a.shape, a.dtype) for a in arrays],
        [],
        0,
        sum(4 * a.size for a in arrays),
        (scalars, *arrays),
        wait,
    )


def join_kernel(s, *refs):
    *parts, out_ref = refs
    for p, part_ref in enumerate(parts):
        out_ref[p] = part_ref[...]


def join(scalars, parts, wait=()):
    shape = (len(parts),) + parts[0].shape
    return call(
        join_kernel,
        (1,),
        [whole(p.shape) for p in parts],
        [whole(shape)],
        [shape_of(shape, parts[0].dtype)],
        [],
        0,
        4 * len(parts) * parts[0].size,
        (scalars, *parts),
        wait,
    )[0]


def wide_kernel(s, from_ref, out_ref):
    out_ref[...] = from_ref[...].astype(F32)


def wide(scalars, values, wait):
    rows, columns = values.shape
    piece = pl.BlockSpec((rows // 4, columns), lambda i, s: (i, 0))
    return call(
        wide_kernel,
        (4,),
        [piece],
        [piece],
        [shape_of(values.shape, F32)],
        [],
        0,
        6 * values.size,
        (scalars, values),
        wait,
    )[0]


def arrange_kernel(s, *refs):
    *parts, out_ref = refs
    for k, part_ref in enumerate(parts):
        out_ref[before(s, k, len(parts))] = part_ref[...]


def arrange(scalars, parts, wait=()):
    shape = (len(parts),) + parts[0].shape
    return call(
        arrange_kernel,
        (1,),
        [whole(p.shape) for p in parts],
        [whole(shape)],
        [shape_of(shape, parts[0].dtype)],
        [],
        0,
        4 * len(parts) * parts[0].size,
        (scalars, *parts),
        wait,
    )[0]


def project_kernel(s, x_ref, we_ref, wo_ref, cos_ref, sin_ref, xn_ref, q_ref, kv_ref, gain_ref):
    H, _, T, D = x_ref.shape
    places, block, columns = we_ref.shape
    QD = q_ref.shape[-1]
    KD = kv_ref.shape[-1] // 2
    used = QD + 2 * KD

    @pl.when(pl.program_id(0) == 0)
    def _():
        for place in range(places):
            for parity, w_ref in enumerate((we_ref, wo_ref)):
                held = w_ref[place, :, used : used + LANES].astype(F32).T
                gain_ref[:, chunk(s, 2 * place + parity, block)] = held[:8]

    x = x_ref[:, 0].reshape(H * T, D).astype(F32)
    inverse = lax.rsqrt(jnp.mean(x * x, -1, keepdims=True) + EPSILON)
    xn = ((x * inverse) * gain_ref[0:1, :]).astype(BF)
    xn_ref[:, 0] = xn.reshape(H, T, D)
    acc = jnp.zeros((H * T, used), F32)
    for place in range(places):
        for parity, w_ref in enumerate((we_ref, wo_ref)):
            left = xn_ref[:, 0, :, chunk(s, 2 * place + parity, block)].reshape(H * T, block)
            acc = acc + nn(left, w_ref[place, :, :used])
    cosine = cos_ref[...]
    sine = sin_ref[...]
    for first in range(0, used, LANES):
        part = acc[:, first : first + LANES]
        if first < QD + KD:
            part = rope_lanes(part, cosine, sine, first, QD + KD)
        if first < QD:
            q_ref[:, 0, :, first : first + LANES] = (
                (part * SCORE_SCALE).astype(BF).reshape(H, T, LANES)
            )
        else:
            kv_ref[:, 0, :, first - QD : first - QD + LANES] = part.astype(BF).reshape(H, T, LANES)


def project(scalars, x, w_even, w_odd, cosine, sine, QD, KD, wait):
    H, M, T, D = x.shape
    used = QD + 2 * KD

    def rows(width):
        return pl.BlockSpec((H, 1, T, width), lambda m, s: (0, m, 0, 0))

    return call(
        project_kernel,
        (M,),
        [rows(D), whole(w_even.shape), whole(w_odd.shape), whole(cosine.shape), whole(sine.shape)],
        [rows(D), rows(QD), rows(2 * KD), whole((8, D))],
        [
            shape_of((H, M, T, D), BF),
            shape_of((H, M, T, QD), BF),
            shape_of((H, M, T, 2 * KD), BF),
            shape_of((8, D), F32),
        ],
        [],
        2 * H * M * T * D * used,
        4 * H * M * T * D + 4 * w_even.size,
        (scalars, x, w_even, w_odd, cosine, sine),
        wait,
    )


def run_offset(index, run, tile, half):
    if run == 0:
        return index
    return (tile - half) - (index // half) * half + index % half


def key_positions(s, natural, run, length, tile, half, blocks):
    row = lax.broadcasted_iota(jnp.int32, (4 * tile, 1), 0)
    part = row // tile
    owner = 4 * natural + ((s[0] & 3) ^ (((part & 1) << 1) | (part >> 1)))
    row_tile = owner if run == 0 else 2 * blocks - 1 - owner
    position = row_tile * tile + run_offset(row % tile, run, tile, half)
    return jnp.where(position < length, position, jnp.int32(1 << 30))


def query_positions(s, run, rows, tile, half, blocks):
    own = s[0] if run == 0 else 2 * blocks - 1 - s[0]
    lane = lax.broadcasted_iota(jnp.int32, (1, rows), 1) % tile
    return own * tile + run_offset(lane, run, tile, half)


def slab(even_ref, odd_ref, y, run, first, last):
    parts = [
        ref[2 * y + i, :, 0, run, :, first:last] for ref in (even_ref, odd_ref) for i in range(2)
    ]
    H, half, width = parts[0].shape
    return jnp.concatenate([part.reshape(H * half, width) for part in parts], 0)


def heads_across(ref, run, head, heads):
    H, _, _, half, _ = ref.shape
    first = head * SHARED * HEAD_SIZE
    values = ref[:, 0, run, :, first : first + SHARED * HEAD_SIZE]
    values = values.reshape(H * half, SHARED * HEAD_SIZE).astype(F32).T
    values = jnp.concatenate(
        [values[g * HEAD_SIZE : (g + 1) * HEAD_SIZE] for g in range(SHARED)], 1
    )
    return values


def padded(values, head, heads):
    values = values.astype(BF)
    if heads == 1:
        return values
    zeros = jnp.zeros_like(values)
    return jnp.concatenate([values, zeros] if head == 0 else [zeros, values], 0)


def heads_back(values, tile):
    return jnp.concatenate(
        [values[:, g * tile : (g + 1) * tile] for g in range(SHARED)], 0
    ).T


def slab_loops(s, length, run, tile, blocks, state, step):
    slabs = blocks // 4
    own = s[0] // 4
    if run == 0:
        return lax.fori_loop(0, own + 1, lambda n, st: step(st, n, 0, True), state)
    state = lax.fori_loop(0, slabs, lambda n, st: step(st, n, 0, False), state)
    within = (2 * blocks * tile - length) // (4 * tile)
    return lax.fori_loop(
        jnp.maximum(own, within), slabs, lambda n, st: step(st, n, 1, True), state
    )


def fold_rows(values, combine):
    rows, lanes = values.shape
    return combine(values.reshape(rows // 8, 8, lanes), axis=0)


def forward_kernel(s, q_ref, ke_ref, ko_ref, o_ref, lse_ref, *, heads):
    H, _, _, half, QD = q_ref.shape
    blocks = 2 * ke_ref.shape[0]
    tile = H * half
    width = heads * HEAD_SIZE
    rows = SHARED * tile
    length = s[2 + pl.program_id(0)]
    for run in range(2):
        q = [padded(heads_across(q_ref, run, head, heads), head, heads) for head in range(heads)]
        at = query_positions(s, run, rows, tile, half, blocks)

        def step(state, natural, key_run, masked, q=q, at=at):
            y = natural ^ (s[0] >> 2)
            k = slab(ke_ref, ko_ref, y, key_run, 0, width)
            v = slab(ke_ref, ko_ref, y, key_run, width, 2 * width)
            if masked:
                seen = key_positions(s, natural, key_run, length, tile, half, blocks) <= at
            new = []
            for head in range(heads):
                top, total, acc = state[head]
                scores = nn(k, q[head])
                if masked:
                    scores = jnp.where(seen, scores, NEG_FILL)
                best = jnp.maximum(top, jnp.max(fold_rows(scores, jnp.max), 0, keepdims=True))
                p = jnp.exp(scores - best)
                scale = jnp.exp(top - best)
                total = total * scale + jnp.sum(fold_rows(p, jnp.sum), 0, keepdims=True)
                new.append((best, total, acc * scale + tn(v, p.astype(BF))))
            return tuple(new)

        start = tuple(
            (
                jnp.full((1, rows), NEG_FILL, F32),
                jnp.zeros((1, rows), F32),
                jnp.zeros((width, rows), F32),
            )
            for _ in range(heads)
        )
        done = slab_loops(s, length, run, tile, blocks, start, step)
        for head in range(heads):
            top, total, acc = done[head]
            lse_ref[0, run, head] = top + jnp.log(total)
            out = acc[head * HEAD_SIZE : (head + 1) * HEAD_SIZE] / total
            first = head * SHARED * HEAD_SIZE
            o_ref[:, 0, run, :, first : first + SHARED * HEAD_SIZE] = (
                heads_back(out, tile).astype(BF).reshape(H, half, SHARED * HEAD_SIZE)
            )


def backward_kernel(
    s, q_ref, ke_ref, ko_ref, o_ref, lse_ref, cos_ref, sin_ref, *refs, heads
):
    H, _, _, half, QD = q_ref.shape
    dq_ref, de_ref, dod_ref, acc_ref, do_ref = refs[H:]
    for k in range(H):
        do_ref[before(s, k, H), 0] = refs[k][0]
    blocks = 2 * ke_ref.shape[0]
    tile = H * half
    width = heads * HEAD_SIZE
    rows = SHARED * tile
    length = s[2 + pl.program_id(0)]
    acc_ref[...] = jnp.zeros(acc_ref.shape, F32)
    for run in range(2):
        q, do, lse, delta = [], [], [], []
        for head in range(heads):
            q.append(padded(heads_across(q_ref, run, head, heads), head, heads))
            up = heads_across(do_ref, run, head, heads)
            do.append(padded(up, head, heads))
            delta.append(
                jnp.sum(up * heads_across(o_ref, run, head, heads), 0, keepdims=True)
            )
            lse.append(lse_ref[0, run, head])
        at = query_positions(s, run, rows, tile, half, blocks)

        def step(state, natural, key_run, masked, q=q, do=do, lse=lse, delta=delta, at=at):
            y = natural ^ (s[0] >> 2)
            k = slab(ke_ref, ko_ref, y, key_run, 0, width)
            v = slab(ke_ref, ko_ref, y, key_run, width, 2 * width)
            if masked:
                seen = key_positions(s, natural, key_run, length, tile, half, blocks) <= at
            new = []
            dk = jnp.zeros((4 * tile, width), F32)
            dv = jnp.zeros((4 * tile, width), F32)
            for head in range(heads):
                p = jnp.exp(nn(k, q[head]) - lse[head])
                if masked:
                    p = jnp.where(seen, p, 0.0)
                ds = (p * (nn(v, do[head]) - delta[head])).astype(BF)
                dk = dk + nt(ds, q[head])
                dv = dv + nt(p.astype(BF), do[head])
                new.append(state[head] + tn(k, ds))
            acc_ref[key_run, y, :, :width] += dk
            acc_ref[key_run, y, :, width:] += dv
            return tuple(new)

        start = tuple(jnp.zeros((width, rows), F32) for _ in range(heads))
        done = slab_loops(s, length, run, tile, blocks, start, step)
        cosine = cos_ref[:, run].reshape(tile, LANES)
        sine = sin_ref[:, run].reshape(tile, LANES)
        for head in range(heads):
            out = done[head][head * HEAD_SIZE : (head + 1) * HEAD_SIZE]
            out = (heads_back(out, tile) * SCORE_SCALE).astype(BF).astype(F32)
            for lanes in range(0, SHARED * HEAD_SIZE, LANES):
                part = out[:, lanes : lanes + LANES]
                part = part * cosine - turned(part) * sine
                first = head * SHARED * HEAD_SIZE + lanes
                dq_ref[:, 0, run, :, first : first + LANES] = part.astype(BF).reshape(
                    H, half, LANES
                )
    for run in range(2):
        for y in range(blocks // 4):
            for index, (ref, i) in enumerate(((de_ref, 0), (de_ref, 1), (dod_ref, 0), (dod_ref, 1))):
                ref[2 * y + i, :, 0, run] = (
                    acc_ref[run, y, index * tile : (index + 1) * tile]
                    .astype(BF)
                    .reshape(H, half, 2 * width)
                )


def attention_specs(q, kv, heads):
    H, M, _, half, QD = q.shape
    places, _, _, _, _, width = kv.shape
    per_q = pl.BlockSpec((H, 1, 2, half, QD), lambda m, s: (0, m, 0, 0, 0))
    per_kv = pl.BlockSpec((places, H, 1, 2, half, width), lambda m, s: (0, 0, m, 0, 0, 0))
    per_row = pl.BlockSpec((1, 2, heads, 1, SHARED * H * half), lambda m, s: (m, 0, 0, 0, 0))
    work = M * places * H * half * SHARED * H * half * QD
    return per_q, per_kv, per_row, work


def attention_forward(scalars, q, k_even, k_odd, heads, wait):
    H, M, _, half, QD = q.shape
    per_q, per_kv, per_row, work = attention_specs(q, k_even, heads)
    return call(
        functools.partial(forward_kernel, heads=heads),
        (M,),
        [per_q, per_kv, per_kv],
        [per_q, per_row],
        [shape_of(q.shape, BF), shape_of((M, 2, heads, 1, SHARED * H * half), F32)],
        [],
        8 * work,
        2 * (2 * q.size + 2 * k_even.size),
        (scalars, q, k_even, k_odd),
        wait,
    )


def attention_backward(scalars, q, k_even, k_odd, do_parts, o, lse, cosine, sine, heads, wait):
    H, M, _, half, QD = q.shape
    per_q, per_kv, per_row, work = attention_specs(q, k_even, heads)
    blocks = 2 * k_even.shape[0]
    return call(
        functools.partial(backward_kernel, heads=heads),
        (M,),
        [per_q, per_kv, per_kv, per_q, per_row, whole(cosine.shape), whole(sine.shape)]
        + [pl.BlockSpec((1, 2, half, QD), lambda m, s: (m, 0, 0, 0))] * H,
        [per_q, per_kv, per_kv],
        [shape_of(q.shape, BF), shape_of(k_even.shape, BF), shape_of(k_odd.shape, BF)],
        [
            pltpu.VMEM((2, blocks // 4, 4 * H * half, 2 * heads * HEAD_SIZE), F32),
            pltpu.VMEM((H, 1, 2, half, QD), BF),
        ],
        20 * work,
        2 * (4 * q.size + 4 * k_even.size),
        (scalars, q, k_even, k_odd, o, lse, cosine, sine, *do_parts),
        wait,
    )


def out_kernel(s, x_ref, gain_ref, we_ref, wo_ref, *refs):
    devices = len(refs) - 5
    xn_ref, own_ref, o_own_ref, acc_ref, o_ref = refs[devices:]
    n = pl.program_id(0)
    _, group, QD = o_ref.shape
    places, width, columns = we_ref.shape
    each = QD // width
    rows = group // devices

    @pl.when(n == 0)
    def _():
        for k in range(devices):
            o_ref[before(s, k, devices)] = refs[k][...]
        at = pl.ds(pl.multiple_of(s[1] * rows, rows), rows)
        for h in range(devices):
            o_own_ref[:, h * QD : (h + 1) * QD] = o_ref[h, at, :]

    got = jnp.zeros((group, columns), F32)
    for place in range(places):
        for parity, w_ref in enumerate((we_ref, wo_ref)):
            c = s[0] ^ (2 * place + parity)
            lanes = pl.ds(pl.multiple_of((c % each) * width, LANES), width)
            got = got + nn(o_ref[c // each, :, lanes], w_ref[place])
    acc_ref[:, pl.ds(pl.multiple_of(n * columns, LANES), columns)] = got

    @pl.when(n == pl.num_programs(0) - 1)
    def _():
        def finish(h, carry):
            at = pl.ds(pl.multiple_of(h * rows, rows), rows)
            resid = x_ref[at, :].astype(F32) + RESIDUAL_SCALE * acc_ref[at, :]
            inverse = lax.rsqrt(jnp.mean(resid * resid, -1, keepdims=True) + EPSILON)
            xn_ref[at, :] = ((resid * inverse) * gain_ref[1:2, :]).astype(BF)

            @pl.when(h == s[1])
            def _():
                own_ref[...] = resid

            return carry

        lax.fori_loop(0, devices, finish, 0)


def out_project(scalars, o_parts, x, gains, w_even, w_odd, wait):
    H = len(o_parts)
    group, QD = o_parts[0].shape
    places, width, D = w_even.shape
    rows = group // H
    columns = 512
    piece = pl.BlockSpec((places, width, columns), lambda n, s: (0, 0, n))
    return call(
        out_kernel,
        (D // columns,),
        [whole(x.shape), whole(gains.shape), piece, piece] + [whole((group, QD))] * H,
        [whole((group, D)), whole((rows, D)), whole((rows, H * QD))],
        [shape_of((group, D), BF), shape_of((rows, D), F32), shape_of((rows, H * QD), BF)],
        [pltpu.VMEM((group, D), F32), pltpu.VMEM((H, group, QD), BF)],
        2 * group * H * QD * D,
        2 * (H * group * QD + 2 * x.size + 2 * w_even.size),
        (scalars, x, gains, w_even, w_odd, *o_parts),
        wait,
    )


def mlp_forward_kernel(s, xn_ref, wg_ref, wu_ref, gate_ref, up_ref, hidden_ref):
    gate = nn(xn_ref[...], wg_ref[...])
    up = nn(xn_ref[...], wu_ref[...])
    gate_ref[...] = gate
    up_ref[...] = up
    hidden_ref[...] = (gate * (1.0 / (1.0 + jnp.exp(-gate))) * up).astype(BF)


def mlp_forward(scalars, xn, w_gate_up, tile, wait):
    group, D = xn.shape
    F = w_gate_up.shape[1] // 2
    count = F // tile
    out = pl.BlockSpec((group, tile), lambda f, s: (0, f))
    return call(
        mlp_forward_kernel,
        (count,),
        [
            whole(xn.shape),
            pl.BlockSpec((D, tile), lambda f, s: (0, f)),
            pl.BlockSpec((D, tile), lambda f, s: (0, f + count)),
        ],
        [out, out, out],
        [shape_of((group, F), F32), shape_of((group, F), F32), shape_of((group, F), BF)],
        [],
        4 * group * D * F,
        2 * (group * D + 2 * D * F + 5 * group * F),
        (scalars, xn, w_gate_up, w_gate_up),
        wait,
    )


def down_kernel(s, hidden_ref, w_ref, out_ref):
    out_ref[...] = nn(hidden_ref[...], w_ref[...]).astype(BF)


def down_project(scalars, hidden, w_down, wait):
    group, F = hidden.shape
    D = w_down.shape[1]
    width = 512
    return call(
        down_kernel,
        (D // width,),
        [whole(hidden.shape), pl.BlockSpec((F, width), lambda n, s: (0, n))],
        [pl.BlockSpec((group, width), lambda n, s: (0, n))],
        [shape_of((group, D), BF)],
        [],
        2 * group * D * F,
        2 * (group * D + D * F + group * F),
        (scalars, hidden, w_down),
        wait,
    )[0]


def mlp_backward_kernel(
    s, gate_ref, up_ref, wg_ref, wu_ref, wd_ref, dmo_ref, dg_ref, du_ref, dxn_ref, acc_ref
):
    f = pl.program_id(0)
    d_hidden = nt(dmo_ref[...], wd_ref[...])
    gate = gate_ref[...]
    sigma = 1.0 / (1.0 + jnp.exp(-gate))
    dg_ref[...] = (d_hidden * up_ref[...] * (sigma * (1.0 + gate * (1.0 - sigma)))).astype(BF)
    du_ref[...] = (d_hidden * (gate * sigma)).astype(BF)
    got = nt(dg_ref[...], wg_ref[...]) + nt(du_ref[...], wu_ref[...])

    @pl.when(f == 0)
    def _():
        acc_ref[...] = got

    @pl.when(f > 0)
    def _():
        acc_ref[...] += got

    @pl.when(f == pl.num_programs(0) - 1)
    def _():
        dxn_ref[...] = acc_ref[...].astype(BF)


def mlp_backward(scalars, gate, up, dmo, w_gate_up, w_down, tile, wait):
    group, D = dmo.shape
    F = gate.shape[1]
    count = F // tile
    per_f = pl.BlockSpec((group, tile), lambda f, s: (0, f))
    return call(
        mlp_backward_kernel,
        (count,),
        [
            per_f,
            per_f,
            pl.BlockSpec((D, tile), lambda f, s: (0, f)),
            pl.BlockSpec((D, tile), lambda f, s: (0, f + count)),
            pl.BlockSpec((tile, D), lambda f, s: (f, 0)),
            whole((group, D)),
        ],
        [per_f, per_f, whole((group, D))],
        [shape_of((group, F), BF), shape_of((group, F), BF), shape_of((group, D), BF)],
        [pltpu.VMEM((group, D), F32)],
        6 * group * D * F,
        2 * (3 * group * D + 3 * D * F + 6 * group * F),
        (scalars, gate, up, w_gate_up, w_gate_up, w_down, dmo),
        wait,
    )


def block_lanes(s, own, near, block):
    i = pl.program_id(0)
    if near:
        index = s[0] ^ (2 * i if own else 2 * i + 1)
    else:
        index = 2 * i + (s[0] % 2 if own else 1 - s[0] % 2)
    return pl.ds(pl.multiple_of(index * block, LANES), block)


def rows_kernel(s, left_ref, *refs, own, count, near):
    right = refs[:count]
    out_ref = refs[-1]
    block = out_ref.shape[0]
    lanes = block_lanes(s, own, near, block)
    left = left_ref[:, lanes]
    at = 0
    for i, right_ref in enumerate(right):
        width = right_ref.shape[1]
        got = tn(left, right_ref[...])
        if own:
            got = got + refs[count][:, at : at + width].astype(F32)
        out_ref[:, at : at + width] = got.astype(BF)
        at += width


def grad_rows(scalars, left, rights, blocks, came=None, near=False, wait=()):
    n, D = left.shape
    block = D // blocks
    width = sum(r.shape[1] for r in rights)
    piece = pl.BlockSpec((block, width), lambda i, s: (i, 0))
    extra = [] if came is None else [came]
    return call(
        functools.partial(
            rows_kernel, own=came is not None, count=len(rights), near=near
        ),
        (blocks // 2,),
        [whole(left.shape)] + [whole(r.shape) for r in rights] + [piece] * len(extra),
        [piece],
        [shape_of((D // 2, width), BF)],
        [],
        n * D * width,
        2 * (left.size + n * width + D * width),
        (scalars, left, *rights, *extra),
        wait,
    )[0]


def columns_kernel(s, left_ref, right_ref, *refs, own):
    out_ref = refs[-1]
    got = tn(left_ref[...], right_ref[:, block_lanes(s, own, True, out_ref.shape[2])])
    if own:
        got = got + refs[0][0].astype(F32)
    out_ref[0] = got.astype(BF)


def grad_columns(scalars, left, right, blocks, came=None, wait=()):
    n, F = left.shape
    D = right.shape[1]
    block = D // blocks
    piece = pl.BlockSpec((1, F, block), lambda i, s: (i, 0, 0))
    extra = [] if came is None else [came]
    return call(
        functools.partial(columns_kernel, own=came is not None),
        (blocks // 2,),
        [whole(left.shape), whole(right.shape)] + [piece] * len(extra),
        [piece],
        [shape_of((blocks // 2, F, block), BF)],
        [],
        n * D * F,
        2 * (left.size + right.size + D * F),
        (scalars, left, right, *extra),
        wait,
    )[0]


def through_norm(upstream, gain, values):
    inverse = lax.rsqrt(jnp.mean(values * values, -1, keepdims=True) + EPSILON)
    scaled = values * inverse
    through = upstream * gain
    inner = jnp.mean(through * scaled, -1, keepdims=True)
    return inverse * (through - scaled * inner), scaled


def branch_kernel(s, parts, resid_ref, up_ref, gain_ref, we_ref, wo_ref, *refs):
    devices = len(refs) - 4
    dresid_ref, da_ref, gg_ref = refs[:3]
    outs = refs[3:-1]
    dattn_ref = refs[-1]
    p = pl.program_id(0)
    _, tokens, QD = dattn_ref.shape
    width = we_ref.shape[1]
    each = QD // width

    @pl.when(p == 0)
    def _():
        upstream = parts[0].astype(F32)
        for h in range(1, parts.shape[0]):
            upstream = upstream + parts[h].astype(F32)
        back, scaled = through_norm(upstream, gain_ref[1:2, :], resid_ref[...])
        gg_ref[...] = jnp.broadcast_to(
            jnp.sum(upstream * scaled, 0, keepdims=True), gg_ref.shape
        )
        d_resid = up_ref[...].astype(F32) + back
        dresid_ref[...] = d_resid
        da_ref[...] = (RESIDUAL_SCALE * d_resid).astype(BF)

    for parity, w_ref in enumerate((we_ref, wo_ref)):
        c = s[0] ^ (2 * p + parity)
        dattn_ref[c // each, :, pl.ds(pl.multiple_of((c % each) * width, LANES), width)] = nt(
            da_ref[...], w_ref[0]
        ).astype(BF)

    @pl.when(p == pl.num_programs(0) - 1)
    def _():
        for k in range(devices):
            outs[k][...] = dattn_ref[after(s, k, devices)]


def branch_back(scalars, parts, resid, upstream, gains, w_even, w_odd, QD, H, wait):
    _, tokens, D = parts.shape
    places, width, _ = w_even.shape
    piece = pl.BlockSpec((1, width, D), lambda p, s: (p, 0, 0))
    return call(
        branch_kernel,
        (places,),
        [whole(a.shape) for a in (parts, resid, upstream, gains)] + [piece, piece],
        [whole((tokens, D)), whole((tokens, D)), whole((8, D))] + [whole((tokens, QD))] * H,
        [shape_of((tokens, D), F32), shape_of((tokens, D), BF), shape_of((8, D), F32)]
        + [shape_of((tokens, QD), BF)] * H,
        [pltpu.VMEM((H, tokens, QD), BF)],
        2 * tokens * D * H * QD,
        2 * (H * tokens * D + 2 * w_even.size + 6 * tokens * D),
        (scalars, parts, resid, upstream, gains, w_even, w_odd),
        wait,
    )


def input_kernel(
    s, dq_ref, dkv_ref, cos_ref, sin_ref, x_ref, xn_ref, gg_ref, we_ref, wo_ref, *refs
):
    out_ref, ge_ref, go_ref, dqkv_ref, inv_ref = refs
    p = pl.program_id(0)
    group, QD = dq_ref.shape
    KD = dkv_ref.shape[1] // 2
    used = QD + 2 * KD
    block = we_ref.shape[1]

    @pl.when(p == 0)
    def _():
        dqkv_ref[:, :QD] = dq_ref[...]
        for first in range(0, 2 * KD, LANES):
            part = dkv_ref[:, first : first + LANES].astype(F32)
            if first < KD:
                part = rope_lanes(part, cos_ref[...], -sin_ref[...], first, KD)
            dqkv_ref[:, QD + first : QD + first + LANES] = part.astype(BF)
        x = x_ref[...].astype(F32)
        inv_ref[...] = jnp.broadcast_to(
            lax.rsqrt(jnp.mean(x * x, -1, keepdims=True) + EPSILON), inv_ref.shape
        )

    for parity, (w_ref, g_ref) in enumerate(((we_ref, ge_ref), (wo_ref, go_ref))):
        lanes = chunk(s, 2 * p + parity, block)
        dxn = nt(dqkv_ref[...], w_ref[0, :, :used])
        out_ref[:, lanes] = dxn.astype(BF)
        scaled = x_ref[:, lanes].astype(F32) * inv_ref[:, 0:1]
        gain_one = jnp.sum(dxn * scaled, 0, keepdims=True)
        g_ref[0, :, :used] = tn(xn_ref[:, lanes], dqkv_ref[...]).astype(BF)
        row = lax.broadcasted_iota(jnp.int32, (LANES, block), 0)
        both = jnp.where(row == 0, gain_one, jnp.where(row == 1, gg_ref[0:1, lanes], 0.0))
        g_ref[0, :, used:] = both.T.astype(BF)


def input_back(scalars, dq, dkv, cosine, sine, x, xn, gain_two, w_even, w_odd, wait):
    group, D = x.shape
    QD = dq.shape[1]
    places, block, columns = w_even.shape
    piece = pl.BlockSpec((1, block, columns), lambda p, s: (p, 0, 0))
    return call(
        input_kernel,
        (places,),
        [whole(a.shape) for a in (dq, dkv, cosine, sine, x, xn, gain_two)] + [piece, piece],
        [whole(x.shape), piece, piece],
        [shape_of(x.shape, BF), shape_of(w_even.shape, BF), shape_of(w_even.shape, BF)],
        [
            pltpu.VMEM((group, QD + dkv.shape[1]), BF),
            pltpu.VMEM((group, LANES), F32),
        ],
        4 * group * D * (QD + dkv.shape[1]),
        2 * (3 * x.size + 4 * w_even.size),
        (scalars, dq, dkv, cosine, sine, x, xn, gain_two, w_even, w_odd),
        wait,
    )


def body(
    inputs,
    cotangent,
    lengths,
    positions,
    attn_gain,
    mlp_gain,
    w_query,
    key_projection,
    value_projection,
    w_out,
    w_gate,
    w_up,
    w_down,
):
    B = lax.axis_size("blk")
    H = lax.axis_size("head")
    me = lax.axis_index("blk")
    mine = lax.axis_index("head")
    T = inputs.shape[1]
    D = MODEL_WIDTH
    half = T // 2
    slots = T * H * B
    heads = KEY_VALUE_HEADS // H
    KD = heads * HEAD_SIZE
    QD = KD * SHARED
    used = QD + 2 * KD
    tokens = MICRO * T
    group = H * tokens
    wrows = w_query.shape[0]
    F = w_gate.shape[1]
    block = D // B
    tile = min(512, F)

    scalars = jnp.concatenate(
        [jnp.stack([me, mine]).astype(jnp.int32), lengths.astype(jnp.int32)]
    )

    gains = jnp.concatenate(
        [attn_gain[:, None], mlp_gain[:, None], jnp.zeros((wrows, LANES - 2), BF)], 1
    )
    pack = pack_weights(scalars, w_query, key_projection, value_projection, gains, H)
    linear = me * H + mine
    my_pos = lax.dynamic_slice_in_dim(positions, linear * T, T, axis=1)
    place = jnp.where(
        my_pos < slots // 2, my_pos - half * linear, half + my_pos - (slots - half * (linear + 1))
    ).astype(jnp.int32)
    order = (place[:, None, :] == jnp.arange(T)[None, :, None]).astype(BF)
    pack = arrange(scalars, head_deal(pack, H)).reshape(H * wrows, used + LANES)
    x_copies, upstream = in_order(scalars, inputs, cotangent, place, H, [pack])
    x_own = x_copies[0]
    x = head_exchange(x_copies)
    qkv_even, qkv_odd = xor_gather(pack, B)

    w_out_rows = lax.all_gather(w_out, "head", axis=0, tiled=True)
    w_gate_up = lax.all_gather(jnp.concatenate([w_gate, w_up], 1), "blk", axis=0, tiled=True)
    w_d = lax.all_gather(w_down, "blk", axis=1, tiled=True)
    dmo_copies = copies(scalars, upstream, H, RESIDUAL_SCALE, [x])
    dmo = head_exchange(dmo_copies).reshape(group, D)

    run_start = jnp.arange(H)[:, None, None] + me * H
    i = jnp.arange(half)[None, None, :]
    row_pos = jnp.concatenate([half * run_start + i, slots - half * (run_start + 1) + i], 1)
    half_dim = HEAD_SIZE // 2
    frequency = ROPE_BASE ** (-(jnp.arange(half_dim).astype(F32) * 2.0) / HEAD_SIZE)
    angles = row_pos.reshape(H * T, 1).astype(F32) * frequency[None, :]
    cosine = jnp.cos(angles)
    sine = jnp.sin(angles)
    cosine = jnp.concatenate([cosine] * 4, 1)
    sine = jnp.concatenate([-sine, sine] * 2, 1)

    def per_group(table):
        return jnp.broadcast_to(
            table.reshape(H, 1, T, LANES), (H, MICRO, T, LANES)
        ).reshape(group, LANES)

    xn1, q, kv, gain_rows = project(
        scalars,
        x.reshape(H, MICRO, T, D),
        qkv_even,
        qkv_odd,
        cosine,
        sine,
        QD,
        KD,
        [dmo_copies],
    )
    x = x.reshape(group, D)
    runs = (H, MICRO, 2, half)
    q = q.reshape(runs + (QD,))
    kv_even, kv_odd = xor_gather(kv.reshape(group, 2 * KD), B)
    kv_even = kv_even.reshape((B // 2,) + runs + (2 * KD,))
    kv_odd = kv_odd.reshape((B // 2,) + runs + (2 * KD,))
    w_out_rows = hold(scalars, [w_out_rows], [kv_odd])[0]
    o, lse = attention_forward(scalars, q, kv_even, kv_odd, heads, [w_out_rows])
    o_parts = head_gather(o.reshape(group, QD), H)
    out_even, out_odd = xor_gather(
        w_out_rows, B, lambda parts: join(scalars, parts, [o_parts[1], dmo])
    )
    xn2, resid, o_own = out_project(
        scalars, o_parts, x, gain_rows, out_even, out_odd, [dmo]
    )
    gate, up, hidden = mlp_forward(scalars, xn2, w_gate_up, tile, ())
    d_gate, d_up, d_xn2 = mlp_backward(scalars, gate, up, dmo, w_gate_up, w_d, tile, ())
    d_xn2 = lax.psum_scatter(d_xn2, "head", scatter_dimension=0, tiled=True)[None]

    came = swap(grad_rows(scalars, xn2, (d_gate, d_up), B), 1, B)
    came_down = swap(grad_columns(scalars, hidden, dmo, B), 1, B)
    sum_gate_up = grad_rows(scalars, xn2, (d_gate, d_up), B, came)
    grad_gate_up = plane_scatter(sum_gate_up, B, 0)
    sum_down = grad_columns(scalars, hidden, dmo, B, came_down, [sum_gate_up])
    grad_down = core_scatter_steps(sum_down, B)

    d_resid, d_branch, gain_two, *d_attn = branch_back(
        scalars,
        d_xn2,
        resid,
        upstream,
        gain_rows,
        out_even,
        out_odd,
        QD,
        H,
        [sum_gate_up],
    )
    mlp_out = down_project(scalars, hidden, w_d, [d_branch])
    d_attn = head_deal(d_attn, H)
    mlp_held = hold(scalars, [mlp_out], d_attn[1:])[0]
    mlp_out = head_exchange(mlp_held.reshape(H, tokens, D))
    d_attn = [part.reshape(MICRO, 2, half, QD) for part in d_attn]
    tables = (H, 2, half, LANES)
    dq, dkv_even, dkv_odd = attention_backward(
        scalars, q, kv_even, kv_odd, d_attn, o, lse, cosine.reshape(tables), sine.reshape(tables), heads,
        [sum_down, mlp_held],
    )
    out_away = grad_rows(scalars, o_own, (d_branch,), B, near=True, wait=[dq])
    sum_out = grad_rows(
        scalars, o_own, (d_branch,), B, came=swap(out_away, 1, B), near=True
    ).reshape(B // 2, block, D)

    def by_distance(values):
        values = values.astype(BF).reshape(H, wrows, -1)
        return head_deal(
            [lax.dynamic_index_in_dim(values, (mine + k) % H, 0, False) for k in range(H)], H
        )

    grad_out = by_distance(core_scatter_steps(sum_out, B))
    grad_out = sum(part.astype(F32) for part in grad_out)
    pieces = (B // 2, group, 2 * KD)
    dkv = xor_scatter(dkv_even.reshape(pieces), dkv_odd.reshape(pieces), B)
    d_xn1, grad_even, grad_odd = input_back(
        scalars,
        dq.reshape(group, QD),
        dkv,
        per_group(cosine),
        per_group(sine),
        x,
        xn1.reshape(group, D),
        gain_two,
        qkv_even,
        qkv_odd,
        [sum_out, mlp_out, grad_gate_up],
    )
    d_xn1 = lax.psum_scatter(d_xn1, "head", scatter_dimension=0, tiled=True)
    grad_gate_up = wide(scalars, grad_gate_up, [d_xn1])
    grad_qkv = arrange(scalars, by_distance(xor_scatter(grad_even, grad_odd, B))).astype(F32)
    grad_gains = jnp.sum(grad_qkv[:, :, used : used + 2], 0)

    def side_by_side(values):
        return values.transpose(1, 0, 2).reshape(wrows, -1)

    output = (resid + RESIDUAL_SCALE * jnp.sum(mlp_out.astype(F32), 0)).astype(BF)
    output = jnp.einsum(
        "mrs,mrd->msd", order, output.reshape(MICRO, T, D), preferred_element_type=F32
    ).astype(BF)
    back, _ = through_norm(d_xn1.astype(F32), gain_rows[0:1], x_own.astype(F32))
    d_input = jnp.einsum(
        "mrs,mrd->msd",
        order.astype(F32),
        (d_resid + back).reshape(MICRO, T, D),
        precision=lax.Precision.HIGHEST,
        preferred_element_type=F32,
    )
    return (
        output,
        d_input,
        grad_gains[:, 0],
        grad_gains[:, 1],
        side_by_side(grad_qkv[:, :, :QD]),
        side_by_side(grad_qkv[:, :, QD : QD + KD]),
        side_by_side(grad_qkv[:, :, QD + KD : used]),
        grad_out,
        grad_gate_up[:, :F],
        grad_gate_up[:, F:],
        grad_down,
    )


def solution(mesh):
    both = ("blk", "head")
    return jax.shard_map(
        body,
        mesh=mesh,
        in_specs=(
            P(None, both, None),
            P(None, both, None),
            P(),
            P(),
            P(both),
            P(both),
            P(both, None),
            P(both, None),
            P(both, None),
            P(both, None),
            P("blk", "head"),
            P("blk", "head"),
            P("head", "blk"),
        ),
        out_specs=(
            P(None, both, None),
            P(None, both, None),
            P(both),
            P(both),
            P(both, None),
            P(both, None),
            P(both, None),
            P(both, None),
            P("blk", "head"),
            P("blk", "head"),
            P("head", "blk"),
        ),
        check_vma=False,
    )
```

```python
import functools

import jax
import jax.numpy as jnp
from jax import lax
from jax.experimental import pallas as pl
from jax.experimental.pallas import tpu as pltpu
from jax.sharding import PartitionSpec as P

MODEL_WIDTH = 2048
QUERY_HEADS = 32
KEY_VALUE_HEADS = 8
HEAD_SIZE = 64
SHARED = QUERY_HEADS // KEY_VALUE_HEADS
MICRO = 2
LANES = 128

SCORE_SCALE = 0.015625
RESIDUAL_SCALE = 0.22
EPSILON = 1e-06
ROPE_BASE = 10000000.0
NEG_FILL = -1e30

BF = jnp.bfloat16
F32 = jnp.float32
VMEM_LIMIT = 56 * 1024 * 1024
COST = 0.1


def dot(left, right, contract):
    return lax.dot_general(left, right, (contract, ((), ())), preferred_element_type=F32)


def nn(left, right):
    return dot(left, right, ((1,), (0,)))


def tn(left, right):
    return dot(left, right, ((0,), (0,)))


def nt(left, right):
    return dot(left, right, ((1,), (1,)))


def swap(x, bit, devices):
    return lax.ppermute(x, "blk", [(i, i ^ bit) for i in range(devices)])


def xor_gather(x, devices, join=None):
    even = [x] + [swap(x, bit, devices) for bit in range(2, devices, 2)]
    even = (join or jnp.stack)(even)
    return even, swap(even, 1, devices)


def add(left, right):
    return (left.astype(F32) + right.astype(F32)).astype(BF)


def core_scatter(held, devices):
    came = [swap(held[bit // 2], bit, devices) for bit in range(2, devices, 2)]
    return sum((part.astype(F32) for part in came), held[0].astype(F32))


def first_step(held, devices):
    if devices != 8:
        return [swap(held[bit // 2], bit, devices) for bit in range(2, devices, 2)]
    half = held.shape[1] // 2
    return [swap(held[3, :half], 2, devices), swap(held[3, half:], 4, devices)]


def second_step(held, came, devices):
    if devices != 8:
        return came
    from_x, from_y = came
    half = held.shape[1] // 2
    h4 = jnp.concatenate([add(held[2, :half], from_x), held[2, half:]], 0)
    h2 = jnp.concatenate([held[1, :half], add(held[1, half:], from_y)], 0)
    return [swap(h2, 2, devices), swap(h4, 4, devices)]


def all_steps(held, came):
    return sum((part.astype(F32) for part in came), held[0].astype(F32))


def core_scatter_steps(held, devices):
    return all_steps(held, second_step(held, first_step(held, devices), devices))


def xor_scatter(even, odd, devices):
    return core_scatter(add(even, swap(odd, 1, devices)), devices)


def head_exchange(parts):
    return lax.all_to_all(parts, "head", split_axis=0, concat_axis=0, tiled=True)


def head_shift(x, by, devices):
    return lax.ppermute(x, "head", [(i, (i + by) % devices) for i in range(devices)])


def head_gather(x, devices):
    return [x] + [head_shift(x, k, devices) for k in range(1, devices)]


def head_deal(parts, devices):
    return [parts[0]] + [head_shift(parts[k], k, devices) for k in range(1, devices)]


def same_core_groups(devices):
    return [list(range(core, devices, 2)) for core in range(2)]


def plane_scatter(kept, devices, axis):
    return lax.psum_scatter(
        kept,
        "blk",
        scatter_dimension=axis,
        tiled=True,
        axis_index_groups=same_core_groups(devices),
    )


def call(kernel, grid, in_specs, out_specs, out_shape, scratch, flops, moved, args, wait=()):
    wait = tuple(wait)
    given = 1 + len(in_specs)
    in_specs = list(in_specs) + [pl.BlockSpec(memory_space=pl.ANY)] * len(wait)
    args = tuple(args) + wait

    def run(*refs):
        kernel(*refs[:given], *refs[given + len(wait) :])

    return pl.pallas_call(
        run,
        grid_spec=pltpu.PrefetchScalarGridSpec(
            num_scalar_prefetch=1,
            grid=grid,
            in_specs=in_specs,
            out_specs=out_specs,
            scratch_shapes=scratch,
        ),
        out_shape=out_shape,
        compiler_params=pltpu.CompilerParams(vmem_limit_bytes=VMEM_LIMIT),
        cost_estimate=pl.CostEstimate(
            flops=int(flops * COST), bytes_accessed=int(moved * COST), transcendentals=0
        ),
    )(*args)


def whole(shape):
    return pl.BlockSpec(shape, lambda *_: (0,) * len(shape))


def shape_of(shape, dtype):
    return jax.ShapeDtypeStruct(shape, dtype)


def chunk(scalars, j, width):
    return pl.ds(pl.multiple_of((scalars[0] ^ j) * width, LANES), width)


def turned(values):
    lane = lax.broadcasted_iota(jnp.int32, values.shape, 1) % HEAD_SIZE
    quarter = HEAD_SIZE // 2
    return jnp.where(
        lane < quarter,
        pltpu.roll(values, LANES - quarter, 1),
        pltpu.roll(values, quarter, 1),
    )


def rope_lanes(values, cosine, sine, first, limit):
    out = values * cosine + turned(values) * sine
    if first + LANES <= limit:
        return out
    lane = lax.broadcasted_iota(jnp.int32, values.shape, 1)
    return jnp.where(lane < limit - first, out, values)


def before(s, k, devices):
    return (s[1] + devices - k) % devices


def after(s, k, devices):
    return (s[1] + k) % devices


def order_kernel(s, x_ref, up_ref, place_ref, xs_ref, us_ref):
    M, T, D = x_ref.shape
    for m in range(M):
        rank = lax.broadcasted_iota(jnp.int32, (T, T), 0)
        order = (place_ref[m] == rank).astype(BF)
        at = pl.ds(m * T, T)
        x = nn(order, x_ref[m]).astype(BF)
        for h in range(xs_ref.shape[0]):
            xs_ref[h, at, :] = x
        us_ref[at, :] = nn(order, up_ref[m]).astype(BF)


def in_order(scalars, x, upstream, place, H, wait):
    M, T, D = x.shape
    out = shape_of((M * T, D), BF)
    return call(
        order_kernel,
        (1,),
        [whole(x.shape), whole(x.shape), whole((M, 1, T))],
        [whole((H,) + out.shape), whole(out.shape)],
        [shape_of((H,) + out.shape, BF), out],
        [],
        4 * M * T * T * D,
        10 * M * T * D,
        (scalars, x, upstream, place.reshape(M, 1, T)),
        wait,
    )


def pack_kernel(s, q_ref, k_ref, v_ref, g_ref, *outs):
    devices = len(outs)
    QD = q_ref.shape[1] // devices
    KD = k_ref.shape[1] // devices
    for k, out_ref in enumerate(outs):
        for h in range(devices):

            @pl.when(after(s, k, devices) == h)
            def _(out_ref=out_ref, h=h):
                out_ref[:, :QD] = q_ref[:, h * QD : (h + 1) * QD]
                out_ref[:, QD : QD + 2 * KD] = jnp.concatenate(
                    [k_ref[:, h * KD : (h + 1) * KD], v_ref[:, h * KD : (h + 1) * KD]], 1
                )
                out_ref[:, QD + 2 * KD :] = g_ref[...]


def pack_weights(scalars, w_query, w_key, w_value, gains, devices):
    rows = w_query.shape[0]
    columns = (w_query.shape[1] + w_key.shape[1] + w_value.shape[1]) // devices + LANES
    out = shape_of((rows, columns), BF)
    args = (scalars, w_query, w_key, w_value, gains)
    return call(
        pack_kernel,
        (1,),
        [whole(a.shape) for a in args[1:]],
        [whole(out.shape)] * devices,
        [out] * devices,
        [],
        0,
        8 * rows * columns * devices,
        args,
    )


def copies_kernel(s, from_ref, out_ref, *, scale):
    values = from_ref[...]
    if scale is not None:
        values = (scale * values.astype(F32)).astype(BF)
    for h in range(out_ref.shape[0]):
        out_ref[h] = values


def copies(scalars, values, m, H, scale, wait):
    rows = (values.shape[0] // MICRO, values.shape[1])
    shape = (H,) + rows
    return call(
        functools.partial(copies_kernel, scale=scale),
        (1,),
        [pl.BlockSpec(rows, lambda i, s: (m, 0))],
        [whole(shape)],
        [shape_of(shape, BF)],
        [],
        0,
        2 * H * values.size,
        (scalars, values),
        wait,
    )[0]


def hold_kernel(s, *refs):
    count = len(refs) // 2
    for from_ref, to_ref in zip(refs[:count], refs[count:]):
        to_ref[...] = from_ref[...]


def hold(scalars, arrays, wait):
    return call(
        hold_kernel,
        (1,),
        [whole(a.shape) for a in arrays],
        [whole(a.shape) for a in arrays],
        [shape_of(a.shape, a.dtype) for a in arrays],
        [],
        0,
        sum(4 * a.size for a in arrays),
        (scalars, *arrays),
        wait,
    )


def join_kernel(s, *refs):
    *parts, out_ref = refs
    for p, part_ref in enumerate(parts):
        out_ref[p] = part_ref[...]


def join(scalars, parts, wait=()):
    shape = (len(parts),) + parts[0].shape
    return call(
        join_kernel,
        (1,),
        [whole(p.shape) for p in parts],
        [whole(shape)],
        [shape_of(shape, parts[0].dtype)],
        [],
        0,
        4 * len(parts) * parts[0].size,
        (scalars, *parts),
        wait,
    )[0]


def add_kernel(s, left_ref, right_ref, out_ref):
    out_ref[...] = add(left_ref[...], right_ref[...])


def add_up(scalars, left, right, wait):
    return call(
        add_kernel,
        (1,),
        [whole(left.shape), whole(left.shape)],
        [whole(left.shape)],
        [shape_of(left.shape, BF)],
        [],
        0,
        6 * left.size,
        (scalars, left, right),
        wait,
    )[0]


def wide_kernel(s, from_ref, out_ref):
    out_ref[...] = from_ref[...].astype(F32)


def wide(scalars, values, wait):
    rows, columns = values.shape
    piece = pl.BlockSpec((rows // 4, columns), lambda i, s: (i, 0))
    return call(
        wide_kernel,
        (4,),
        [piece],
        [piece],
        [shape_of(values.shape, F32)],
        [],
        0,
        6 * values.size,
        (scalars, values),
        wait,
    )[0]


def merge_kernel(s, *refs):
    *parts, out_ref = refs
    for m, part_ref in enumerate(parts):
        out_ref[:, m] = part_ref[...]


def merge(scalars, parts, wait):
    H, T, D = parts[0].shape
    shape = (H, len(parts), T, D)
    return call(
        merge_kernel,
        (1,),
        [whole((H, T, D))] * len(parts),
        [whole(shape)],
        [shape_of(shape, BF)],
        [],
        0,
        4 * len(parts) * H * T * D,
        (scalars, *parts),
        wait,
    )[0].reshape(H * len(parts) * T, D)


def arrange_kernel(s, *refs):
    *parts, out_ref = refs
    for k, part_ref in enumerate(parts):
        out_ref[before(s, k, len(parts))] = part_ref[...]


def arrange(scalars, parts, wait=()):
    shape = (len(parts),) + parts[0].shape
    return call(
        arrange_kernel,
        (1,),
        [whole(p.shape) for p in parts],
        [whole(shape)],
        [shape_of(shape, parts[0].dtype)],
        [],
        0,
        4 * len(parts) * parts[0].size,
        (scalars, *parts),
        wait,
    )[0]


def project_kernel(s, x_ref, we_ref, wo_ref, cos_ref, sin_ref, xn_ref, q_ref, kv_ref, gain_ref):
    H, _, T, D = x_ref.shape
    places, block, columns = we_ref.shape
    QD = q_ref.shape[-1]
    KD = kv_ref.shape[-1] // 2
    used = QD + 2 * KD

    @pl.when(pl.program_id(0) == 0)
    def _():
        for place in range(places):
            for parity, w_ref in enumerate((we_ref, wo_ref)):
                held = w_ref[place, :, used : used + LANES].astype(F32).T
                gain_ref[:, chunk(s, 2 * place + parity, block)] = held[:8]

    x = x_ref[:, 0].reshape(H * T, D).astype(F32)
    inverse = lax.rsqrt(jnp.mean(x * x, -1, keepdims=True) + EPSILON)
    xn = ((x * inverse) * gain_ref[0:1, :]).astype(BF)
    xn_ref[:, 0] = xn.reshape(H, T, D)
    acc = jnp.zeros((H * T, used), F32)
    for place in range(places):
        for parity, w_ref in enumerate((we_ref, wo_ref)):
            left = xn_ref[:, 0, :, chunk(s, 2 * place + parity, block)].reshape(H * T, block)
            acc = acc + nn(left, w_ref[place, :, :used])
    cosine = cos_ref[...]
    sine = sin_ref[...]
    for first in range(0, used, LANES):
        part = acc[:, first : first + LANES]
        if first < QD + KD:
            part = rope_lanes(part, cosine, sine, first, QD + KD)
        if first < QD:
            q_ref[:, 0, :, first : first + LANES] = (
                (part * SCORE_SCALE).astype(BF).reshape(H, T, LANES)
            )
        else:
            kv_ref[:, 0, :, first - QD : first - QD + LANES] = part.astype(BF).reshape(H, T, LANES)


def project(scalars, x, w_even, w_odd, cosine, sine, QD, KD, wait):
    H, M, T, D = x.shape
    used = QD + 2 * KD

    def rows(width):
        return pl.BlockSpec((H, 1, T, width), lambda m, s: (0, m, 0, 0))

    return call(
        project_kernel,
        (M,),
        [rows(D), whole(w_even.shape), whole(w_odd.shape), whole(cosine.shape), whole(sine.shape)],
        [rows(D), rows(QD), rows(2 * KD), whole((8, D))],
        [
            shape_of((H, M, T, D), BF),
            shape_of((H, M, T, QD), BF),
            shape_of((H, M, T, 2 * KD), BF),
            shape_of((8, D), F32),
        ],
        [],
        2 * H * M * T * D * used,
        4 * H * M * T * D + 4 * w_even.size,
        (scalars, x, w_even, w_odd, cosine, sine),
        wait,
    )


def run_offset(index, run, tile, half):
    if run == 0:
        return index
    return (tile - half) - (index // half) * half + index % half


def key_positions(s, natural, run, length, tile, half, blocks):
    row = lax.broadcasted_iota(jnp.int32, (4 * tile, 1), 0)
    part = row // tile
    owner = 4 * natural + ((s[0] & 3) ^ (((part & 1) << 1) | (part >> 1)))
    row_tile = owner if run == 0 else 2 * blocks - 1 - owner
    position = row_tile * tile + run_offset(row % tile, run, tile, half)
    return jnp.where(position < length, position, jnp.int32(1 << 30))


def query_positions(s, run, rows, tile, half, blocks):
    own = s[0] if run == 0 else 2 * blocks - 1 - s[0]
    lane = lax.broadcasted_iota(jnp.int32, (1, rows), 1) % tile
    return own * tile + run_offset(lane, run, tile, half)


def slab(even_ref, odd_ref, y, run, first, last):
    parts = [
        ref[2 * y + i, :, 0, run, :, first:last] for ref in (even_ref, odd_ref) for i in range(2)
    ]
    H, half, width = parts[0].shape
    return jnp.concatenate([part.reshape(H * half, width) for part in parts], 0)


def heads_across(ref, run, head, heads):
    H, _, _, half, _ = ref.shape
    first = head * SHARED * HEAD_SIZE
    values = ref[:, 0, run, :, first : first + SHARED * HEAD_SIZE]
    values = values.reshape(H * half, SHARED * HEAD_SIZE).astype(F32).T
    values = jnp.concatenate(
        [values[g * HEAD_SIZE : (g + 1) * HEAD_SIZE] for g in range(SHARED)], 1
    )
    return values


def padded(values, head, heads):
    values = values.astype(BF)
    if heads == 1:
        return values
    zeros = jnp.zeros_like(values)
    return jnp.concatenate([values, zeros] if head == 0 else [zeros, values], 0)


def heads_back(values, tile):
    return jnp.concatenate(
        [values[:, g * tile : (g + 1) * tile] for g in range(SHARED)], 0
    ).T


def slab_loops(s, length, run, tile, blocks, state, step):
    slabs = blocks // 4
    own = s[0] // 4
    if run == 0:
        return lax.fori_loop(0, own + 1, lambda n, st: step(st, n, 0, True), state)
    state = lax.fori_loop(0, slabs, lambda n, st: step(st, n, 0, False), state)
    within = (2 * blocks * tile - length) // (4 * tile)
    return lax.fori_loop(
        jnp.maximum(own, within), slabs, lambda n, st: step(st, n, 1, True), state
    )


def fold_rows(values, combine):
    rows, lanes = values.shape
    return combine(values.reshape(rows // 8, 8, lanes), axis=0)


def forward_kernel(s, q_ref, ke_ref, ko_ref, o_ref, lse_ref, *, heads):
    H, _, _, half, QD = q_ref.shape
    blocks = 2 * ke_ref.shape[0]
    tile = H * half
    width = heads * HEAD_SIZE
    rows = SHARED * tile
    length = s[2 + pl.program_id(0)]
    for run in range(2):
        q = [padded(heads_across(q_ref, run, head, heads), head, heads) for head in range(heads)]
        at = query_positions(s, run, rows, tile, half, blocks)

        def step(state, natural, key_run, masked, q=q, at=at):
            y = natural ^ (s[0] >> 2)
            k = slab(ke_ref, ko_ref, y, key_run, 0, width)
            v = slab(ke_ref, ko_ref, y, key_run, width, 2 * width)
            if masked:
                seen = key_positions(s, natural, key_run, length, tile, half, blocks) <= at
            new = []
            for head in range(heads):
                top, total, acc = state[head]
                scores = nn(k, q[head])
                if masked:
                    scores = jnp.where(seen, scores, NEG_FILL)
                best = jnp.maximum(top, jnp.max(fold_rows(scores, jnp.max), 0, keepdims=True))
                p = jnp.exp(scores - best)
                scale = jnp.exp(top - best)
                total = total * scale + jnp.sum(fold_rows(p, jnp.sum), 0, keepdims=True)
                new.append((best, total, acc * scale + tn(v, p.astype(BF))))
            return tuple(new)

        start = tuple(
            (
                jnp.full((1, rows), NEG_FILL, F32),
                jnp.zeros((1, rows), F32),
                jnp.zeros((width, rows), F32),
            )
            for _ in range(heads)
        )
        done = slab_loops(s, length, run, tile, blocks, start, step)
        for head in range(heads):
            top, total, acc = done[head]
            lse_ref[0, run, head] = top + jnp.log(total)
            out = acc[head * HEAD_SIZE : (head + 1) * HEAD_SIZE] / total
            first = head * SHARED * HEAD_SIZE
            o_ref[:, 0, run, :, first : first + SHARED * HEAD_SIZE] = (
                heads_back(out, tile).astype(BF).reshape(H, half, SHARED * HEAD_SIZE)
            )


def backward_kernel(
    s, q_ref, ke_ref, ko_ref, o_ref, lse_ref, cos_ref, sin_ref, *refs, heads
):
    H, _, _, half, QD = q_ref.shape
    dq_ref, de_ref, dod_ref, acc_ref, do_ref = refs[H:]
    for k in range(H):
        do_ref[before(s, k, H), 0] = refs[k][0]
    blocks = 2 * ke_ref.shape[0]
    tile = H * half
    width = heads * HEAD_SIZE
    rows = SHARED * tile
    length = s[2 + pl.program_id(0)]
    acc_ref[...] = jnp.zeros(acc_ref.shape, F32)
    for run in range(2):
        q, do, lse, delta = [], [], [], []
        for head in range(heads):
            q.append(padded(heads_across(q_ref, run, head, heads), head, heads))
            up = heads_across(do_ref, run, head, heads)
            do.append(padded(up, head, heads))
            delta.append(
                jnp.sum(up * heads_across(o_ref, run, head, heads), 0, keepdims=True)
            )
            lse.append(lse_ref[0, run, head])
        at = query_positions(s, run, rows, tile, half, blocks)

        def step(state, natural, key_run, masked, q=q, do=do, lse=lse, delta=delta, at=at):
            y = natural ^ (s[0] >> 2)
            k = slab(ke_ref, ko_ref, y, key_run, 0, width)
            v = slab(ke_ref, ko_ref, y, key_run, width, 2 * width)
            if masked:
                seen = key_positions(s, natural, key_run, length, tile, half, blocks) <= at
            new = []
            dk = jnp.zeros((4 * tile, width), F32)
            dv = jnp.zeros((4 * tile, width), F32)
            for head in range(heads):
                p = jnp.exp(nn(k, q[head]) - lse[head])
                if masked:
                    p = jnp.where(seen, p, 0.0)
                ds = (p * (nn(v, do[head]) - delta[head])).astype(BF)
                dk = dk + nt(ds, q[head])
                dv = dv + nt(p.astype(BF), do[head])
                new.append(state[head] + tn(k, ds))
            acc_ref[key_run, y, :, :width] += dk
            acc_ref[key_run, y, :, width:] += dv
            return tuple(new)

        start = tuple(jnp.zeros((width, rows), F32) for _ in range(heads))
        done = slab_loops(s, length, run, tile, blocks, start, step)
        cosine = cos_ref[:, run].reshape(tile, LANES)
        sine = sin_ref[:, run].reshape(tile, LANES)
        for head in range(heads):
            out = done[head][head * HEAD_SIZE : (head + 1) * HEAD_SIZE]
            out = (heads_back(out, tile) * SCORE_SCALE).astype(BF).astype(F32)
            for lanes in range(0, SHARED * HEAD_SIZE, LANES):
                part = out[:, lanes : lanes + LANES]
                part = part * cosine - turned(part) * sine
                first = head * SHARED * HEAD_SIZE + lanes
                dq_ref[:, 0, run, :, first : first + LANES] = part.astype(BF).reshape(
                    H, half, LANES
                )
    for run in range(2):
        for y in range(blocks // 4):
            for index, (ref, i) in enumerate(((de_ref, 0), (de_ref, 1), (dod_ref, 0), (dod_ref, 1))):
                ref[2 * y + i, :, 0, run] = (
                    acc_ref[run, y, index * tile : (index + 1) * tile]
                    .astype(BF)
                    .reshape(H, half, 2 * width)
                )


def attention_specs(q, kv, heads):
    H, M, _, half, QD = q.shape
    places, _, _, _, _, width = kv.shape
    per_q = pl.BlockSpec((H, 1, 2, half, QD), lambda m, s: (0, m, 0, 0, 0))
    per_kv = pl.BlockSpec((places, H, 1, 2, half, width), lambda m, s: (0, 0, m, 0, 0, 0))
    per_row = pl.BlockSpec((1, 2, heads, 1, SHARED * H * half), lambda m, s: (m, 0, 0, 0, 0))
    work = M * places * H * half * SHARED * H * half * QD
    return per_q, per_kv, per_row, work


def attention_forward(scalars, q, k_even, k_odd, heads, wait):
    H, M, _, half, QD = q.shape
    per_q, per_kv, per_row, work = attention_specs(q, k_even, heads)
    return call(
        functools.partial(forward_kernel, heads=heads),
        (M,),
        [per_q, per_kv, per_kv],
        [per_q, per_row],
        [shape_of(q.shape, BF), shape_of((M, 2, heads, 1, SHARED * H * half), F32)],
        [],
        8 * work,
        2 * (2 * q.size + 2 * k_even.size),
        (scalars, q, k_even, k_odd),
        wait,
    )


def attention_backward(scalars, q, k_even, k_odd, do_parts, o, lse, cosine, sine, heads, wait):
    H, M, _, half, QD = q.shape
    per_q, per_kv, per_row, work = attention_specs(q, k_even, heads)
    blocks = 2 * k_even.shape[0]
    return call(
        functools.partial(backward_kernel, heads=heads),
        (M,),
        [per_q, per_kv, per_kv, per_q, per_row, whole(cosine.shape), whole(sine.shape)]
        + [pl.BlockSpec((1, 2, half, QD), lambda m, s: (m, 0, 0, 0))] * H,
        [per_q, per_kv, per_kv],
        [shape_of(q.shape, BF), shape_of(k_even.shape, BF), shape_of(k_odd.shape, BF)],
        [
            pltpu.VMEM((2, blocks // 4, 4 * H * half, 2 * heads * HEAD_SIZE), F32),
            pltpu.VMEM((H, 1, 2, half, QD), BF),
        ],
        20 * work,
        2 * (4 * q.size + 4 * k_even.size),
        (scalars, q, k_even, k_odd, o, lse, cosine, sine, *do_parts),
        wait,
    )


def out_kernel(s, x_ref, gain_ref, w_ref, *refs):
    devices = len(refs) - 4
    xn_ref, own_ref, o_own_ref, acc_ref = refs[devices:]
    n = pl.program_id(0)
    group, QD = refs[0].shape
    columns = w_ref.shape[1]
    rows = group // devices

    @pl.when(n == 0)
    def _():
        at = pl.ds(pl.multiple_of(s[1] * rows, rows), rows)
        for k in range(devices):
            lanes = pl.ds(pl.multiple_of(before(s, k, devices) * QD, LANES), QD)
            o_own_ref[:, lanes] = refs[k][at, :]

    got = jnp.zeros((group, columns), F32)
    for k in range(devices):
        first = pl.multiple_of(before(s, k, devices) * QD, QD)
        got = got + nn(refs[k][...], w_ref[pl.ds(first, QD), :])
    acc_ref[:, pl.ds(pl.multiple_of(n * columns, LANES), columns)] = got

    @pl.when(n == pl.num_programs(0) - 1)
    def _():
        def finish(h, carry):
            at = pl.ds(pl.multiple_of(h * rows, rows), rows)
            resid = x_ref[at, :].astype(F32) + RESIDUAL_SCALE * acc_ref[at, :]
            inverse = lax.rsqrt(jnp.mean(resid * resid, -1, keepdims=True) + EPSILON)
            xn_ref[at, :] = ((resid * inverse) * gain_ref[1:2, :]).astype(BF)

            @pl.when(h == s[1])
            def _():
                own_ref[...] = resid

            return carry

        lax.fori_loop(0, devices, finish, 0)


def out_project(scalars, o_parts, x, gains, w_out, wait):
    H = len(o_parts)
    group, QD = o_parts[0].shape
    D = w_out.shape[1]
    rows = group // H
    columns = 512
    piece = pl.BlockSpec((H * QD, columns), lambda n, s: (0, n))
    return call(
        out_kernel,
        (D // columns,),
        [whole(x.shape), whole(gains.shape), piece] + [whole((group, QD))] * H,
        [whole((group, D)), whole((rows, D)), whole((rows, H * QD))],
        [shape_of((group, D), BF), shape_of((rows, D), F32), shape_of((rows, H * QD), BF)],
        [pltpu.VMEM((group, D), F32)],
        2 * group * H * QD * D,
        2 * (H * group * QD + 2 * x.size + w_out.size),
        (scalars, x, gains, w_out, *o_parts),
        wait,
    )


def mlp_forward_kernel(s, xn_ref, wg_ref, wu_ref, gate_ref, up_ref, hidden_ref):
    gate = nn(xn_ref[...], wg_ref[...])
    up = nn(xn_ref[...], wu_ref[...])
    gate_ref[...] = gate
    up_ref[...] = up
    hidden_ref[...] = (gate * (1.0 / (1.0 + jnp.exp(-gate))) * up).astype(BF)


def mlp_forward(scalars, xn, w_gate_up, tile, wait):
    group, D = xn.shape
    F = w_gate_up.shape[1] // 2
    count = F // tile
    out = pl.BlockSpec((group, tile), lambda f, s: (0, f))
    return call(
        mlp_forward_kernel,
        (count,),
        [
            whole(xn.shape),
            pl.BlockSpec((D, tile), lambda f, s: (0, f)),
            pl.BlockSpec((D, tile), lambda f, s: (0, f + count)),
        ],
        [out, out, out],
        [shape_of((group, F), F32), shape_of((group, F), F32), shape_of((group, F), BF)],
        [],
        4 * group * D * F,
        2 * (group * D + 2 * D * F + 5 * group * F),
        (scalars, xn, w_gate_up, w_gate_up),
        wait,
    )


def down_kernel(s, hidden_ref, w_ref, *outs):
    got_ref = outs[-1]
    rows = outs[0].shape[0]
    devices = got_ref.shape[0] // rows
    got_ref[...] = nn(hidden_ref[...], w_ref[...]).astype(BF)
    for k in range(devices):
        at = pl.ds(pl.multiple_of(after(s, k, devices) * rows, rows), rows)
        outs[k][...] = got_ref[at, :]


def down_project(scalars, hidden, w_down, devices, wait):
    group, F = hidden.shape
    D = w_down.shape[1]
    width = 512
    rows = group // devices
    return call(
        down_kernel,
        (D // width,),
        [whole(hidden.shape), pl.BlockSpec((F, width), lambda n, s: (0, n))],
        [pl.BlockSpec((rows, width), lambda n, s: (0, n))] * devices,
        [shape_of((rows, D), BF)] * devices,
        [pltpu.VMEM((group, width), BF)],
        2 * group * D * F,
        2 * (group * D + D * F + group * F),
        (scalars, hidden, w_down),
        wait,
    )


def mlp_backward_kernel(
    s, gate_ref, up_ref, wg_ref, wu_ref, wd_ref, dmo_ref, dg_ref, du_ref, dxn_ref, acc_ref
):
    f = pl.program_id(0)
    d_hidden = nt(dmo_ref[...], wd_ref[...])
    gate = gate_ref[...]
    sigma = 1.0 / (1.0 + jnp.exp(-gate))
    dg_ref[...] = (d_hidden * up_ref[...] * (sigma * (1.0 + gate * (1.0 - sigma)))).astype(BF)
    du_ref[...] = (d_hidden * (gate * sigma)).astype(BF)
    got = nt(dg_ref[...], wg_ref[...]) + nt(du_ref[...], wu_ref[...])

    @pl.when(f == 0)
    def _():
        acc_ref[...] = got

    @pl.when(f > 0)
    def _():
        acc_ref[...] += got

    @pl.when(f == pl.num_programs(0) - 1)
    def _():
        dxn_ref[...] = acc_ref[...].astype(BF)


def mlp_backward(scalars, gate, up, dmo, w_gate_up, w_down, tile, wait):
    group, D = dmo.shape
    F = gate.shape[1]
    count = F // tile
    per_f = pl.BlockSpec((group, tile), lambda f, s: (0, f))
    return call(
        mlp_backward_kernel,
        (count,),
        [
            per_f,
            per_f,
            pl.BlockSpec((D, tile), lambda f, s: (0, f)),
            pl.BlockSpec((D, tile), lambda f, s: (0, f + count)),
            pl.BlockSpec((tile, D), lambda f, s: (f, 0)),
            whole((group, D)),
        ],
        [per_f, per_f, whole((group, D))],
        [shape_of((group, F), BF), shape_of((group, F), BF), shape_of((group, D), BF)],
        [pltpu.VMEM((group, D), F32)],
        6 * group * D * F,
        2 * (3 * group * D + 3 * D * F + 6 * group * F),
        (scalars, gate, up, w_gate_up, w_gate_up, w_down, dmo),
        wait,
    )


def block_lanes(s, own, near, block):
    i = pl.program_id(0)
    if near:
        index = s[0] ^ (2 * i if own else 2 * i + 1)
    else:
        index = 2 * i + (s[0] % 2 if own else 1 - s[0] % 2)
    return pl.ds(pl.multiple_of(index * block, LANES), block)


def rows_kernel(s, left_ref, *refs, own, count, near):
    right = refs[:count]
    out_ref = refs[-1]
    block = out_ref.shape[0]
    lanes = block_lanes(s, own, near, block)
    left = left_ref[:, lanes]
    at = 0
    for i, right_ref in enumerate(right):
        width = right_ref.shape[1]
        got = tn(left, right_ref[...])
        if own:
            got = got + refs[count][:, at : at + width].astype(F32)
        out_ref[:, at : at + width] = got.astype(BF)
        at += width


def grad_rows(scalars, left, rights, blocks, came=None, near=False, wait=()):
    n, D = left.shape
    block = D // blocks
    width = sum(r.shape[1] for r in rights)
    piece = pl.BlockSpec((block, width), lambda i, s: (i, 0))
    extra = [] if came is None else [came]
    return call(
        functools.partial(
            rows_kernel, own=came is not None, count=len(rights), near=near
        ),
        (blocks // 2,),
        [whole(left.shape)] + [whole(r.shape) for r in rights] + [piece] * len(extra),
        [piece],
        [shape_of((D // 2, width), BF)],
        [],
        n * D * width,
        2 * (left.size + n * width + D * width),
        (scalars, left, *rights, *extra),
        wait,
    )[0]


def columns_kernel(s, left_ref, right_ref, *refs, own):
    out_ref = refs[-1]
    got = tn(left_ref[...], right_ref[:, block_lanes(s, own, True, out_ref.shape[2])])
    if own:
        got = got + refs[0][0].astype(F32)
    out_ref[0] = got.astype(BF)


def grad_columns(scalars, left, right, blocks, came=None, wait=()):
    n, F = left.shape
    D = right.shape[1]
    block = D // blocks
    piece = pl.BlockSpec((1, F, block), lambda i, s: (i, 0, 0))
    extra = [] if came is None else [came]
    return call(
        functools.partial(columns_kernel, own=came is not None),
        (blocks // 2,),
        [whole(left.shape), whole(right.shape)] + [piece] * len(extra),
        [piece],
        [shape_of((blocks // 2, F, block), BF)],
        [],
        n * D * F,
        2 * (left.size + right.size + D * F),
        (scalars, left, right, *extra),
        wait,
    )[0]


def through_norm(upstream, gain, values):
    inverse = lax.rsqrt(jnp.mean(values * values, -1, keepdims=True) + EPSILON)
    scaled = values * inverse
    through = upstream * gain
    inner = jnp.mean(through * scaled, -1, keepdims=True)
    return inverse * (through - scaled * inner), scaled


def branch_kernel(s, parts, resid_ref, up_ref, gain_ref, w_ref, *refs):
    devices = len(refs) - 4
    dresid_ref, da_ref, gg_ref = refs[:3]
    outs = refs[3:-1]
    dattn_ref = refs[-1]
    p = pl.program_id(0)

    @pl.when(p == 0)
    def _():
        upstream = parts[0].astype(F32)
        for h in range(1, parts.shape[0]):
            upstream = upstream + parts[h].astype(F32)
        back, scaled = through_norm(upstream, gain_ref[1:2, :], resid_ref[...])
        gg_ref[...] = jnp.broadcast_to(
            jnp.sum(upstream * scaled, 0, keepdims=True), gg_ref.shape
        )
        d_resid = up_ref[...].astype(F32) + back
        dresid_ref[...] = d_resid
        da_ref[...] = (RESIDUAL_SCALE * d_resid).astype(BF)

    dattn_ref[p] = nt(da_ref[...], w_ref[...]).astype(BF)

    @pl.when(p == pl.num_programs(0) - 1)
    def _():
        for k in range(devices):
            outs[k][...] = dattn_ref[after(s, k, devices)]


def branch_back(scalars, parts, resid, upstream, gains, w_out, H, wait):
    _, tokens, D = parts.shape
    QD = w_out.shape[0] // H
    return call(
        branch_kernel,
        (H,),
        [whole(a.shape) for a in (parts, resid, upstream, gains)]
        + [pl.BlockSpec((QD, D), lambda p, s: (p, 0))],
        [whole((tokens, D)), whole((tokens, D)), whole((8, D))] + [whole((tokens, QD))] * H,
        [shape_of((tokens, D), F32), shape_of((tokens, D), BF), shape_of((8, D), F32)]
        + [shape_of((tokens, QD), BF)] * H,
        [pltpu.VMEM((H, tokens, QD), BF)],
        2 * tokens * D * H * QD,
        2 * (H * tokens * D + w_out.size + 6 * tokens * D),
        (scalars, parts, resid, upstream, gains, w_out),
        wait,
    )


def input_kernel(
    s, dq_ref, dkv_ref, cos_ref, sin_ref, x_ref, xn_ref, gg_ref, we_ref, wo_ref, *refs
):
    out_ref, ge_ref, go_ref, dqkv_ref, inv_ref = refs
    p = pl.program_id(0)
    group, QD = dq_ref.shape
    KD = dkv_ref.shape[1] // 2
    used = QD + 2 * KD
    block = we_ref.shape[1]

    @pl.when(p == 0)
    def _():
        dqkv_ref[:, :QD] = dq_ref[...]
        for first in range(0, 2 * KD, LANES):
            part = dkv_ref[:, first : first + LANES].astype(F32)
            if first < KD:
                part = rope_lanes(part, cos_ref[...], -sin_ref[...], first, KD)
            dqkv_ref[:, QD + first : QD + first + LANES] = part.astype(BF)
        x = x_ref[...].astype(F32)
        inv_ref[...] = jnp.broadcast_to(
            lax.rsqrt(jnp.mean(x * x, -1, keepdims=True) + EPSILON), inv_ref.shape
        )

    for parity, (w_ref, g_ref) in enumerate(((we_ref, ge_ref), (wo_ref, go_ref))):
        lanes = chunk(s, 2 * p + parity, block)
        dxn = nt(dqkv_ref[...], w_ref[0, :, :used])
        out_ref[:, lanes] = dxn.astype(BF)
        scaled = x_ref[:, lanes].astype(F32) * inv_ref[:, 0:1]
        gain_one = jnp.sum(dxn * scaled, 0, keepdims=True)
        g_ref[0, :, :used] = tn(xn_ref[:, lanes], dqkv_ref[...]).astype(BF)
        row = lax.broadcasted_iota(jnp.int32, (LANES, block), 0)
        both = jnp.where(row == 0, gain_one, jnp.where(row == 1, gg_ref[0:1, lanes], 0.0))
        g_ref[0, :, used:] = both.T.astype(BF)


def input_back(scalars, dq, dkv, cosine, sine, x, xn, gain_two, w_even, w_odd, wait):
    group, D = x.shape
    QD = dq.shape[1]
    places, block, columns = w_even.shape
    piece = pl.BlockSpec((1, block, columns), lambda p, s: (p, 0, 0))
    return call(
        input_kernel,
        (places,),
        [whole(a.shape) for a in (dq, dkv, cosine, sine, x, xn, gain_two)] + [piece, piece],
        [whole(x.shape), piece, piece],
        [shape_of(x.shape, BF), shape_of(w_even.shape, BF), shape_of(w_even.shape, BF)],
        [
            pltpu.VMEM((group, QD + dkv.shape[1]), BF),
            pltpu.VMEM((group, LANES), F32),
        ],
        4 * group * D * (QD + dkv.shape[1]),
        2 * (3 * x.size + 4 * w_even.size),
        (scalars, dq, dkv, cosine, sine, x, xn, gain_two, w_even, w_odd),
        wait,
    )


def last_kernel(s, parts_ref, x_ref, resid_ref, gain_ref, place_ref, out_ref):
    M, T, _ = out_ref.shape
    for m in range(M):
        at = pl.ds(m * T, T)
        upstream = parts_ref[0, at, :].astype(F32)
        for h in range(1, parts_ref.shape[0]):
            upstream = upstream + parts_ref[h, at, :].astype(F32)
        back, _ = through_norm(upstream, gain_ref[0:1, :], x_ref[at, :].astype(F32))
        total = resid_ref[at, :] + back
        rank = lax.broadcasted_iota(jnp.int32, (T, T), 0)
        order = (place_ref[m] == rank).astype(F32)
        out_ref[m] = lax.dot_general(
            order,
            total,
            (((0,), (0,)), ((), ())),
            precision=lax.Precision.HIGHEST,
            preferred_element_type=F32,
        )


def input_gradient(scalars, parts, x, d_resid, gains, place):
    M, T = place.shape
    D = x.shape[1]
    place = place.reshape(M, 1, T)
    args = (scalars, parts, x, d_resid, gains, place)
    return call(
        last_kernel,
        (1,),
        [whole(a.shape) for a in args[1:]],
        [whole((M, T, D))],
        [shape_of((M, T, D), F32)],
        [],
        4 * M * T * T * D,
        12 * M * T * D,
        args,
    )[0]


def body(
    inputs,
    cotangent,
    lengths,
    positions,
    attn_gain,
    mlp_gain,
    w_query,
    key_projection,
    value_projection,
    w_out,
    w_gate,
    w_up,
    w_down,
):
    B = lax.axis_size("blk")
    H = lax.axis_size("head")
    me = lax.axis_index("blk")
    mine = lax.axis_index("head")
    T = inputs.shape[1]
    D = MODEL_WIDTH
    half = T // 2
    slots = T * H * B
    heads = KEY_VALUE_HEADS // H
    KD = heads * HEAD_SIZE
    QD = KD * SHARED
    used = QD + 2 * KD
    tokens = MICRO * T
    group = H * tokens
    wrows = w_query.shape[0]
    F = w_gate.shape[1]
    block = D // B
    tile = min(512, F)

    scalars = jnp.concatenate(
        [jnp.stack([me, mine]).astype(jnp.int32), lengths.astype(jnp.int32)]
    )

    gains = jnp.concatenate(
        [attn_gain[:, None], mlp_gain[:, None], jnp.zeros((wrows, LANES - 2), BF)], 1
    )
    pack = pack_weights(scalars, w_query, key_projection, value_projection, gains, H)
    linear = me * H + mine
    my_pos = lax.dynamic_slice_in_dim(positions, linear * T, T, axis=1)
    place = jnp.where(
        my_pos < slots // 2, my_pos - half * linear, half + my_pos - (slots - half * (linear + 1))
    ).astype(jnp.int32)
    order = (place[:, None, :] == jnp.arange(T)[None, :, None]).astype(BF)
    pack = arrange(scalars, head_deal(pack, H)).reshape(H * wrows, used + LANES)
    x_copies, upstream = in_order(scalars, inputs, cotangent, place, H, [pack])
    x_own = x_copies[0]
    x = head_exchange(x_copies)
    qkv_even, qkv_odd = xor_gather(pack, B)

    w_gate_up = lax.all_gather(jnp.concatenate([w_gate, w_up], 1), "blk", axis=0, tiled=True)
    dmo_copies = copies(scalars, upstream, 0, H, RESIDUAL_SCALE, [x])
    dmo_parts = [head_exchange(dmo_copies)]

    run_start = jnp.arange(H)[:, None, None] + me * H
    i = jnp.arange(half)[None, None, :]
    row_pos = jnp.concatenate([half * run_start + i, slots - half * (run_start + 1) + i], 1)
    half_dim = HEAD_SIZE // 2
    frequency = ROPE_BASE ** (-(jnp.arange(half_dim).astype(F32) * 2.0) / HEAD_SIZE)
    angles = row_pos.reshape(H * T, 1).astype(F32) * frequency[None, :]
    cosine = jnp.cos(angles)
    sine = jnp.sin(angles)
    cosine = jnp.concatenate([cosine] * 4, 1)
    sine = jnp.concatenate([-sine, sine] * 2, 1)

    def per_group(table):
        return jnp.broadcast_to(
            table.reshape(H, 1, T, LANES), (H, MICRO, T, LANES)
        ).reshape(group, LANES)

    xn1, q, kv, gain_rows = project(
        scalars,
        x.reshape(H, MICRO, T, D),
        qkv_even,
        qkv_odd,
        cosine,
        sine,
        QD,
        KD,
        [dmo_copies],
    )
    x = x.reshape(group, D)
    runs = (H, MICRO, 2, half)
    q = q.reshape(runs + (QD,))
    kv_even, kv_odd = xor_gather(kv.reshape(group, 2 * KD), B)
    kv_even = kv_even.reshape((B // 2,) + runs + (2 * KD,))
    kv_odd = kv_odd.reshape((B // 2,) + runs + (2 * KD,))
    w_o = lax.all_gather(
        hold(scalars, [w_out], [w_gate_up, kv])[0], "head", axis=0, tiled=True
    )
    o, lse = attention_forward(scalars, q, kv_even, kv_odd, heads, dmo_parts)
    o_parts = head_gather(o.reshape(group, QD), H)
    w_o = lax.all_gather(hold(scalars, [w_o], [lse])[0], "blk", axis=0, tiled=True)
    w_d = lax.all_gather(hold(scalars, [w_down], [lse])[0], "blk", axis=1, tiled=True)
    later = [copies(scalars, upstream, m, H, RESIDUAL_SCALE, o_parts[1:]) for m in range(1, MICRO)]
    dmo_parts = dmo_parts + [head_exchange(part) for part in later]
    xn2, resid, o_own = out_project(
        scalars, o_parts, x, gain_rows, w_o, later
    )
    gate, up, hidden = mlp_forward(scalars, xn2, w_gate_up, tile, ())
    dmo = merge(scalars, dmo_parts, [hidden])
    came_down = swap(grad_columns(scalars, hidden, dmo, B), 1, B)
    sum_down = grad_columns(scalars, hidden, dmo, B, came_down)
    down_first = first_step(sum_down, B)
    d_gate, d_up, d_xn2 = mlp_backward(
        scalars, gate, up, dmo, w_gate_up, w_d, tile, [sum_down]
    )
    d_xn2 = lax.psum_scatter(d_xn2, "head", scatter_dimension=0, tiled=True)[None]

    came = swap(grad_rows(scalars, xn2, (d_gate, d_up), B, wait=down_first), 1, B)
    down_second = second_step(sum_down, down_first, B)
    grad_down = all_steps(sum_down, down_second)
    sum_gate_up = grad_rows(scalars, xn2, (d_gate, d_up), B, came, wait=down_second)
    grad_gate_up = plane_scatter(sum_gate_up, B, 0)
    mlp_sum = down_project(scalars, hidden, w_d, H, [sum_gate_up])


    d_resid, d_branch, gain_two, *d_attn = branch_back(
        scalars,
        d_xn2,
        resid,
        upstream,
        gain_rows,
        w_o,
        H,
        [sum_gate_up, mlp_sum[0]],
    )
    d_attn = head_deal(d_attn, H)
    mlp_out = head_deal(mlp_sum, H)
    d_attn = [part.reshape(MICRO, 2, half, QD) for part in d_attn]
    tables = (H, 2, half, LANES)
    dq, dkv_even, dkv_odd = attention_backward(
        scalars, q, kv_even, kv_odd, d_attn, o, lse, cosine.reshape(tables), sine.reshape(tables), heads,
        mlp_out[1:2],
    )
    pieces = (B // 2, group, 2 * KD)
    came = swap(dkv_odd.reshape(pieces), 1, B)
    dkv = core_scatter(add_up(scalars, dkv_even.reshape(pieces), came, ()), B)
    d_xn1, grad_even, grad_odd = input_back(
        scalars,
        dq.reshape(group, QD),
        dkv,
        per_group(cosine),
        per_group(sine),
        x,
        xn1.reshape(group, D),
        gain_two,
        qkv_even,
        qkv_odd,
        mlp_out[3:4],
    )
    out_away = grad_rows(scalars, o_own, (d_branch,), B, near=True, wait=[d_xn1])
    sum_out = grad_rows(
        scalars, o_own, (d_branch,), B, came=swap(out_away, 1, B), near=True, wait=[grad_gate_up]
    ).reshape(B // 2, block, D)

    def by_distance(values):
        values = values.astype(BF).reshape(H, wrows, -1)
        return head_deal(
            [lax.dynamic_index_in_dim(values, (mine + k) % H, 0, False) for k in range(H)], H
        )

    grad_out = by_distance(core_scatter_steps(sum_out, B))
    grad_gate_up = wide(scalars, grad_gate_up, grad_out[1:2])
    d_xn1 = head_exchange(d_xn1.reshape(H, tokens, D))
    grad_out = sum(part.astype(F32) for part in grad_out)
    grad_qkv = arrange(scalars, by_distance(xor_scatter(grad_even, grad_odd, B))).astype(F32)
    grad_gains = jnp.sum(grad_qkv[:, :, used : used + 2], 0)

    def side_by_side(values):
        return values.transpose(1, 0, 2).reshape(wrows, -1)

    output = (resid + RESIDUAL_SCALE * sum(part.astype(F32) for part in mlp_out)).astype(BF)
    output = jnp.einsum(
        "mrs,mrd->msd", order, output.reshape(MICRO, T, D), preferred_element_type=F32
    ).astype(BF)
    d_input = input_gradient(scalars, d_xn1, x_own, d_resid, gain_rows, place)
    return (
        output,
        d_input,
        grad_gains[:, 0],
        grad_gains[:, 1],
        side_by_side(grad_qkv[:, :, :QD]),
        side_by_side(grad_qkv[:, :, QD : QD + KD]),
        side_by_side(grad_qkv[:, :, QD + KD : used]),
        grad_out,
        grad_gate_up[:, :F],
        grad_gate_up[:, F:],
        grad_down,
    )


def solution(mesh):
    both = ("blk", "head")
    return jax.shard_map(
        body,
        mesh=mesh,
        in_specs=(
            P(None, both, None),
            P(None, both, None),
            P(),
            P(),
            P(both),
            P(both),
            P(both, None),
            P(both, None),
            P(both, None),
            P(both, None),
            P("blk", "head"),
            P("blk", "head"),
            P("head", "blk"),
        ),
        out_specs=(
            P(None, both, None),
            P(None, both, None),
            P(both),
            P(both),
            P(both, None),
            P(both, None),
            P(both, None),
            P(both, None),
            P("blk", "head"),
            P("blk", "head"),
            P("head", "blk"),
        ),
        check_vma=False,
    )
```

```python
import functools

import jax
import jax.numpy as jnp
from jax import lax
from jax.experimental import pallas as pl
from jax.experimental.pallas import tpu as pltpu
from jax.sharding import PartitionSpec as P

MODEL_WIDTH = 2048
QUERY_HEADS = 32
KEY_VALUE_HEADS = 8
HEAD_SIZE = 64
SHARED = QUERY_HEADS // KEY_VALUE_HEADS
MICRO = 2
LANES = 128

SCORE_SCALE = 0.015625
RESIDUAL_SCALE = 0.22
EPSILON = 1e-06
ROPE_BASE = 10000000.0
NEG_FILL = -1e30

BF = jnp.bfloat16
F32 = jnp.float32
VMEM_LIMIT = 56 * 1024 * 1024
COST = 0.1


def dot(left, right, contract):
    return lax.dot_general(left, right, (contract, ((), ())), preferred_element_type=F32)


def nn(left, right):
    return dot(left, right, ((1,), (0,)))


def tn(left, right):
    return dot(left, right, ((0,), (0,)))


def nt(left, right):
    return dot(left, right, ((1,), (1,)))


def swap(x, bit, devices):
    return lax.ppermute(x, "blk", [(i, i ^ bit) for i in range(devices)])


def xor_gather(x, devices, join=None):
    even = [x] + [swap(x, bit, devices) for bit in range(2, devices, 2)]
    even = (join or jnp.stack)(even)
    return even, swap(even, 1, devices)


def add(left, right):
    return (left.astype(F32) + right.astype(F32)).astype(BF)


def core_scatter(held, devices):
    came = [swap(held[bit // 2], bit, devices) for bit in range(2, devices, 2)]
    return sum((part.astype(F32) for part in came), held[0].astype(F32))


def first_step(held, devices):
    if devices != 8:
        return [swap(held[bit // 2], bit, devices) for bit in range(2, devices, 2)]
    half = held.shape[1] // 2
    return [swap(held[3, :half], 2, devices), swap(held[3, half:], 4, devices)]


def second_step(held, came, devices):
    if devices != 8:
        return came
    from_x, from_y = came
    half = held.shape[1] // 2
    h4 = jnp.concatenate([add(held[2, :half], from_x), held[2, half:]], 0)
    h2 = jnp.concatenate([held[1, :half], add(held[1, half:], from_y)], 0)
    return [swap(h2, 2, devices), swap(h4, 4, devices)]


def all_steps(held, came):
    return sum((part.astype(F32) for part in came), held[0].astype(F32))


def core_scatter_steps(held, devices):
    return all_steps(held, second_step(held, first_step(held, devices), devices))


def xor_scatter(even, odd, devices):
    return core_scatter(add(even, swap(odd, 1, devices)), devices)


def head_exchange(parts):
    return lax.all_to_all(parts, "head", split_axis=0, concat_axis=0, tiled=True)


def head_shift(x, by, devices):
    return lax.ppermute(x, "head", [(i, (i + by) % devices) for i in range(devices)])


def head_gather(x, devices):
    return [x] + [head_shift(x, k, devices) for k in range(1, devices)]


def head_deal(parts, devices):
    return [parts[0]] + [head_shift(parts[k], k, devices) for k in range(1, devices)]


def same_core_groups(devices):
    return [list(range(core, devices, 2)) for core in range(2)]


def plane_scatter(kept, devices, axis):
    return lax.psum_scatter(
        kept,
        "blk",
        scatter_dimension=axis,
        tiled=True,
        axis_index_groups=same_core_groups(devices),
    )


def call(kernel, grid, in_specs, out_specs, out_shape, scratch, flops, moved, args, wait=()):
    wait = tuple(wait)
    given = 1 + len(in_specs)
    in_specs = list(in_specs) + [pl.BlockSpec(memory_space=pl.ANY)] * len(wait)
    args = tuple(args) + wait

    def run(*refs):
        kernel(*refs[:given], *refs[given + len(wait) :])

    return pl.pallas_call(
        run,
        grid_spec=pltpu.PrefetchScalarGridSpec(
            num_scalar_prefetch=1,
            grid=grid,
            in_specs=in_specs,
            out_specs=out_specs,
            scratch_shapes=scratch,
        ),
        out_shape=out_shape,
        compiler_params=pltpu.CompilerParams(vmem_limit_bytes=VMEM_LIMIT),
        cost_estimate=pl.CostEstimate(
            flops=int(flops * COST), bytes_accessed=int(moved * COST), transcendentals=0
        ),
    )(*args)


def whole(shape):
    return pl.BlockSpec(shape, lambda *_: (0,) * len(shape))


def shape_of(shape, dtype):
    return jax.ShapeDtypeStruct(shape, dtype)


def chunk(scalars, j, width):
    return pl.ds(pl.multiple_of((scalars[0] ^ j) * width, LANES), width)


def turned(values):
    lane = lax.broadcasted_iota(jnp.int32, values.shape, 1) % HEAD_SIZE
    quarter = HEAD_SIZE // 2
    return jnp.where(
        lane < quarter,
        pltpu.roll(values, LANES - quarter, 1),
        pltpu.roll(values, quarter, 1),
    )


def rope_lanes(values, cosine, sine, first, limit):
    out = values * cosine + turned(values) * sine
    if first + LANES <= limit:
        return out
    lane = lax.broadcasted_iota(jnp.int32, values.shape, 1)
    return jnp.where(lane < limit - first, out, values)


def before(s, k, devices):
    return (s[1] + devices - k) % devices


def after(s, k, devices):
    return (s[1] + k) % devices


def order_kernel(s, x_ref, up_ref, place_ref, xs_ref, us_ref):
    M, T, D = x_ref.shape
    for m in range(M):
        rank = lax.broadcasted_iota(jnp.int32, (T, T), 0)
        order = (place_ref[m] == rank).astype(BF)
        at = pl.ds(m * T, T)
        x = nn(order, x_ref[m]).astype(BF)
        for h in range(xs_ref.shape[0]):
            xs_ref[h, at, :] = x
        us_ref[at, :] = nn(order, up_ref[m]).astype(BF)


def in_order(scalars, x, upstream, place, H, wait):
    M, T, D = x.shape
    out = shape_of((M * T, D), BF)
    return call(
        order_kernel,
        (1,),
        [whole(x.shape), whole(x.shape), whole((M, 1, T))],
        [whole((H,) + out.shape), whole(out.shape)],
        [shape_of((H,) + out.shape, BF), out],
        [],
        4 * M * T * T * D,
        10 * M * T * D,
        (scalars, x, upstream, place.reshape(M, 1, T)),
        wait,
    )


def pack_kernel(s, q_ref, k_ref, v_ref, g_ref, *outs):
    devices = len(outs)
    QD = q_ref.shape[1] // devices
    KD = k_ref.shape[1] // devices
    for k, out_ref in enumerate(outs):
        for h in range(devices):

            @pl.when(after(s, k, devices) == h)
            def _(out_ref=out_ref, h=h):
                out_ref[:, :QD] = q_ref[:, h * QD : (h + 1) * QD]
                out_ref[:, QD : QD + 2 * KD] = jnp.concatenate(
                    [k_ref[:, h * KD : (h + 1) * KD], v_ref[:, h * KD : (h + 1) * KD]], 1
                )
                out_ref[:, QD + 2 * KD :] = g_ref[...]


def pack_weights(scalars, w_query, w_key, w_value, gains, devices):
    rows = w_query.shape[0]
    columns = (w_query.shape[1] + w_key.shape[1] + w_value.shape[1]) // devices + LANES
    out = shape_of((rows, columns), BF)
    args = (scalars, w_query, w_key, w_value, gains)
    return call(
        pack_kernel,
        (1,),
        [whole(a.shape) for a in args[1:]],
        [whole(out.shape)] * devices,
        [out] * devices,
        [],
        0,
        8 * rows * columns * devices,
        args,
    )


def copies_kernel(s, from_ref, out_ref, *, scale):
    values = from_ref[...]
    if scale is not None:
        values = (scale * values.astype(F32)).astype(BF)
    for h in range(out_ref.shape[0]):
        out_ref[h] = values


def copies(scalars, values, m, H, scale, wait):
    rows = (values.shape[0] // MICRO, values.shape[1])
    shape = (H,) + rows
    return call(
        functools.partial(copies_kernel, scale=scale),
        (1,),
        [pl.BlockSpec(rows, lambda i, s: (m, 0))],
        [whole(shape)],
        [shape_of(shape, BF)],
        [],
        0,
        2 * H * values.size,
        (scalars, values),
        wait,
    )[0]


def hold_kernel(s, *refs):
    count = len(refs) // 2
    for from_ref, to_ref in zip(refs[:count], refs[count:]):
        to_ref[...] = from_ref[...]


def hold(scalars, arrays, wait):
    return call(
        hold_kernel,
        (1,),
        [whole(a.shape) for a in arrays],
        [whole(a.shape) for a in arrays],
        [shape_of(a.shape, a.dtype) for a in arrays],
        [],
        0,
        sum(4 * a.size for a in arrays),
        (scalars, *arrays),
        wait,
    )


def join_kernel(s, *refs):
    *parts, out_ref = refs
    for p, part_ref in enumerate(parts):
        out_ref[p] = part_ref[...]


def join(scalars, parts, wait=()):
    shape = (len(parts),) + parts[0].shape
    return call(
        join_kernel,
        (1,),
        [whole(p.shape) for p in parts],
        [whole(shape)],
        [shape_of(shape, parts[0].dtype)],
        [],
        0,
        4 * len(parts) * parts[0].size,
        (scalars, *parts),
        wait,
    )[0]


def total_kernel(s, held_ref, *refs):
    *came, out_ref = refs
    out_ref[...] = sum((part[...].astype(F32) for part in came), held_ref[0].astype(F32))


def total(scalars, held, came, wait):
    _, rows, columns = held.shape
    piece = pl.BlockSpec((rows // 4, columns), lambda i, s: (i, 0))
    return call(
        total_kernel,
        (4,),
        [pl.BlockSpec((1, rows // 4, columns), lambda i, s: (0, i, 0))] + [piece] * len(came),
        [piece],
        [shape_of((rows, columns), F32)],
        [],
        0,
        10 * rows * columns,
        (scalars, held, *came),
        wait,
    )[0]


def add_kernel(s, left_ref, right_ref, out_ref):
    out_ref[...] = add(left_ref[...], right_ref[...])


def add_up(scalars, left, right, wait):
    return call(
        add_kernel,
        (1,),
        [whole(left.shape), whole(left.shape)],
        [whole(left.shape)],
        [shape_of(left.shape, BF)],
        [],
        0,
        6 * left.size,
        (scalars, left, right),
        wait,
    )[0]


def wide_kernel(s, from_ref, out_ref):
    out_ref[...] = from_ref[...].astype(F32)


def wide(scalars, values, wait):
    rows, columns = values.shape
    piece = pl.BlockSpec((rows // 4, columns), lambda i, s: (i, 0))
    return call(
        wide_kernel,
        (4,),
        [piece],
        [piece],
        [shape_of(values.shape, F32)],
        [],
        0,
        6 * values.size,
        (scalars, values),
        wait,
    )[0]


def merge_kernel(s, *refs):
    *parts, out_ref = refs
    for m, part_ref in enumerate(parts):
        out_ref[:, m] = part_ref[...]


def merge(scalars, parts, wait):
    H, T, D = parts[0].shape
    shape = (H, len(parts), T, D)
    return call(
        merge_kernel,
        (1,),
        [whole((H, T, D))] * len(parts),
        [whole(shape)],
        [shape_of(shape, BF)],
        [],
        0,
        4 * len(parts) * H * T * D,
        (scalars, *parts),
        wait,
    )[0].reshape(H * len(parts) * T, D)


def arrange_kernel(s, *refs):
    *parts, out_ref = refs
    for k, part_ref in enumerate(parts):
        out_ref[before(s, k, len(parts))] = part_ref[...]


def arrange(scalars, parts, wait=()):
    shape = (len(parts),) + parts[0].shape
    return call(
        arrange_kernel,
        (1,),
        [whole(p.shape) for p in parts],
        [whole(shape)],
        [shape_of(shape, parts[0].dtype)],
        [],
        0,
        4 * len(parts) * parts[0].size,
        (scalars, *parts),
        wait,
    )[0]


def project_kernel(s, x_ref, we_ref, wo_ref, cos_ref, sin_ref, xn_ref, q_ref, kv_ref, gain_ref):
    H, _, T, D = x_ref.shape
    places, block, columns = we_ref.shape
    QD = q_ref.shape[-1]
    KD = kv_ref.shape[-1] // 2
    used = QD + 2 * KD

    @pl.when(pl.program_id(0) == 0)
    def _():
        for place in range(places):
            for parity, w_ref in enumerate((we_ref, wo_ref)):
                held = w_ref[place, :, used : used + LANES].astype(F32).T
                gain_ref[:, chunk(s, 2 * place + parity, block)] = held[:8]

    x = x_ref[:, 0].reshape(H * T, D).astype(F32)
    inverse = lax.rsqrt(jnp.mean(x * x, -1, keepdims=True) + EPSILON)
    xn = ((x * inverse) * gain_ref[0:1, :]).astype(BF)
    xn_ref[:, 0] = xn.reshape(H, T, D)
    acc = jnp.zeros((H * T, used), F32)
    for place in range(places):
        for parity, w_ref in enumerate((we_ref, wo_ref)):
            left = xn_ref[:, 0, :, chunk(s, 2 * place + parity, block)].reshape(H * T, block)
            acc = acc + nn(left, w_ref[place, :, :used])
    cosine = cos_ref[...]
    sine = sin_ref[...]
    for first in range(0, used, LANES):
        part = acc[:, first : first + LANES]
        if first < QD + KD:
            part = rope_lanes(part, cosine, sine, first, QD + KD)
        if first < QD:
            q_ref[:, 0, :, first : first + LANES] = (
                (part * SCORE_SCALE).astype(BF).reshape(H, T, LANES)
            )
        else:
            kv_ref[:, 0, :, first - QD : first - QD + LANES] = part.astype(BF).reshape(H, T, LANES)


def project(scalars, x, w_even, w_odd, cosine, sine, QD, KD, wait):
    H, M, T, D = x.shape
    used = QD + 2 * KD

    def rows(width):
        return pl.BlockSpec((H, 1, T, width), lambda m, s: (0, m, 0, 0))

    return call(
        project_kernel,
        (M,),
        [rows(D), whole(w_even.shape), whole(w_odd.shape), whole(cosine.shape), whole(sine.shape)],
        [rows(D), rows(QD), rows(2 * KD), whole((8, D))],
        [
            shape_of((H, M, T, D), BF),
            shape_of((H, M, T, QD), BF),
            shape_of((H, M, T, 2 * KD), BF),
            shape_of((8, D), F32),
        ],
        [],
        2 * H * M * T * D * used,
        4 * H * M * T * D + 4 * w_even.size,
        (scalars, x, w_even, w_odd, cosine, sine),
        wait,
    )


def run_offset(index, run, tile, half):
    if run == 0:
        return index
    return (tile - half) - (index // half) * half + index % half


def key_positions(s, natural, run, length, tile, half, blocks):
    row = lax.broadcasted_iota(jnp.int32, (4 * tile, 1), 0)
    part = row // tile
    owner = 4 * natural + ((s[0] & 3) ^ (((part & 1) << 1) | (part >> 1)))
    row_tile = owner if run == 0 else 2 * blocks - 1 - owner
    position = row_tile * tile + run_offset(row % tile, run, tile, half)
    return jnp.where(position < length, position, jnp.int32(1 << 30))


def query_positions(s, run, rows, tile, half, blocks):
    own = s[0] if run == 0 else 2 * blocks - 1 - s[0]
    lane = lax.broadcasted_iota(jnp.int32, (1, rows), 1) % tile
    return own * tile + run_offset(lane, run, tile, half)


def slab(even_ref, odd_ref, y, run, first, last):
    parts = [
        ref[2 * y + i, :, 0, run, :, first:last] for ref in (even_ref, odd_ref) for i in range(2)
    ]
    H, half, width = parts[0].shape
    return jnp.concatenate([part.reshape(H * half, width) for part in parts], 0)


def heads_across(ref, run, head, heads):
    H, _, _, half, _ = ref.shape
    first = head * SHARED * HEAD_SIZE
    values = ref[:, 0, run, :, first : first + SHARED * HEAD_SIZE]
    values = values.reshape(H * half, SHARED * HEAD_SIZE).astype(F32).T
    values = jnp.concatenate(
        [values[g * HEAD_SIZE : (g + 1) * HEAD_SIZE] for g in range(SHARED)], 1
    )
    return values


def padded(values, head, heads):
    values = values.astype(BF)
    if heads == 1:
        return values
    zeros = jnp.zeros_like(values)
    return jnp.concatenate([values, zeros] if head == 0 else [zeros, values], 0)


def heads_back(values, tile):
    return jnp.concatenate(
        [values[:, g * tile : (g + 1) * tile] for g in range(SHARED)], 0
    ).T


def slab_loops(s, length, run, tile, blocks, state, step):
    slabs = blocks // 4
    own = s[0] // 4
    if run == 0:
        return lax.fori_loop(0, own + 1, lambda n, st: step(st, n, 0, True), state)
    state = lax.fori_loop(0, slabs, lambda n, st: step(st, n, 0, False), state)
    within = (2 * blocks * tile - length) // (4 * tile)
    return lax.fori_loop(
        jnp.maximum(own, within), slabs, lambda n, st: step(st, n, 1, True), state
    )


def fold_rows(values, combine):
    rows, lanes = values.shape
    return combine(values.reshape(rows // 8, 8, lanes), axis=0)


def forward_kernel(s, q_ref, ke_ref, ko_ref, o_ref, lse_ref, *, heads):
    H, _, _, half, QD = q_ref.shape
    blocks = 2 * ke_ref.shape[0]
    tile = H * half
    width = heads * HEAD_SIZE
    rows = SHARED * tile
    length = s[2 + pl.program_id(0)]
    for run in range(2):
        q = [padded(heads_across(q_ref, run, head, heads), head, heads) for head in range(heads)]
        at = query_positions(s, run, rows, tile, half, blocks)

        def step(state, natural, key_run, masked, q=q, at=at):
            y = natural ^ (s[0] >> 2)
            k = slab(ke_ref, ko_ref, y, key_run, 0, width)
            v = slab(ke_ref, ko_ref, y, key_run, width, 2 * width)
            if masked:
                seen = key_positions(s, natural, key_run, length, tile, half, blocks) <= at
            new = []
            for head in range(heads):
                top, total, acc = state[head]
                scores = nn(k, q[head])
                if masked:
                    scores = jnp.where(seen, scores, NEG_FILL)
                best = jnp.maximum(top, jnp.max(fold_rows(scores, jnp.max), 0, keepdims=True))
                p = jnp.exp(scores - best)
                scale = jnp.exp(top - best)
                total = total * scale + jnp.sum(fold_rows(p, jnp.sum), 0, keepdims=True)
                new.append((best, total, acc * scale + tn(v, p.astype(BF))))
            return tuple(new)

        start = tuple(
            (
                jnp.full((1, rows), NEG_FILL, F32),
                jnp.zeros((1, rows), F32),
                jnp.zeros((width, rows), F32),
            )
            for _ in range(heads)
        )
        done = slab_loops(s, length, run, tile, blocks, start, step)
        for head in range(heads):
            top, total, acc = done[head]
            lse_ref[0, run, head] = top + jnp.log(total)
            out = acc[head * HEAD_SIZE : (head + 1) * HEAD_SIZE] / total
            first = head * SHARED * HEAD_SIZE
            o_ref[:, 0, run, :, first : first + SHARED * HEAD_SIZE] = (
                heads_back(out, tile).astype(BF).reshape(H, half, SHARED * HEAD_SIZE)
            )


def backward_kernel(
    s, q_ref, ke_ref, ko_ref, o_ref, lse_ref, cos_ref, sin_ref, *refs, heads
):
    H, _, _, half, QD = q_ref.shape
    dq_ref, de_ref, dod_ref, acc_ref, do_ref = refs[H:]
    for k in range(H):
        do_ref[before(s, k, H), 0] = refs[k][0]
    blocks = 2 * ke_ref.shape[0]
    tile = H * half
    width = heads * HEAD_SIZE
    rows = SHARED * tile
    length = s[2 + pl.program_id(0)]
    acc_ref[...] = jnp.zeros(acc_ref.shape, F32)
    for run in range(2):
        q, do, lse, delta = [], [], [], []
        for head in range(heads):
            q.append(padded(heads_across(q_ref, run, head, heads), head, heads))
            up = heads_across(do_ref, run, head, heads)
            do.append(padded(up, head, heads))
            delta.append(
                jnp.sum(up * heads_across(o_ref, run, head, heads), 0, keepdims=True)
            )
            lse.append(lse_ref[0, run, head])
        at = query_positions(s, run, rows, tile, half, blocks)

        def step(state, natural, key_run, masked, q=q, do=do, lse=lse, delta=delta, at=at):
            y = natural ^ (s[0] >> 2)
            k = slab(ke_ref, ko_ref, y, key_run, 0, width)
            v = slab(ke_ref, ko_ref, y, key_run, width, 2 * width)
            if masked:
                seen = key_positions(s, natural, key_run, length, tile, half, blocks) <= at
            new = []
            dk = jnp.zeros((4 * tile, width), F32)
            dv = jnp.zeros((4 * tile, width), F32)
            for head in range(heads):
                p = jnp.exp(nn(k, q[head]) - lse[head])
                if masked:
                    p = jnp.where(seen, p, 0.0)
                ds = (p * (nn(v, do[head]) - delta[head])).astype(BF)
                dk = dk + nt(ds, q[head])
                dv = dv + nt(p.astype(BF), do[head])
                new.append(state[head] + tn(k, ds))
            acc_ref[key_run, y, :, :width] += dk
            acc_ref[key_run, y, :, width:] += dv
            return tuple(new)

        start = tuple(jnp.zeros((width, rows), F32) for _ in range(heads))
        done = slab_loops(s, length, run, tile, blocks, start, step)
        cosine = cos_ref[:, run].reshape(tile, LANES)
        sine = sin_ref[:, run].reshape(tile, LANES)
        for head in range(heads):
            out = done[head][head * HEAD_SIZE : (head + 1) * HEAD_SIZE]
            out = (heads_back(out, tile) * SCORE_SCALE).astype(BF).astype(F32)
            for lanes in range(0, SHARED * HEAD_SIZE, LANES):
                part = out[:, lanes : lanes + LANES]
                part = part * cosine - turned(part) * sine
                first = head * SHARED * HEAD_SIZE + lanes
                dq_ref[:, 0, run, :, first : first + LANES] = part.astype(BF).reshape(
                    H, half, LANES
                )
    for run in range(2):
        for y in range(blocks // 4):
            for index, (ref, i) in enumerate(((de_ref, 0), (de_ref, 1), (dod_ref, 0), (dod_ref, 1))):
                ref[2 * y + i, :, 0, run] = (
                    acc_ref[run, y, index * tile : (index + 1) * tile]
                    .astype(BF)
                    .reshape(H, half, 2 * width)
                )


def attention_specs(q, kv, heads):
    H, M, _, half, QD = q.shape
    places, _, _, _, _, width = kv.shape
    per_q = pl.BlockSpec((H, 1, 2, half, QD), lambda m, s: (0, m, 0, 0, 0))
    per_kv = pl.BlockSpec((places, H, 1, 2, half, width), lambda m, s: (0, 0, m, 0, 0, 0))
    per_row = pl.BlockSpec((1, 2, heads, 1, SHARED * H * half), lambda m, s: (m, 0, 0, 0, 0))
    work = M * places * H * half * SHARED * H * half * QD
    return per_q, per_kv, per_row, work


def attention_forward(scalars, q, k_even, k_odd, heads, wait):
    H, M, _, half, QD = q.shape
    per_q, per_kv, per_row, work = attention_specs(q, k_even, heads)
    return call(
        functools.partial(forward_kernel, heads=heads),
        (M,),
        [per_q, per_kv, per_kv],
        [per_q, per_row],
        [shape_of(q.shape, BF), shape_of((M, 2, heads, 1, SHARED * H * half), F32)],
        [],
        8 * work,
        2 * (2 * q.size + 2 * k_even.size),
        (scalars, q, k_even, k_odd),
        wait,
    )


def attention_backward(scalars, q, k_even, k_odd, do_parts, o, lse, cosine, sine, heads, wait):
    H, M, _, half, QD = q.shape
    per_q, per_kv, per_row, work = attention_specs(q, k_even, heads)
    blocks = 2 * k_even.shape[0]
    return call(
        functools.partial(backward_kernel, heads=heads),
        (M,),
        [per_q, per_kv, per_kv, per_q, per_row, whole(cosine.shape), whole(sine.shape)]
        + [pl.BlockSpec((1, 2, half, QD), lambda m, s: (m, 0, 0, 0))] * H,
        [per_q, per_kv, per_kv],
        [shape_of(q.shape, BF), shape_of(k_even.shape, BF), shape_of(k_odd.shape, BF)],
        [
            pltpu.VMEM((2, blocks // 4, 4 * H * half, 2 * heads * HEAD_SIZE), F32),
            pltpu.VMEM((H, 1, 2, half, QD), BF),
        ],
        20 * work,
        2 * (4 * q.size + 4 * k_even.size),
        (scalars, q, k_even, k_odd, o, lse, cosine, sine, *do_parts),
        wait,
    )


def out_kernel(s, x_ref, gain_ref, w_ref, *refs):
    devices = len(refs) - 4
    xn_ref, own_ref, o_own_ref, acc_ref = refs[devices:]
    n = pl.program_id(0)
    group, QD = refs[0].shape
    columns = w_ref.shape[1]
    rows = group // devices

    @pl.when(n == 0)
    def _():
        at = pl.ds(pl.multiple_of(s[1] * rows, rows), rows)
        for k in range(devices):
            lanes = pl.ds(pl.multiple_of(before(s, k, devices) * QD, LANES), QD)
            o_own_ref[:, lanes] = refs[k][at, :]

    got = jnp.zeros((group, columns), F32)
    for k in range(devices):
        first = pl.multiple_of(before(s, k, devices) * QD, QD)
        got = got + nn(refs[k][...], w_ref[pl.ds(first, QD), :])
    acc_ref[:, pl.ds(pl.multiple_of(n * columns, LANES), columns)] = got

    @pl.when(n == pl.num_programs(0) - 1)
    def _():
        def finish(h, carry):
            at = pl.ds(pl.multiple_of(h * rows, rows), rows)
            resid = x_ref[at, :].astype(F32) + RESIDUAL_SCALE * acc_ref[at, :]
            inverse = lax.rsqrt(jnp.mean(resid * resid, -1, keepdims=True) + EPSILON)
            xn_ref[at, :] = ((resid * inverse) * gain_ref[1:2, :]).astype(BF)

            @pl.when(h == s[1])
            def _():
                own_ref[...] = resid

            return carry

        lax.fori_loop(0, devices, finish, 0)


def out_project(scalars, o_parts, x, gains, w_out, wait):
    H = len(o_parts)
    group, QD = o_parts[0].shape
    D = w_out.shape[1]
    rows = group // H
    columns = 512
    piece = pl.BlockSpec((H * QD, columns), lambda n, s: (0, n))
    return call(
        out_kernel,
        (D // columns,),
        [whole(x.shape), whole(gains.shape), piece] + [whole((group, QD))] * H,
        [whole((group, D)), whole((rows, D)), whole((rows, H * QD))],
        [shape_of((group, D), BF), shape_of((rows, D), F32), shape_of((rows, H * QD), BF)],
        [pltpu.VMEM((group, D), F32)],
        2 * group * H * QD * D,
        2 * (H * group * QD + 2 * x.size + w_out.size),
        (scalars, x, gains, w_out, *o_parts),
        wait,
    )


def mlp_forward_kernel(s, xn_ref, wg_ref, wu_ref, gate_ref, up_ref, hidden_ref):
    gate = nn(xn_ref[...], wg_ref[...])
    up = nn(xn_ref[...], wu_ref[...])
    gate_ref[...] = gate
    up_ref[...] = up
    hidden_ref[...] = (gate * (1.0 / (1.0 + jnp.exp(-gate))) * up).astype(BF)


def mlp_forward(scalars, xn, w_gate_up, tile, wait):
    group, D = xn.shape
    F = w_gate_up.shape[1] // 2
    count = F // tile
    out = pl.BlockSpec((group, tile), lambda f, s: (0, f))
    return call(
        mlp_forward_kernel,
        (count,),
        [
            whole(xn.shape),
            pl.BlockSpec((D, tile), lambda f, s: (0, f)),
            pl.BlockSpec((D, tile), lambda f, s: (0, f + count)),
        ],
        [out, out, out],
        [shape_of((group, F), F32), shape_of((group, F), F32), shape_of((group, F), BF)],
        [],
        4 * group * D * F,
        2 * (group * D + 2 * D * F + 5 * group * F),
        (scalars, xn, w_gate_up, w_gate_up),
        wait,
    )


def down_kernel(s, hidden_ref, w_ref, *outs):
    got_ref = outs[-1]
    rows = outs[0].shape[0]
    devices = got_ref.shape[0] // rows
    got_ref[...] = nn(hidden_ref[...], w_ref[...]).astype(BF)
    for k in range(devices):
        at = pl.ds(pl.multiple_of(after(s, k, devices) * rows, rows), rows)
        outs[k][...] = got_ref[at, :]


def down_project(scalars, hidden, w_down, devices, wait):
    group, F = hidden.shape
    D = w_down.shape[1]
    width = 512
    rows = group // devices
    return call(
        down_kernel,
        (D // width,),
        [whole(hidden.shape), pl.BlockSpec((F, width), lambda n, s: (0, n))],
        [pl.BlockSpec((rows, width), lambda n, s: (0, n))] * devices,
        [shape_of((rows, D), BF)] * devices,
        [pltpu.VMEM((group, width), BF)],
        2 * group * D * F,
        2 * (group * D + D * F + group * F),
        (scalars, hidden, w_down),
        wait,
    )


def mlp_backward_kernel(
    s, gate_ref, up_ref, wg_ref, wu_ref, wd_ref, dmo_ref, dg_ref, du_ref, dxn_ref, acc_ref
):
    f = pl.program_id(0)
    d_hidden = nt(dmo_ref[...], wd_ref[...])
    gate = gate_ref[...]
    sigma = 1.0 / (1.0 + jnp.exp(-gate))
    dg_ref[...] = (d_hidden * up_ref[...] * (sigma * (1.0 + gate * (1.0 - sigma)))).astype(BF)
    du_ref[...] = (d_hidden * (gate * sigma)).astype(BF)
    got = nt(dg_ref[...], wg_ref[...]) + nt(du_ref[...], wu_ref[...])

    @pl.when(f == 0)
    def _():
        acc_ref[...] = got

    @pl.when(f > 0)
    def _():
        acc_ref[...] += got

    @pl.when(f == pl.num_programs(0) - 1)
    def _():
        dxn_ref[...] = acc_ref[...].astype(BF)


def mlp_backward(scalars, gate, up, dmo, w_gate_up, w_down, tile, wait):
    group, D = dmo.shape
    F = gate.shape[1]
    count = F // tile
    per_f = pl.BlockSpec((group, tile), lambda f, s: (0, f))
    return call(
        mlp_backward_kernel,
        (count,),
        [
            per_f,
            per_f,
            pl.BlockSpec((D, tile), lambda f, s: (0, f)),
            pl.BlockSpec((D, tile), lambda f, s: (0, f + count)),
            pl.BlockSpec((tile, D), lambda f, s: (f, 0)),
            whole((group, D)),
        ],
        [per_f, per_f, whole((group, D))],
        [shape_of((group, F), BF), shape_of((group, F), BF), shape_of((group, D), BF)],
        [pltpu.VMEM((group, D), F32)],
        6 * group * D * F,
        2 * (3 * group * D + 3 * D * F + 6 * group * F),
        (scalars, gate, up, w_gate_up, w_gate_up, w_down, dmo),
        wait,
    )


def block_lanes(s, own, near, block):
    i = pl.program_id(0)
    if near:
        index = s[0] ^ (2 * i if own else 2 * i + 1)
    else:
        index = 2 * i + (s[0] % 2 if own else 1 - s[0] % 2)
    return pl.ds(pl.multiple_of(index * block, LANES), block)


def rows_kernel(s, left_ref, *refs, own, count, near):
    right = refs[:count]
    out_ref = refs[-1]
    block = out_ref.shape[0]
    lanes = block_lanes(s, own, near, block)
    left = left_ref[:, lanes]
    at = 0
    for i, right_ref in enumerate(right):
        width = right_ref.shape[1]
        got = tn(left, right_ref[...])
        if own:
            got = got + refs[count][:, at : at + width].astype(F32)
        out_ref[:, at : at + width] = got.astype(BF)
        at += width


def grad_rows(scalars, left, rights, blocks, came=None, near=False, wait=()):
    n, D = left.shape
    block = D // blocks
    width = sum(r.shape[1] for r in rights)
    piece = pl.BlockSpec((block, width), lambda i, s: (i, 0))
    extra = [] if came is None else [came]
    return call(
        functools.partial(
            rows_kernel, own=came is not None, count=len(rights), near=near
        ),
        (blocks // 2,),
        [whole(left.shape)] + [whole(r.shape) for r in rights] + [piece] * len(extra),
        [piece],
        [shape_of((D // 2, width), BF)],
        [],
        n * D * width,
        2 * (left.size + n * width + D * width),
        (scalars, left, *rights, *extra),
        wait,
    )[0]


def columns_kernel(s, left_ref, right_ref, *refs, own):
    out_ref = refs[-1]
    got = tn(left_ref[...], right_ref[:, block_lanes(s, own, True, out_ref.shape[2])])
    if own:
        got = got + refs[0][0].astype(F32)
    out_ref[0] = got.astype(BF)


def grad_columns(scalars, left, right, blocks, came=None, wait=()):
    n, F = left.shape
    D = right.shape[1]
    block = D // blocks
    piece = pl.BlockSpec((1, F, block), lambda i, s: (i, 0, 0))
    extra = [] if came is None else [came]
    return call(
        functools.partial(columns_kernel, own=came is not None),
        (blocks // 2,),
        [whole(left.shape), whole(right.shape)] + [piece] * len(extra),
        [piece],
        [shape_of((blocks // 2, F, block), BF)],
        [],
        n * D * F,
        2 * (left.size + right.size + D * F),
        (scalars, left, right, *extra),
        wait,
    )[0]


def through_norm(upstream, gain, values):
    inverse = lax.rsqrt(jnp.mean(values * values, -1, keepdims=True) + EPSILON)
    scaled = values * inverse
    through = upstream * gain
    inner = jnp.mean(through * scaled, -1, keepdims=True)
    return inverse * (through - scaled * inner), scaled


def branch_kernel(s, parts, resid_ref, up_ref, gain_ref, w_ref, *refs):
    devices = len(refs) - 4
    dresid_ref, da_ref, gg_ref = refs[:3]
    outs = refs[3:-1]
    dattn_ref = refs[-1]
    p = pl.program_id(0)

    @pl.when(p == 0)
    def _():
        upstream = parts[0].astype(F32)
        for h in range(1, parts.shape[0]):
            upstream = upstream + parts[h].astype(F32)
        back, scaled = through_norm(upstream, gain_ref[1:2, :], resid_ref[...])
        gg_ref[...] = jnp.broadcast_to(
            jnp.sum(upstream * scaled, 0, keepdims=True), gg_ref.shape
        )
        d_resid = up_ref[...].astype(F32) + back
        dresid_ref[...] = d_resid
        da_ref[...] = (RESIDUAL_SCALE * d_resid).astype(BF)

    dattn_ref[p] = nt(da_ref[...], w_ref[...]).astype(BF)

    @pl.when(p == pl.num_programs(0) - 1)
    def _():
        for k in range(devices):
            outs[k][...] = dattn_ref[after(s, k, devices)]


def branch_back(scalars, parts, resid, upstream, gains, w_out, H, wait):
    _, tokens, D = parts.shape
    QD = w_out.shape[0] // H
    return call(
        branch_kernel,
        (H,),
        [whole(a.shape) for a in (parts, resid, upstream, gains)]
        + [pl.BlockSpec((QD, D), lambda p, s: (p, 0))],
        [whole((tokens, D)), whole((tokens, D)), whole((8, D))] + [whole((tokens, QD))] * H,
        [shape_of((tokens, D), F32), shape_of((tokens, D), BF), shape_of((8, D), F32)]
        + [shape_of((tokens, QD), BF)] * H,
        [pltpu.VMEM((H, tokens, QD), BF)],
        2 * tokens * D * H * QD,
        2 * (H * tokens * D + w_out.size + 6 * tokens * D),
        (scalars, parts, resid, upstream, gains, w_out),
        wait,
    )


def input_kernel(
    s, dq_ref, dkv_ref, cos_ref, sin_ref, x_ref, xn_ref, gg_ref, we_ref, wo_ref, *refs
):
    out_ref, ge_ref, go_ref, dqkv_ref, inv_ref = refs
    p = pl.program_id(0)
    group, QD = dq_ref.shape
    KD = dkv_ref.shape[1] // 2
    used = QD + 2 * KD
    block = we_ref.shape[1]

    @pl.when(p == 0)
    def _():
        dqkv_ref[:, :QD] = dq_ref[...]
        for first in range(0, 2 * KD, LANES):
            part = dkv_ref[:, first : first + LANES].astype(F32)
            if first < KD:
                part = rope_lanes(part, cos_ref[...], -sin_ref[...], first, KD)
            dqkv_ref[:, QD + first : QD + first + LANES] = part.astype(BF)
        x = x_ref[...].astype(F32)
        inv_ref[...] = jnp.broadcast_to(
            lax.rsqrt(jnp.mean(x * x, -1, keepdims=True) + EPSILON), inv_ref.shape
        )

    for parity, (w_ref, g_ref) in enumerate(((we_ref, ge_ref), (wo_ref, go_ref))):
        lanes = chunk(s, 2 * p + parity, block)
        dxn = nt(dqkv_ref[...], w_ref[0, :, :used])
        out_ref[:, lanes] = dxn.astype(BF)
        scaled = x_ref[:, lanes].astype(F32) * inv_ref[:, 0:1]
        gain_one = jnp.sum(dxn * scaled, 0, keepdims=True)
        g_ref[0, :, :used] = tn(xn_ref[:, lanes], dqkv_ref[...]).astype(BF)
        row = lax.broadcasted_iota(jnp.int32, (LANES, block), 0)
        both = jnp.where(row == 0, gain_one, jnp.where(row == 1, gg_ref[0:1, lanes], 0.0))
        g_ref[0, :, used:] = both.T.astype(BF)


def input_back(scalars, dq, dkv, cosine, sine, x, xn, gain_two, w_even, w_odd, wait):
    group, D = x.shape
    QD = dq.shape[1]
    places, block, columns = w_even.shape
    piece = pl.BlockSpec((1, block, columns), lambda p, s: (p, 0, 0))
    return call(
        input_kernel,
        (places,),
        [whole(a.shape) for a in (dq, dkv, cosine, sine, x, xn, gain_two)] + [piece, piece],
        [whole(x.shape), piece, piece],
        [shape_of(x.shape, BF), shape_of(w_even.shape, BF), shape_of(w_even.shape, BF)],
        [
            pltpu.VMEM((group, QD + dkv.shape[1]), BF),
            pltpu.VMEM((group, LANES), F32),
        ],
        4 * group * D * (QD + dkv.shape[1]),
        2 * (3 * x.size + 4 * w_even.size),
        (scalars, dq, dkv, cosine, sine, x, xn, gain_two, w_even, w_odd),
        wait,
    )


def last_kernel(s, parts_ref, x_ref, resid_ref, gain_ref, place_ref, out_ref):
    M, T, _ = out_ref.shape
    for m in range(M):
        at = pl.ds(m * T, T)
        upstream = parts_ref[0, at, :].astype(F32)
        for h in range(1, parts_ref.shape[0]):
            upstream = upstream + parts_ref[h, at, :].astype(F32)
        back, _ = through_norm(upstream, gain_ref[0:1, :], x_ref[at, :].astype(F32))
        total = resid_ref[at, :] + back
        rank = lax.broadcasted_iota(jnp.int32, (T, T), 0)
        order = (place_ref[m] == rank).astype(F32)
        out_ref[m] = lax.dot_general(
            order,
            total,
            (((0,), (0,)), ((), ())),
            precision=lax.Precision.HIGHEST,
            preferred_element_type=F32,
        )


def input_gradient(scalars, parts, x, d_resid, gains, place, wait):
    M, T = place.shape
    D = x.shape[1]
    place = place.reshape(M, 1, T)
    args = (scalars, parts, x, d_resid, gains, place)
    return call(
        last_kernel,
        (1,),
        [whole(a.shape) for a in args[1:]],
        [whole((M, T, D))],
        [shape_of((M, T, D), F32)],
        [],
        4 * M * T * T * D,
        12 * M * T * D,
        args,
        wait,
    )[0]


def body(
    inputs,
    cotangent,
    lengths,
    positions,
    attn_gain,
    mlp_gain,
    w_query,
    key_projection,
    value_projection,
    w_out,
    w_gate,
    w_up,
    w_down,
):
    B = lax.axis_size("blk")
    H = lax.axis_size("head")
    me = lax.axis_index("blk")
    mine = lax.axis_index("head")
    T = inputs.shape[1]
    D = MODEL_WIDTH
    half = T // 2
    slots = T * H * B
    heads = KEY_VALUE_HEADS // H
    KD = heads * HEAD_SIZE
    QD = KD * SHARED
    used = QD + 2 * KD
    tokens = MICRO * T
    group = H * tokens
    wrows = w_query.shape[0]
    F = w_gate.shape[1]
    block = D // B
    tile = min(512, F)

    scalars = jnp.concatenate(
        [jnp.stack([me, mine]).astype(jnp.int32), lengths.astype(jnp.int32)]
    )

    gains = jnp.concatenate(
        [attn_gain[:, None], mlp_gain[:, None], jnp.zeros((wrows, LANES - 2), BF)], 1
    )
    pack = pack_weights(scalars, w_query, key_projection, value_projection, gains, H)
    linear = me * H + mine
    my_pos = lax.dynamic_slice_in_dim(positions, linear * T, T, axis=1)
    place = jnp.where(
        my_pos < slots // 2, my_pos - half * linear, half + my_pos - (slots - half * (linear + 1))
    ).astype(jnp.int32)
    order = (place[:, None, :] == jnp.arange(T)[None, :, None]).astype(BF)
    pack = arrange(scalars, head_deal(pack, H)).reshape(H * wrows, used + LANES)
    x_copies, upstream = in_order(scalars, inputs, cotangent, place, H, [pack])
    x_own = x_copies[0]
    x = head_exchange(x_copies)
    qkv_even, qkv_odd = xor_gather(pack, B)

    w_gate_up = lax.all_gather(jnp.concatenate([w_gate, w_up], 1), "blk", axis=0, tiled=True)
    dmo_copies = copies(scalars, upstream, 0, H, RESIDUAL_SCALE, [x])
    dmo_parts = [head_exchange(dmo_copies)]

    run_start = jnp.arange(H)[:, None, None] + me * H
    i = jnp.arange(half)[None, None, :]
    row_pos = jnp.concatenate([half * run_start + i, slots - half * (run_start + 1) + i], 1)
    half_dim = HEAD_SIZE // 2
    frequency = ROPE_BASE ** (-(jnp.arange(half_dim).astype(F32) * 2.0) / HEAD_SIZE)
    angles = row_pos.reshape(H * T, 1).astype(F32) * frequency[None, :]
    cosine = jnp.cos(angles)
    sine = jnp.sin(angles)
    cosine = jnp.concatenate([cosine] * 4, 1)
    sine = jnp.concatenate([-sine, sine] * 2, 1)

    def per_group(table):
        return jnp.broadcast_to(
            table.reshape(H, 1, T, LANES), (H, MICRO, T, LANES)
        ).reshape(group, LANES)

    xn1, q, kv, gain_rows = project(
        scalars,
        x.reshape(H, MICRO, T, D),
        qkv_even,
        qkv_odd,
        cosine,
        sine,
        QD,
        KD,
        [dmo_copies],
    )
    x = x.reshape(group, D)
    runs = (H, MICRO, 2, half)
    q = q.reshape(runs + (QD,))
    kv_even, kv_odd = xor_gather(kv.reshape(group, 2 * KD), B)
    kv_even = kv_even.reshape((B // 2,) + runs + (2 * KD,))
    kv_odd = kv_odd.reshape((B // 2,) + runs + (2 * KD,))
    w_o = lax.all_gather(
        hold(scalars, [w_out], [w_gate_up, kv])[0], "head", axis=0, tiled=True
    )
    o, lse = attention_forward(scalars, q, kv_even, kv_odd, heads, dmo_parts)
    o_parts = head_gather(o.reshape(group, QD), H)
    w_o = lax.all_gather(hold(scalars, [w_o], [lse])[0], "blk", axis=0, tiled=True)
    w_d = lax.all_gather(hold(scalars, [w_down], [lse])[0], "blk", axis=1, tiled=True)
    later = [copies(scalars, upstream, m, H, RESIDUAL_SCALE, o_parts[1:]) for m in range(1, MICRO)]
    dmo_parts = dmo_parts + [head_exchange(part) for part in later]
    xn2, resid, o_own = out_project(
        scalars, o_parts, x, gain_rows, w_o, later
    )
    gate, up, hidden = mlp_forward(scalars, xn2, w_gate_up, tile, ())
    dmo = merge(scalars, dmo_parts, [hidden])
    came_down = swap(grad_columns(scalars, hidden, dmo, B), 1, B)
    sum_down = grad_columns(scalars, hidden, dmo, B, came_down)
    down_first = first_step(sum_down, B)
    d_gate, d_up, d_xn2 = mlp_backward(
        scalars, gate, up, dmo, w_gate_up, w_d, tile, [sum_down]
    )
    d_xn2 = lax.psum_scatter(d_xn2, "head", scatter_dimension=0, tiled=True)[None]

    came = swap(grad_rows(scalars, xn2, (d_gate, d_up), B, wait=down_first), 1, B)
    down_second = second_step(sum_down, down_first, B)
    sum_gate_up = grad_rows(scalars, xn2, (d_gate, d_up), B, came)
    grad_gate_up = plane_scatter(sum_gate_up, B, 0)
    mlp_sum = down_project(scalars, hidden, w_d, H, [sum_gate_up])


    d_resid, d_branch, gain_two, *d_attn = branch_back(
        scalars,
        d_xn2,
        resid,
        upstream,
        gain_rows,
        w_o,
        H,
        [sum_gate_up, mlp_sum[0]],
    )
    d_attn = head_deal(d_attn, H)
    mlp_out = head_deal(mlp_sum, H)
    d_attn = [part.reshape(MICRO, 2, half, QD) for part in d_attn]
    tables = (H, 2, half, LANES)
    dq, dkv_even, dkv_odd = attention_backward(
        scalars, q, kv_even, kv_odd, d_attn, o, lse, cosine.reshape(tables), sine.reshape(tables), heads,
        mlp_out[1:2],
    )
    pieces = (B // 2, group, 2 * KD)
    came = swap(dkv_odd.reshape(pieces), 1, B)
    dkv = core_scatter(add_up(scalars, dkv_even.reshape(pieces), came, ()), B)
    d_xn1, grad_even, grad_odd = input_back(
        scalars,
        dq.reshape(group, QD),
        dkv,
        per_group(cosine),
        per_group(sine),
        x,
        xn1.reshape(group, D),
        gain_two,
        qkv_even,
        qkv_odd,
        mlp_out[2:],
    )
    out_away = grad_rows(scalars, o_own, (d_branch,), B, near=True, wait=[d_xn1])
    sum_out = grad_rows(
        scalars, o_own, (d_branch,), B, came=swap(out_away, 1, B), near=True, wait=[grad_gate_up]
    ).reshape(B // 2, block, D)

    def by_distance(values):
        values = values.astype(BF).reshape(H, wrows, -1)
        return head_deal(
            [lax.dynamic_index_in_dim(values, (mine + k) % H, 0, False) for k in range(H)], H
        )

    grad_out = by_distance(core_scatter_steps(sum_out, B))
    grad_gate_up = wide(scalars, grad_gate_up, grad_out[2:3])
    d_xn1 = lax.psum_scatter(d_xn1, "head", scatter_dimension=0, tiled=True)[None]
    grad_down = total(scalars, sum_down, down_second, [d_xn1] + grad_out[1:2])
    grad_qkv = arrange(scalars, by_distance(xor_scatter(grad_even, grad_odd, B))).astype(F32)
    grad_gains = jnp.sum(grad_qkv[:, :, used : used + 2], 0)

    def side_by_side(values):
        return values.transpose(1, 0, 2).reshape(wrows, -1)

    output = (resid + RESIDUAL_SCALE * sum(part.astype(F32) for part in mlp_out)).astype(BF)
    output = jnp.einsum(
        "mrs,mrd->msd", order, output.reshape(MICRO, T, D), preferred_element_type=F32
    ).astype(BF)
    d_input = input_gradient(scalars, d_xn1, x_own, d_resid, gain_rows, place, grad_out[3:])
    grad_out = sum(part.astype(F32) for part in grad_out)
    return (
        output,
        d_input,
        grad_gains[:, 0],
        grad_gains[:, 1],
        side_by_side(grad_qkv[:, :, :QD]),
        side_by_side(grad_qkv[:, :, QD : QD + KD]),
        side_by_side(grad_qkv[:, :, QD + KD : used]),
        grad_out,
        grad_gate_up[:, :F],
        grad_gate_up[:, F:],
        grad_down,
    )


def solution(mesh):
    both = ("blk", "head")
    return jax.shard_map(
        body,
        mesh=mesh,
        in_specs=(
            P(None, both, None),
            P(None, both, None),
            P(),
            P(),
            P(both),
            P(both),
            P(both, None),
            P(both, None),
            P(both, None),
            P(both, None),
            P("blk", "head"),
            P("blk", "head"),
            P("head", "blk"),
        ),
        out_specs=(
            P(None, both, None),
            P(None, both, None),
            P(both),
            P(both),
            P(both, None),
            P(both, None),
            P(both, None),
            P(both, None),
            P("blk", "head"),
            P("blk", "head"),
            P("head", "blk"),
        ),
        check_vma=False,
    )
```

```python
import functools

import jax
import jax.numpy as jnp
from jax import lax
from jax.experimental import pallas as pl
from jax.experimental.pallas import tpu as pltpu
from jax.sharding import PartitionSpec as P

MODEL_WIDTH = 2048
QUERY_HEADS = 32
KEY_VALUE_HEADS = 8
HEAD_SIZE = 64
SHARED = QUERY_HEADS // KEY_VALUE_HEADS
MICRO = 2
LANES = 128

SCORE_SCALE = 0.015625
RESIDUAL_SCALE = 0.22
EPSILON = 1e-06
ROPE_BASE = 10000000.0
NEG_FILL = -1e30

BF = jnp.bfloat16
F32 = jnp.float32
VMEM_LIMIT = 56 * 1024 * 1024
COST = 0.1


def dot(left, right, contract):
    return lax.dot_general(left, right, (contract, ((), ())), preferred_element_type=F32)


def nn(left, right):
    return dot(left, right, ((1,), (0,)))


def tn(left, right):
    return dot(left, right, ((0,), (0,)))


def nt(left, right):
    return dot(left, right, ((1,), (1,)))


def swap(x, bit, devices):
    return lax.ppermute(x, "blk", [(i, i ^ bit) for i in range(devices)])


def xor_gather(x, devices, join=None):
    even = [x] + [swap(x, bit, devices) for bit in range(2, devices, 2)]
    even = (join or jnp.stack)(even)
    return even, swap(even, 1, devices)


def add(left, right):
    return (left.astype(F32) + right.astype(F32)).astype(BF)


def core_scatter(held, devices):
    came = [swap(held[bit // 2], bit, devices) for bit in range(2, devices, 2)]
    return sum((part.astype(F32) for part in came), held[0].astype(F32))


def first_step(held, devices):
    if devices != 8:
        return [swap(held[bit // 2], bit, devices) for bit in range(2, devices, 2)]
    half = held.shape[1] // 2
    return [swap(held[3, :half], 2, devices), swap(held[3, half:], 4, devices)]


def second_step(held, came, devices):
    if devices != 8:
        return came
    from_x, from_y = came
    half = held.shape[1] // 2
    h4 = jnp.concatenate([add(held[2, :half], from_x), held[2, half:]], 0)
    h2 = jnp.concatenate([held[1, :half], add(held[1, half:], from_y)], 0)
    return [swap(h2, 2, devices), swap(h4, 4, devices)]


def all_steps(held, came):
    return sum((part.astype(F32) for part in came), held[0].astype(F32))


def core_scatter_steps(held, devices):
    return all_steps(held, second_step(held, first_step(held, devices), devices))


def xor_scatter(even, odd, devices):
    return core_scatter(add(even, swap(odd, 1, devices)), devices)


def head_exchange(parts):
    return lax.all_to_all(parts, "head", split_axis=0, concat_axis=0, tiled=True)


def head_shift(x, by, devices):
    return lax.ppermute(x, "head", [(i, (i + by) % devices) for i in range(devices)])


def head_gather(x, devices):
    return [x] + [head_shift(x, k, devices) for k in range(1, devices)]


def head_deal(parts, devices):
    return [parts[0]] + [head_shift(parts[k], k, devices) for k in range(1, devices)]


def same_core_groups(devices):
    return [list(range(core, devices, 2)) for core in range(2)]


def plane_scatter(kept, devices, axis):
    return lax.psum_scatter(
        kept,
        "blk",
        scatter_dimension=axis,
        tiled=True,
        axis_index_groups=same_core_groups(devices),
    )


def call(kernel, grid, in_specs, out_specs, out_shape, scratch, flops, moved, args, wait=()):
    wait = tuple(wait)
    given = 1 + len(in_specs)
    in_specs = list(in_specs) + [pl.BlockSpec(memory_space=pl.ANY)] * len(wait)
    args = tuple(args) + wait

    def run(*refs):
        kernel(*refs[:given], *refs[given + len(wait) :])

    return pl.pallas_call(
        run,
        grid_spec=pltpu.PrefetchScalarGridSpec(
            num_scalar_prefetch=1,
            grid=grid,
            in_specs=in_specs,
            out_specs=out_specs,
            scratch_shapes=scratch,
        ),
        out_shape=out_shape,
        compiler_params=pltpu.CompilerParams(vmem_limit_bytes=VMEM_LIMIT),
        cost_estimate=pl.CostEstimate(
            flops=int(flops * COST), bytes_accessed=int(moved * COST), transcendentals=0
        ),
    )(*args)


def whole(shape):
    return pl.BlockSpec(shape, lambda *_: (0,) * len(shape))


def shape_of(shape, dtype):
    return jax.ShapeDtypeStruct(shape, dtype)


def chunk(scalars, j, width):
    return pl.ds(pl.multiple_of((scalars[0] ^ j) * width, LANES), width)


def turned(values):
    lane = lax.broadcasted_iota(jnp.int32, values.shape, 1) % HEAD_SIZE
    quarter = HEAD_SIZE // 2
    return jnp.where(
        lane < quarter,
        pltpu.roll(values, LANES - quarter, 1),
        pltpu.roll(values, quarter, 1),
    )


def rope_lanes(values, cosine, sine, first, limit):
    out = values * cosine + turned(values) * sine
    if first + LANES <= limit:
        return out
    lane = lax.broadcasted_iota(jnp.int32, values.shape, 1)
    return jnp.where(lane < limit - first, out, values)


def before(s, k, devices):
    return (s[1] + devices - k) % devices


def after(s, k, devices):
    return (s[1] + k) % devices


def order_kernel(s, x_ref, up_ref, place_ref, xs_ref, us_ref):
    M, T, D = x_ref.shape
    for m in range(M):
        rank = lax.broadcasted_iota(jnp.int32, (T, T), 0)
        order = (place_ref[m] == rank).astype(BF)
        at = pl.ds(m * T, T)
        x = nn(order, x_ref[m]).astype(BF)
        for h in range(xs_ref.shape[0]):
            xs_ref[h, at, :] = x
        us_ref[at, :] = nn(order, up_ref[m]).astype(BF)


def in_order(scalars, x, upstream, place, H, wait):
    M, T, D = x.shape
    out = shape_of((M * T, D), BF)
    return call(
        order_kernel,
        (1,),
        [whole(x.shape), whole(x.shape), whole((M, 1, T))],
        [whole((H,) + out.shape), whole(out.shape)],
        [shape_of((H,) + out.shape, BF), out],
        [],
        4 * M * T * T * D,
        10 * M * T * D,
        (scalars, x, upstream, place.reshape(M, 1, T)),
        wait,
    )


def pack_kernel(s, q_ref, k_ref, v_ref, g_ref, *outs):
    devices = len(outs)
    QD = q_ref.shape[1] // devices
    KD = k_ref.shape[1] // devices
    for k, out_ref in enumerate(outs):
        for h in range(devices):

            @pl.when(after(s, k, devices) == h)
            def _(out_ref=out_ref, h=h):
                out_ref[:, :QD] = q_ref[:, h * QD : (h + 1) * QD]
                out_ref[:, QD : QD + 2 * KD] = jnp.concatenate(
                    [k_ref[:, h * KD : (h + 1) * KD], v_ref[:, h * KD : (h + 1) * KD]], 1
                )
                out_ref[:, QD + 2 * KD :] = g_ref[...]


def pack_weights(scalars, w_query, w_key, w_value, gains, devices):
    rows = w_query.shape[0]
    columns = (w_query.shape[1] + w_key.shape[1] + w_value.shape[1]) // devices + LANES
    out = shape_of((rows, columns), BF)
    args = (scalars, w_query, w_key, w_value, gains)
    return call(
        pack_kernel,
        (1,),
        [whole(a.shape) for a in args[1:]],
        [whole(out.shape)] * devices,
        [out] * devices,
        [],
        0,
        8 * rows * columns * devices,
        args,
    )


def copies_kernel(s, from_ref, out_ref, *, scale):
    values = from_ref[...]
    if scale is not None:
        values = (scale * values.astype(F32)).astype(BF)
    for h in range(out_ref.shape[0]):
        out_ref[h] = values


def copies(scalars, values, m, H, scale, wait):
    rows = (values.shape[0] // MICRO, values.shape[1])
    shape = (H,) + rows
    return call(
        functools.partial(copies_kernel, scale=scale),
        (1,),
        [pl.BlockSpec(rows, lambda i, s: (m, 0))],
        [whole(shape)],
        [shape_of(shape, BF)],
        [],
        0,
        2 * H * values.size,
        (scalars, values),
        wait,
    )[0]


def hold_kernel(s, *refs):
    count = len(refs) // 2
    for from_ref, to_ref in zip(refs[:count], refs[count:]):
        to_ref[...] = from_ref[...]


def hold(scalars, arrays, wait):
    return call(
        hold_kernel,
        (1,),
        [whole(a.shape) for a in arrays],
        [whole(a.shape) for a in arrays],
        [shape_of(a.shape, a.dtype) for a in arrays],
        [],
        0,
        sum(4 * a.size for a in arrays),
        (scalars, *arrays),
        wait,
    )


def join_kernel(s, *refs):
    *parts, out_ref = refs
    for p, part_ref in enumerate(parts):
        out_ref[p] = part_ref[...]


def join(scalars, parts, wait=()):
    shape = (len(parts),) + parts[0].shape
    return call(
        join_kernel,
        (1,),
        [whole(p.shape) for p in parts],
        [whole(shape)],
        [shape_of(shape, parts[0].dtype)],
        [],
        0,
        4 * len(parts) * parts[0].size,
        (scalars, *parts),
        wait,
    )[0]


def total_kernel(s, held_ref, *refs):
    *came, out_ref = refs
    out_ref[...] = sum((part[...].astype(F32) for part in came), held_ref[0].astype(F32))


def total(scalars, held, came, wait):
    _, rows, columns = held.shape
    piece = pl.BlockSpec((rows // 4, columns), lambda i, s: (i, 0))
    return call(
        total_kernel,
        (4,),
        [pl.BlockSpec((1, rows // 4, columns), lambda i, s: (0, i, 0))] + [piece] * len(came),
        [piece],
        [shape_of((rows, columns), F32)],
        [],
        0,
        10 * rows * columns,
        (scalars, held, *came),
        wait,
    )[0]


def add_kernel(s, left_ref, right_ref, out_ref):
    out_ref[...] = add(left_ref[...], right_ref[...])


def add_up(scalars, left, right, wait):
    return call(
        add_kernel,
        (1,),
        [whole(left.shape), whole(left.shape)],
        [whole(left.shape)],
        [shape_of(left.shape, BF)],
        [],
        0,
        6 * left.size,
        (scalars, left, right),
        wait,
    )[0]


def wide_kernel(s, from_ref, out_ref):
    out_ref[...] = from_ref[...].astype(F32)


def wide(scalars, values, wait):
    rows, columns = values.shape
    piece = pl.BlockSpec((rows // 4, columns), lambda i, s: (i, 0))
    return call(
        wide_kernel,
        (4,),
        [piece],
        [piece],
        [shape_of(values.shape, F32)],
        [],
        0,
        6 * values.size,
        (scalars, values),
        wait,
    )[0]


def merge_kernel(s, *refs):
    *parts, out_ref = refs
    for m, part_ref in enumerate(parts):
        out_ref[:, m] = part_ref[...]


def merge(scalars, parts, wait):
    H, T, D = parts[0].shape
    shape = (H, len(parts), T, D)
    return call(
        merge_kernel,
        (1,),
        [whole((H, T, D))] * len(parts),
        [whole(shape)],
        [shape_of(shape, BF)],
        [],
        0,
        4 * len(parts) * H * T * D,
        (scalars, *parts),
        wait,
    )[0].reshape(H * len(parts) * T, D)


def arrange_kernel(s, *refs):
    *parts, out_ref = refs
    for k, part_ref in enumerate(parts):
        out_ref[before(s, k, len(parts))] = part_ref[...]


def arrange(scalars, parts, wait=()):
    shape = (len(parts),) + parts[0].shape
    return call(
        arrange_kernel,
        (1,),
        [whole(p.shape) for p in parts],
        [whole(shape)],
        [shape_of(shape, parts[0].dtype)],
        [],
        0,
        4 * len(parts) * parts[0].size,
        (scalars, *parts),
        wait,
    )[0]


def project_kernel(s, x_ref, we_ref, wo_ref, cos_ref, sin_ref, xn_ref, q_ref, kv_ref, gain_ref):
    H, _, T, D = x_ref.shape
    places, block, columns = we_ref.shape
    QD = q_ref.shape[-1]
    KD = kv_ref.shape[-1] // 2
    used = QD + 2 * KD

    @pl.when(pl.program_id(0) == 0)
    def _():
        for place in range(places):
            for parity, w_ref in enumerate((we_ref, wo_ref)):
                held = w_ref[place, :, used : used + LANES].astype(F32).T
                gain_ref[:, chunk(s, 2 * place + parity, block)] = held[:8]

    x = x_ref[:, 0].reshape(H * T, D).astype(F32)
    inverse = lax.rsqrt(jnp.mean(x * x, -1, keepdims=True) + EPSILON)
    xn = ((x * inverse) * gain_ref[0:1, :]).astype(BF)
    xn_ref[:, 0] = xn.reshape(H, T, D)
    acc = jnp.zeros((H * T, used), F32)
    for place in range(places):
        for parity, w_ref in enumerate((we_ref, wo_ref)):
            left = xn_ref[:, 0, :, chunk(s, 2 * place + parity, block)].reshape(H * T, block)
            acc = acc + nn(left, w_ref[place, :, :used])
    cosine = cos_ref[...]
    sine = sin_ref[...]
    for first in range(0, used, LANES):
        part = acc[:, first : first + LANES]
        if first < QD + KD:
            part = rope_lanes(part, cosine, sine, first, QD + KD)
        if first < QD:
            q_ref[:, 0, :, first : first + LANES] = (
                (part * SCORE_SCALE).astype(BF).reshape(H, T, LANES)
            )
        else:
            kv_ref[:, 0, :, first - QD : first - QD + LANES] = part.astype(BF).reshape(H, T, LANES)


def project(scalars, x, w_even, w_odd, cosine, sine, QD, KD, wait):
    H, M, T, D = x.shape
    used = QD + 2 * KD

    def rows(width):
        return pl.BlockSpec((H, 1, T, width), lambda m, s: (0, m, 0, 0))

    return call(
        project_kernel,
        (M,),
        [rows(D), whole(w_even.shape), whole(w_odd.shape), whole(cosine.shape), whole(sine.shape)],
        [rows(D), rows(QD), rows(2 * KD), whole((8, D))],
        [
            shape_of((H, M, T, D), BF),
            shape_of((H, M, T, QD), BF),
            shape_of((H, M, T, 2 * KD), BF),
            shape_of((8, D), F32),
        ],
        [],
        2 * H * M * T * D * used,
        4 * H * M * T * D + 4 * w_even.size,
        (scalars, x, w_even, w_odd, cosine, sine),
        wait,
    )


def run_offset(index, run, tile, half):
    if run == 0:
        return index
    return (tile - half) - (index // half) * half + index % half


def key_positions(s, natural, run, length, tile, half, blocks):
    row = lax.broadcasted_iota(jnp.int32, (4 * tile, 1), 0)
    part = row // tile
    owner = 4 * natural + ((s[0] & 3) ^ (((part & 1) << 1) | (part >> 1)))
    row_tile = owner if run == 0 else 2 * blocks - 1 - owner
    position = row_tile * tile + run_offset(row % tile, run, tile, half)
    return jnp.where(position < length, position, jnp.int32(1 << 30))


def query_positions(s, run, rows, tile, half, blocks):
    own = s[0] if run == 0 else 2 * blocks - 1 - s[0]
    lane = lax.broadcasted_iota(jnp.int32, (1, rows), 1) % tile
    return own * tile + run_offset(lane, run, tile, half)


def slab(even_ref, odd_ref, y, run, first, last):
    parts = [
        ref[2 * y + i, :, 0, run, :, first:last] for ref in (even_ref, odd_ref) for i in range(2)
    ]
    H, half, width = parts[0].shape
    return jnp.concatenate([part.reshape(H * half, width) for part in parts], 0)


def heads_across(ref, run, head, heads):
    H, _, _, half, _ = ref.shape
    first = head * SHARED * HEAD_SIZE
    values = ref[:, 0, run, :, first : first + SHARED * HEAD_SIZE]
    values = values.reshape(H * half, SHARED * HEAD_SIZE).astype(F32).T
    values = jnp.concatenate(
        [values[g * HEAD_SIZE : (g + 1) * HEAD_SIZE] for g in range(SHARED)], 1
    )
    return values


def padded(values, head, heads):
    values = values.astype(BF)
    if heads == 1:
        return values
    zeros = jnp.zeros_like(values)
    return jnp.concatenate([values, zeros] if head == 0 else [zeros, values], 0)


def heads_back(values, tile):
    return jnp.concatenate(
        [values[:, g * tile : (g + 1) * tile] for g in range(SHARED)], 0
    ).T


def slab_loops(s, length, run, tile, blocks, state, step):
    slabs = blocks // 4
    own = s[0] // 4
    if run == 0:
        return lax.fori_loop(0, own + 1, lambda n, st: step(st, n, 0, True), state)
    state = lax.fori_loop(0, slabs, lambda n, st: step(st, n, 0, False), state)
    within = (2 * blocks * tile - length) // (4 * tile)
    return lax.fori_loop(
        jnp.maximum(own, within), slabs, lambda n, st: step(st, n, 1, True), state
    )


def fold_rows(values, combine):
    rows, lanes = values.shape
    return combine(values.reshape(rows // 8, 8, lanes), axis=0)


def forward_kernel(s, q_ref, ke_ref, ko_ref, o_ref, lse_ref, *, heads):
    H, _, _, half, QD = q_ref.shape
    blocks = 2 * ke_ref.shape[0]
    tile = H * half
    width = heads * HEAD_SIZE
    rows = SHARED * tile
    length = s[2 + pl.program_id(0)]
    for run in range(2):
        q = [padded(heads_across(q_ref, run, head, heads), head, heads) for head in range(heads)]
        at = query_positions(s, run, rows, tile, half, blocks)

        def step(state, natural, key_run, masked, q=q, at=at):
            y = natural ^ (s[0] >> 2)
            k = slab(ke_ref, ko_ref, y, key_run, 0, width)
            v = slab(ke_ref, ko_ref, y, key_run, width, 2 * width)
            if masked:
                seen = key_positions(s, natural, key_run, length, tile, half, blocks) <= at
            new = []
            for head in range(heads):
                top, total, acc = state[head]
                scores = nn(k, q[head])
                if masked:
                    scores = jnp.where(seen, scores, NEG_FILL)
                best = jnp.maximum(top, jnp.max(fold_rows(scores, jnp.max), 0, keepdims=True))
                p = jnp.exp(scores - best)
                scale = jnp.exp(top - best)
                total = total * scale + jnp.sum(fold_rows(p, jnp.sum), 0, keepdims=True)
                new.append((best, total, acc * scale + tn(v, p.astype(BF))))
            return tuple(new)

        start = tuple(
            (
                jnp.full((1, rows), NEG_FILL, F32),
                jnp.zeros((1, rows), F32),
                jnp.zeros((width, rows), F32),
            )
            for _ in range(heads)
        )
        done = slab_loops(s, length, run, tile, blocks, start, step)
        for head in range(heads):
            top, total, acc = done[head]
            lse_ref[0, run, head] = top + jnp.log(total)
            out = acc[head * HEAD_SIZE : (head + 1) * HEAD_SIZE] / total
            first = head * SHARED * HEAD_SIZE
            o_ref[:, 0, run, :, first : first + SHARED * HEAD_SIZE] = (
                heads_back(out, tile).astype(BF).reshape(H, half, SHARED * HEAD_SIZE)
            )


def backward_kernel(
    s, q_ref, ke_ref, ko_ref, o_ref, lse_ref, cos_ref, sin_ref, *refs, heads
):
    H, _, _, half, QD = q_ref.shape
    dq_ref, de_ref, dod_ref, acc_ref, do_ref = refs[H:]
    for k in range(H):
        do_ref[before(s, k, H), 0] = refs[k][0]
    blocks = 2 * ke_ref.shape[0]
    tile = H * half
    width = heads * HEAD_SIZE
    rows = SHARED * tile
    length = s[2 + pl.program_id(0)]
    acc_ref[...] = jnp.zeros(acc_ref.shape, F32)
    for run in range(2):
        q, do, lse, delta = [], [], [], []
        for head in range(heads):
            q.append(padded(heads_across(q_ref, run, head, heads), head, heads))
            up = heads_across(do_ref, run, head, heads)
            do.append(padded(up, head, heads))
            delta.append(
                jnp.sum(up * heads_across(o_ref, run, head, heads), 0, keepdims=True)
            )
            lse.append(lse_ref[0, run, head])
        at = query_positions(s, run, rows, tile, half, blocks)

        def step(state, natural, key_run, masked, q=q, do=do, lse=lse, delta=delta, at=at):
            y = natural ^ (s[0] >> 2)
            k = slab(ke_ref, ko_ref, y, key_run, 0, width)
            v = slab(ke_ref, ko_ref, y, key_run, width, 2 * width)
            if masked:
                seen = key_positions(s, natural, key_run, length, tile, half, blocks) <= at
            new = []
            dk = jnp.zeros((4 * tile, width), F32)
            dv = jnp.zeros((4 * tile, width), F32)
            for head in range(heads):
                p = jnp.exp(nn(k, q[head]) - lse[head])
                if masked:
                    p = jnp.where(seen, p, 0.0)
                ds = (p * (nn(v, do[head]) - delta[head])).astype(BF)
                dk = dk + nt(ds, q[head])
                dv = dv + nt(p.astype(BF), do[head])
                new.append(state[head] + tn(k, ds))
            acc_ref[key_run, y, :, :width] += dk
            acc_ref[key_run, y, :, width:] += dv
            return tuple(new)

        start = tuple(jnp.zeros((width, rows), F32) for _ in range(heads))
        done = slab_loops(s, length, run, tile, blocks, start, step)
        cosine = cos_ref[:, run].reshape(tile, LANES)
        sine = sin_ref[:, run].reshape(tile, LANES)
        for head in range(heads):
            out = done[head][head * HEAD_SIZE : (head + 1) * HEAD_SIZE]
            out = (heads_back(out, tile) * SCORE_SCALE).astype(BF).astype(F32)
            for lanes in range(0, SHARED * HEAD_SIZE, LANES):
                part = out[:, lanes : lanes + LANES]
                part = part * cosine - turned(part) * sine
                first = head * SHARED * HEAD_SIZE + lanes
                dq_ref[:, 0, run, :, first : first + LANES] = part.astype(BF).reshape(
                    H, half, LANES
                )
    for run in range(2):
        for y in range(blocks // 4):
            for index, (ref, i) in enumerate(((de_ref, 0), (de_ref, 1), (dod_ref, 0), (dod_ref, 1))):
                ref[2 * y + i, :, 0, run] = (
                    acc_ref[run, y, index * tile : (index + 1) * tile]
                    .astype(BF)
                    .reshape(H, half, 2 * width)
                )


def attention_specs(q, kv, heads):
    H, M, _, half, QD = q.shape
    places, _, _, _, _, width = kv.shape
    per_q = pl.BlockSpec((H, 1, 2, half, QD), lambda m, s: (0, m, 0, 0, 0))
    per_kv = pl.BlockSpec((places, H, 1, 2, half, width), lambda m, s: (0, 0, m, 0, 0, 0))
    per_row = pl.BlockSpec((1, 2, heads, 1, SHARED * H * half), lambda m, s: (m, 0, 0, 0, 0))
    work = M * places * H * half * SHARED * H * half * QD
    return per_q, per_kv, per_row, work


def attention_forward(scalars, q, k_even, k_odd, heads, wait):
    H, M, _, half, QD = q.shape
    per_q, per_kv, per_row, work = attention_specs(q, k_even, heads)
    return call(
        functools.partial(forward_kernel, heads=heads),
        (M,),
        [per_q, per_kv, per_kv],
        [per_q, per_row],
        [shape_of(q.shape, BF), shape_of((M, 2, heads, 1, SHARED * H * half), F32)],
        [],
        8 * work,
        2 * (2 * q.size + 2 * k_even.size),
        (scalars, q, k_even, k_odd),
        wait,
    )


def attention_backward(scalars, q, k_even, k_odd, do_parts, o, lse, cosine, sine, heads, wait):
    H, M, _, half, QD = q.shape
    per_q, per_kv, per_row, work = attention_specs(q, k_even, heads)
    blocks = 2 * k_even.shape[0]
    return call(
        functools.partial(backward_kernel, heads=heads),
        (M,),
        [per_q, per_kv, per_kv, per_q, per_row, whole(cosine.shape), whole(sine.shape)]
        + [pl.BlockSpec((1, 2, half, QD), lambda m, s: (m, 0, 0, 0))] * H,
        [per_q, per_kv, per_kv],
        [shape_of(q.shape, BF), shape_of(k_even.shape, BF), shape_of(k_odd.shape, BF)],
        [
            pltpu.VMEM((2, blocks // 4, 4 * H * half, 2 * heads * HEAD_SIZE), F32),
            pltpu.VMEM((H, 1, 2, half, QD), BF),
        ],
        20 * work,
        2 * (4 * q.size + 4 * k_even.size),
        (scalars, q, k_even, k_odd, o, lse, cosine, sine, *do_parts),
        wait,
    )


def out_kernel(s, x_ref, gain_ref, w_ref, *refs):
    devices = len(refs) - 4
    xn_ref, own_ref, o_own_ref, acc_ref = refs[devices:]
    n = pl.program_id(0)
    group, QD = refs[0].shape
    columns = w_ref.shape[1]
    rows = group // devices

    @pl.when(n == 0)
    def _():
        at = pl.ds(pl.multiple_of(s[1] * rows, rows), rows)
        for k in range(devices):
            lanes = pl.ds(pl.multiple_of(before(s, k, devices) * QD, LANES), QD)
            o_own_ref[:, lanes] = refs[k][at, :]

    got = jnp.zeros((group, columns), F32)
    for k in range(devices):
        first = pl.multiple_of(before(s, k, devices) * QD, QD)
        got = got + nn(refs[k][...], w_ref[pl.ds(first, QD), :])
    acc_ref[:, pl.ds(pl.multiple_of(n * columns, LANES), columns)] = got

    @pl.when(n == pl.num_programs(0) - 1)
    def _():
        def finish(h, carry):
            at = pl.ds(pl.multiple_of(h * rows, rows), rows)
            resid = x_ref[at, :].astype(F32) + RESIDUAL_SCALE * acc_ref[at, :]
            inverse = lax.rsqrt(jnp.mean(resid * resid, -1, keepdims=True) + EPSILON)
            xn_ref[at, :] = ((resid * inverse) * gain_ref[1:2, :]).astype(BF)

            @pl.when(h == s[1])
            def _():
                own_ref[...] = resid

            return carry

        lax.fori_loop(0, devices, finish, 0)


def out_project(scalars, o_parts, x, gains, w_out, wait):
    H = len(o_parts)
    group, QD = o_parts[0].shape
    D = w_out.shape[1]
    rows = group // H
    columns = 1024
    piece = pl.BlockSpec((H * QD, columns), lambda n, s: (0, n))
    return call(
        out_kernel,
        (D // columns,),
        [whole(x.shape), whole(gains.shape), piece] + [whole((group, QD))] * H,
        [whole((group, D)), whole((rows, D)), whole((rows, H * QD))],
        [shape_of((group, D), BF), shape_of((rows, D), F32), shape_of((rows, H * QD), BF)],
        [pltpu.VMEM((group, D), F32)],
        2 * group * H * QD * D,
        2 * (H * group * QD + 2 * x.size + w_out.size),
        (scalars, x, gains, w_out, *o_parts),
        wait,
    )


def mlp_forward_kernel(s, xn_ref, wg_ref, wu_ref, gate_ref, up_ref, hidden_ref):
    gate = nn(xn_ref[...], wg_ref[...])
    up = nn(xn_ref[...], wu_ref[...])
    gate_ref[...] = gate
    up_ref[...] = up
    hidden_ref[...] = (gate * (1.0 / (1.0 + jnp.exp(-gate))) * up).astype(BF)


def mlp_forward(scalars, xn, w_gate_up, tile, wait):
    group, D = xn.shape
    F = w_gate_up.shape[1] // 2
    count = F // tile
    out = pl.BlockSpec((group, tile), lambda f, s: (0, f))
    return call(
        mlp_forward_kernel,
        (count,),
        [
            whole(xn.shape),
            pl.BlockSpec((D, tile), lambda f, s: (0, f)),
            pl.BlockSpec((D, tile), lambda f, s: (0, f + count)),
        ],
        [out, out, out],
        [shape_of((group, F), F32), shape_of((group, F), F32), shape_of((group, F), BF)],
        [],
        4 * group * D * F,
        2 * (group * D + 2 * D * F + 5 * group * F),
        (scalars, xn, w_gate_up, w_gate_up),
        wait,
    )


def down_kernel(s, hidden_ref, w_ref, *outs):
    got_ref = outs[-1]
    rows = outs[0].shape[0]
    devices = got_ref.shape[0] // rows
    got_ref[...] = nn(hidden_ref[...], w_ref[...]).astype(BF)
    for k in range(devices):
        at = pl.ds(pl.multiple_of(after(s, k, devices) * rows, rows), rows)
        outs[k][...] = got_ref[at, :]


def down_project(scalars, hidden, w_down, devices, wait):
    group, F = hidden.shape
    D = w_down.shape[1]
    width = 512
    rows = group // devices
    return call(
        down_kernel,
        (D // width,),
        [whole(hidden.shape), pl.BlockSpec((F, width), lambda n, s: (0, n))],
        [pl.BlockSpec((rows, width), lambda n, s: (0, n))] * devices,
        [shape_of((rows, D), BF)] * devices,
        [pltpu.VMEM((group, width), BF)],
        2 * group * D * F,
        2 * (group * D + D * F + group * F),
        (scalars, hidden, w_down),
        wait,
    )


def mlp_backward_kernel(
    s, gate_ref, up_ref, wg_ref, wu_ref, wd_ref, dmo_ref, dg_ref, du_ref, dxn_ref, acc_ref
):
    f = pl.program_id(0)
    d_hidden = nt(dmo_ref[...], wd_ref[...])
    gate = gate_ref[...]
    sigma = 1.0 / (1.0 + jnp.exp(-gate))
    dg_ref[...] = (d_hidden * up_ref[...] * (sigma * (1.0 + gate * (1.0 - sigma)))).astype(BF)
    du_ref[...] = (d_hidden * (gate * sigma)).astype(BF)
    got = nt(dg_ref[...], wg_ref[...]) + nt(du_ref[...], wu_ref[...])

    @pl.when(f == 0)
    def _():
        acc_ref[...] = got

    @pl.when(f > 0)
    def _():
        acc_ref[...] += got

    @pl.when(f == pl.num_programs(0) - 1)
    def _():
        dxn_ref[...] = acc_ref[...].astype(BF)


def mlp_backward(scalars, gate, up, dmo, w_gate_up, w_down, tile, wait):
    group, D = dmo.shape
    F = gate.shape[1]
    count = F // tile
    per_f = pl.BlockSpec((group, tile), lambda f, s: (0, f))
    return call(
        mlp_backward_kernel,
        (count,),
        [
            per_f,
            per_f,
            pl.BlockSpec((D, tile), lambda f, s: (0, f)),
            pl.BlockSpec((D, tile), lambda f, s: (0, f + count)),
            pl.BlockSpec((tile, D), lambda f, s: (f, 0)),
            whole((group, D)),
        ],
        [per_f, per_f, whole((group, D))],
        [shape_of((group, F), BF), shape_of((group, F), BF), shape_of((group, D), BF)],
        [pltpu.VMEM((group, D), F32)],
        6 * group * D * F,
        2 * (3 * group * D + 3 * D * F + 6 * group * F),
        (scalars, gate, up, w_gate_up, w_gate_up, w_down, dmo),
        wait,
    )


def block_lanes(s, own, near, block):
    i = pl.program_id(0)
    if near:
        index = s[0] ^ (2 * i if own else 2 * i + 1)
    else:
        index = 2 * i + (s[0] % 2 if own else 1 - s[0] % 2)
    return pl.ds(pl.multiple_of(index * block, LANES), block)


def rows_kernel(s, left_ref, *refs, own, count, near):
    right = refs[:count]
    out_ref = refs[-1]
    block = out_ref.shape[0]
    lanes = block_lanes(s, own, near, block)
    left = left_ref[:, lanes]
    at = 0
    for i, right_ref in enumerate(right):
        width = right_ref.shape[1]
        got = tn(left, right_ref[...])
        if own:
            got = got + refs[count][:, at : at + width].astype(F32)
        out_ref[:, at : at + width] = got.astype(BF)
        at += width


def grad_rows(scalars, left, rights, blocks, came=None, near=False, wait=()):
    n, D = left.shape
    block = D // blocks
    width = sum(r.shape[1] for r in rights)
    piece = pl.BlockSpec((block, width), lambda i, s: (i, 0))
    extra = [] if came is None else [came]
    return call(
        functools.partial(
            rows_kernel, own=came is not None, count=len(rights), near=near
        ),
        (blocks // 2,),
        [whole(left.shape)] + [whole(r.shape) for r in rights] + [piece] * len(extra),
        [piece],
        [shape_of((D // 2, width), BF)],
        [],
        n * D * width,
        2 * (left.size + n * width + D * width),
        (scalars, left, *rights, *extra),
        wait,
    )[0]


def columns_kernel(s, left_ref, right_ref, *refs, own):
    out_ref = refs[-1]
    got = tn(left_ref[...], right_ref[:, block_lanes(s, own, True, out_ref.shape[2])])
    if own:
        got = got + refs[0][0].astype(F32)
    out_ref[0] = got.astype(BF)


def grad_columns(scalars, left, right, blocks, came=None, wait=()):
    n, F = left.shape
    D = right.shape[1]
    block = D // blocks
    piece = pl.BlockSpec((1, F, block), lambda i, s: (i, 0, 0))
    extra = [] if came is None else [came]
    return call(
        functools.partial(columns_kernel, own=came is not None),
        (blocks // 2,),
        [whole(left.shape), whole(right.shape)] + [piece] * len(extra),
        [piece],
        [shape_of((blocks // 2, F, block), BF)],
        [],
        n * D * F,
        2 * (left.size + right.size + D * F),
        (scalars, left, right, *extra),
        wait,
    )[0]


def through_norm(upstream, gain, values):
    inverse = lax.rsqrt(jnp.mean(values * values, -1, keepdims=True) + EPSILON)
    scaled = values * inverse
    through = upstream * gain
    inner = jnp.mean(through * scaled, -1, keepdims=True)
    return inverse * (through - scaled * inner), scaled


def branch_kernel(s, parts, resid_ref, up_ref, gain_ref, w_ref, *refs):
    devices = len(refs) - 4
    dresid_ref, da_ref, gg_ref = refs[:3]
    outs = refs[3:-1]
    dattn_ref = refs[-1]
    p = pl.program_id(0)

    @pl.when(p == 0)
    def _():
        upstream = parts[0].astype(F32)
        for h in range(1, parts.shape[0]):
            upstream = upstream + parts[h].astype(F32)
        back, scaled = through_norm(upstream, gain_ref[1:2, :], resid_ref[...])
        gg_ref[...] = jnp.broadcast_to(
            jnp.sum(upstream * scaled, 0, keepdims=True), gg_ref.shape
        )
        d_resid = up_ref[...].astype(F32) + back
        dresid_ref[...] = d_resid
        da_ref[...] = (RESIDUAL_SCALE * d_resid).astype(BF)

    dattn_ref[p] = nt(da_ref[...], w_ref[...]).astype(BF)

    @pl.when(p == pl.num_programs(0) - 1)
    def _():
        for k in range(devices):
            outs[k][...] = dattn_ref[after(s, k, devices)]


def branch_back(scalars, parts, resid, upstream, gains, w_out, H, wait):
    _, tokens, D = parts.shape
    QD = w_out.shape[0] // H
    return call(
        branch_kernel,
        (H,),
        [whole(a.shape) for a in (parts, resid, upstream, gains)]
        + [pl.BlockSpec((QD, D), lambda p, s: (p, 0))],
        [whole((tokens, D)), whole((tokens, D)), whole((8, D))] + [whole((tokens, QD))] * H,
        [shape_of((tokens, D), F32), shape_of((tokens, D), BF), shape_of((8, D), F32)]
        + [shape_of((tokens, QD), BF)] * H,
        [pltpu.VMEM((H, tokens, QD), BF)],
        2 * tokens * D * H * QD,
        2 * (H * tokens * D + w_out.size + 6 * tokens * D),
        (scalars, parts, resid, upstream, gains, w_out),
        wait,
    )


def input_kernel(
    s, dq_ref, dkv_ref, cos_ref, sin_ref, x_ref, xn_ref, gg_ref, we_ref, wo_ref, *refs
):
    out_ref, ge_ref, go_ref, dqkv_ref, inv_ref = refs
    p = pl.program_id(0)
    group, QD = dq_ref.shape
    KD = dkv_ref.shape[1] // 2
    used = QD + 2 * KD
    block = we_ref.shape[1]

    @pl.when(p == 0)
    def _():
        dqkv_ref[:, :QD] = dq_ref[...]
        for first in range(0, 2 * KD, LANES):
            part = dkv_ref[:, first : first + LANES].astype(F32)
            if first < KD:
                part = rope_lanes(part, cos_ref[...], -sin_ref[...], first, KD)
            dqkv_ref[:, QD + first : QD + first + LANES] = part.astype(BF)
        x = x_ref[...].astype(F32)
        inv_ref[...] = jnp.broadcast_to(
            lax.rsqrt(jnp.mean(x * x, -1, keepdims=True) + EPSILON), inv_ref.shape
        )

    for parity, (w_ref, g_ref) in enumerate(((we_ref, ge_ref), (wo_ref, go_ref))):
        lanes = chunk(s, 2 * p + parity, block)
        dxn = nt(dqkv_ref[...], w_ref[0, :, :used])
        out_ref[:, lanes] = dxn.astype(BF)
        scaled = x_ref[:, lanes].astype(F32) * inv_ref[:, 0:1]
        gain_one = jnp.sum(dxn * scaled, 0, keepdims=True)
        g_ref[0, :, :used] = tn(xn_ref[:, lanes], dqkv_ref[...]).astype(BF)
        row = lax.broadcasted_iota(jnp.int32, (LANES, block), 0)
        both = jnp.where(row == 0, gain_one, jnp.where(row == 1, gg_ref[0:1, lanes], 0.0))
        g_ref[0, :, used:] = both.T.astype(BF)


def input_back(scalars, dq, dkv, cosine, sine, x, xn, gain_two, w_even, w_odd, wait):
    group, D = x.shape
    QD = dq.shape[1]
    places, block, columns = w_even.shape
    piece = pl.BlockSpec((1, block, columns), lambda p, s: (p, 0, 0))
    return call(
        input_kernel,
        (places,),
        [whole(a.shape) for a in (dq, dkv, cosine, sine, x, xn, gain_two)] + [piece, piece],
        [whole(x.shape), piece, piece],
        [shape_of(x.shape, BF), shape_of(w_even.shape, BF), shape_of(w_even.shape, BF)],
        [
            pltpu.VMEM((group, QD + dkv.shape[1]), BF),
            pltpu.VMEM((group, LANES), F32),
        ],
        4 * group * D * (QD + dkv.shape[1]),
        2 * (3 * x.size + 4 * w_even.size),
        (scalars, dq, dkv, cosine, sine, x, xn, gain_two, w_even, w_odd),
        wait,
    )


def last_kernel(s, parts_ref, x_ref, resid_ref, gain_ref, place_ref, out_ref):
    M, T, _ = out_ref.shape
    for m in range(M):
        at = pl.ds(m * T, T)
        upstream = parts_ref[0, at, :].astype(F32)
        for h in range(1, parts_ref.shape[0]):
            upstream = upstream + parts_ref[h, at, :].astype(F32)
        back, _ = through_norm(upstream, gain_ref[0:1, :], x_ref[at, :].astype(F32))
        total = resid_ref[at, :] + back
        rank = lax.broadcasted_iota(jnp.int32, (T, T), 0)
        order = (place_ref[m] == rank).astype(F32)
        out_ref[m] = lax.dot_general(
            order,
            total,
            (((0,), (0,)), ((), ())),
            precision=lax.Precision.HIGHEST,
            preferred_element_type=F32,
        )


def input_gradient(scalars, parts, x, d_resid, gains, place, wait):
    M, T = place.shape
    D = x.shape[1]
    place = place.reshape(M, 1, T)
    args = (scalars, parts, x, d_resid, gains, place)
    return call(
        last_kernel,
        (1,),
        [whole(a.shape) for a in args[1:]],
        [whole((M, T, D))],
        [shape_of((M, T, D), F32)],
        [],
        4 * M * T * T * D,
        12 * M * T * D,
        args,
        wait,
    )[0]


def body(
    inputs,
    cotangent,
    lengths,
    positions,
    attn_gain,
    mlp_gain,
    w_query,
    key_projection,
    value_projection,
    w_out,
    w_gate,
    w_up,
    w_down,
):
    B = lax.axis_size("blk")
    H = lax.axis_size("head")
    me = lax.axis_index("blk")
    mine = lax.axis_index("head")
    T = inputs.shape[1]
    D = MODEL_WIDTH
    half = T // 2
    slots = T * H * B
    heads = KEY_VALUE_HEADS // H
    KD = heads * HEAD_SIZE
    QD = KD * SHARED
    used = QD + 2 * KD
    tokens = MICRO * T
    group = H * tokens
    wrows = w_query.shape[0]
    F = w_gate.shape[1]
    block = D // B
    tile = min(512, F)

    scalars = jnp.concatenate(
        [jnp.stack([me, mine]).astype(jnp.int32), lengths.astype(jnp.int32)]
    )

    gains = jnp.concatenate(
        [attn_gain[:, None], mlp_gain[:, None], jnp.zeros((wrows, LANES - 2), BF)], 1
    )
    pack = pack_weights(scalars, w_query, key_projection, value_projection, gains, H)
    linear = me * H + mine
    my_pos = lax.dynamic_slice_in_dim(positions, linear * T, T, axis=1)
    place = jnp.where(
        my_pos < slots // 2, my_pos - half * linear, half + my_pos - (slots - half * (linear + 1))
    ).astype(jnp.int32)
    order = (place[:, None, :] == jnp.arange(T)[None, :, None]).astype(BF)
    pack = arrange(scalars, head_deal(pack, H)).reshape(H * wrows, used + LANES)
    x_copies, upstream = in_order(scalars, inputs, cotangent, place, H, [pack])
    x_own = x_copies[0]
    x = head_exchange(x_copies)
    qkv_even, qkv_odd = xor_gather(pack, B)

    w_gate_up = lax.all_gather(jnp.concatenate([w_gate, w_up], 1), "blk", axis=0, tiled=True)
    dmo_copies = copies(scalars, upstream, 0, H, RESIDUAL_SCALE, [x])
    dmo_parts = [head_exchange(dmo_copies)]

    run_start = jnp.arange(H)[:, None, None] + me * H
    i = jnp.arange(half)[None, None, :]
    row_pos = jnp.concatenate([half * run_start + i, slots - half * (run_start + 1) + i], 1)
    half_dim = HEAD_SIZE // 2
    frequency = ROPE_BASE ** (-(jnp.arange(half_dim).astype(F32) * 2.0) / HEAD_SIZE)
    angles = row_pos.reshape(H * T, 1).astype(F32) * frequency[None, :]
    cosine = jnp.cos(angles)
    sine = jnp.sin(angles)
    cosine = jnp.concatenate([cosine] * 4, 1)
    sine = jnp.concatenate([-sine, sine] * 2, 1)

    def per_group(table):
        return jnp.broadcast_to(
            table.reshape(H, 1, T, LANES), (H, MICRO, T, LANES)
        ).reshape(group, LANES)

    xn1, q, kv, gain_rows = project(
        scalars,
        x.reshape(H, MICRO, T, D),
        qkv_even,
        qkv_odd,
        cosine,
        sine,
        QD,
        KD,
        [dmo_copies],
    )
    x = x.reshape(group, D)
    runs = (H, MICRO, 2, half)
    q = q.reshape(runs + (QD,))
    kv_even, kv_odd = xor_gather(kv.reshape(group, 2 * KD), B)
    kv_even = kv_even.reshape((B // 2,) + runs + (2 * KD,))
    kv_odd = kv_odd.reshape((B // 2,) + runs + (2 * KD,))
    w_o = lax.all_gather(
        hold(scalars, [w_out], [w_gate_up, kv])[0], "head", axis=0, tiled=True
    )
    o, lse = attention_forward(scalars, q, kv_even, kv_odd, heads, dmo_parts)
    o_parts = head_gather(o.reshape(group, QD), H)
    w_o = lax.all_gather(hold(scalars, [w_o], [lse])[0], "blk", axis=0, tiled=True)
    w_d = lax.all_gather(hold(scalars, [w_down], [lse])[0], "blk", axis=1, tiled=True)
    later = [copies(scalars, upstream, m, H, RESIDUAL_SCALE, o_parts[1:]) for m in range(1, MICRO)]
    dmo_parts = dmo_parts + [head_exchange(part) for part in later]
    xn2, resid, o_own = out_project(
        scalars, o_parts, x, gain_rows, w_o, later
    )
    gate, up, hidden = mlp_forward(scalars, xn2, w_gate_up, tile, ())
    dmo = merge(scalars, dmo_parts, [hidden])
    came_down = swap(grad_columns(scalars, hidden, dmo, B), 1, B)
    sum_down = grad_columns(scalars, hidden, dmo, B, came_down)
    down_first = first_step(sum_down, B)
    d_gate, d_up, d_xn2 = mlp_backward(
        scalars, gate, up, dmo, w_gate_up, w_d, tile, [sum_down]
    )
    d_xn2 = lax.psum_scatter(d_xn2, "head", scatter_dimension=0, tiled=True)[None]

    came = swap(grad_rows(scalars, xn2, (d_gate, d_up), B, wait=down_first), 1, B)
    down_second = second_step(sum_down, down_first, B)
    sum_gate_up = grad_rows(scalars, xn2, (d_gate, d_up), B, came)
    grad_gate_up = plane_scatter(sum_gate_up, B, 0)
    mlp_sum = down_project(scalars, hidden, w_d, H, [sum_gate_up])


    d_resid, d_branch, gain_two, *d_attn = branch_back(
        scalars,
        d_xn2,
        resid,
        upstream,
        gain_rows,
        w_o,
        H,
        [sum_gate_up, mlp_sum[0]],
    )
    d_attn = head_deal(d_attn, H)
    mlp_out = head_deal(mlp_sum, H)
    d_attn = [part.reshape(MICRO, 2, half, QD) for part in d_attn]
    tables = (H, 2, half, LANES)
    dq, dkv_even, dkv_odd = attention_backward(
        scalars, q, kv_even, kv_odd, d_attn, o, lse, cosine.reshape(tables), sine.reshape(tables), heads,
        mlp_out[1:2],
    )
    pieces = (B // 2, group, 2 * KD)
    came = swap(dkv_odd.reshape(pieces), 1, B)
    dkv = core_scatter(add_up(scalars, dkv_even.reshape(pieces), came, ()), B)
    d_xn1, grad_even, grad_odd = input_back(
        scalars,
        dq.reshape(group, QD),
        dkv,
        per_group(cosine),
        per_group(sine),
        x,
        xn1.reshape(group, D),
        gain_two,
        qkv_even,
        qkv_odd,
        mlp_out[2:],
    )
    out_away = grad_rows(scalars, o_own, (d_branch,), B, near=True, wait=[d_xn1])
    sum_out = grad_rows(
        scalars, o_own, (d_branch,), B, came=swap(out_away, 1, B), near=True, wait=[grad_gate_up]
    ).reshape(B // 2, block, D)

    def by_distance(values):
        values = values.astype(BF).reshape(H, wrows, -1)
        return head_deal(
            [lax.dynamic_index_in_dim(values, (mine + k) % H, 0, False) for k in range(H)], H
        )

    grad_out = by_distance(core_scatter_steps(sum_out, B))
    grad_gate_up = wide(scalars, grad_gate_up, grad_out[2:3])
    d_xn1 = lax.psum_scatter(d_xn1, "head", scatter_dimension=0, tiled=True)[None]
    grad_down = total(scalars, sum_down, down_second, [d_xn1] + grad_out[1:2])
    grad_qkv = arrange(scalars, by_distance(xor_scatter(grad_even, grad_odd, B))).astype(F32)
    grad_gains = jnp.sum(grad_qkv[:, :, used : used + 2], 0)

    def side_by_side(values):
        return values.transpose(1, 0, 2).reshape(wrows, -1)

    output = (resid + RESIDUAL_SCALE * sum(part.astype(F32) for part in mlp_out)).astype(BF)
    output = jnp.einsum(
        "mrs,mrd->msd", order, output.reshape(MICRO, T, D), preferred_element_type=F32
    ).astype(BF)
    d_input = input_gradient(scalars, d_xn1, x_own, d_resid, gain_rows, place, grad_out[3:])
    grad_out = sum(part.astype(F32) for part in grad_out)
    return (
        output,
        d_input,
        grad_gains[:, 0],
        grad_gains[:, 1],
        side_by_side(grad_qkv[:, :, :QD]),
        side_by_side(grad_qkv[:, :, QD : QD + KD]),
        side_by_side(grad_qkv[:, :, QD + KD : used]),
        grad_out,
        grad_gate_up[:, :F],
        grad_gate_up[:, F:],
        grad_down,
    )


def solution(mesh):
    both = ("blk", "head")
    return jax.shard_map(
        body,
        mesh=mesh,
        in_specs=(
            P(None, both, None),
            P(None, both, None),
            P(),
            P(),
            P(both),
            P(both),
            P(both, None),
            P(both, None),
            P(both, None),
            P(both, None),
            P("blk", "head"),
            P("blk", "head"),
            P("head", "blk"),
        ),
        out_specs=(
            P(None, both, None),
            P(None, both, None),
            P(both),
            P(both),
            P(both, None),
            P(both, None),
            P(both, None),
            P(both, None),
            P("blk", "head"),
            P("blk", "head"),
            P("head", "blk"),
        ),
        check_vma=False,
    )
```
